32 devices in a mesh: seq: 8 (over z, x), fsdp: 4 (over y, core).
Axes of the slice: x: 2, y: 2, z: 4, core: 2. Of those that a mesh axis runs over, the one named last changes fastest.
Arguments:
- tokens: bfloat16 [4, 2048, 768], P('fsdp', 'seq'), may hold values from -6 to 6
- block_order: int32 [16], replicated, may hold values from 0 to 15, as said below
- doc_lengths: int32 [4, 4], P('fsdp'), may hold values from 1 to 1024, 2048 in all within a row
- norm_one_gain: bfloat16 [768], P('fsdp'), may hold values from 0.099609375 to 1.8984375
- norm_one_bias: bfloat16 [768], P('fsdp'), may hold values from -4 to 4
- query_weight: bfloat16 [768, 768], P('fsdp'), may hold values from -0.21875 to 0.21875
- query_bias: bfloat16 [768], P('fsdp'), may hold values from -6 to 6
- key_weight: bfloat16 [768, 64], P('fsdp'), may hold values from -0.21875 to 0.21875
- key_bias: bfloat16 [16], P('fsdp'), may hold values from -6 to 6
- value_weight: bfloat16 [768, 64], P('fsdp'), may hold values from -0.21875 to 0.21875
- value_bias: bfloat16 [64], P('fsdp'), may hold values from -6 to 6
- out_weight: bfloat16 [768, 768], P('fsdp'), may hold values from -1.75 to 1.75
- out_bias: bfloat16 [768], P('fsdp'), may hold values from -6 to 6
- norm_two_gain: bfloat16 [768], P('fsdp'), may hold values from 0.099609375 to 1.8984375
- norm_two_bias: bfloat16 [768], P('fsdp'), may hold values from -4 to 4
- up_weight: bfloat16 [3072, 768], P('fsdp'), may hold values from -0.21875 to 0.21875
- up_bias: bfloat16 [3072], P('fsdp'), may hold values from -6 to 6
- down_weight: bfloat16 [3072, 768], P('fsdp'), may hold values from -0.109375 to 0.109375
- down_bias: bfloat16 [768], P('fsdp'), may hold values from -6 to 6
- cotangent: bfloat16 [4, 2048, 768], P('fsdp', 'seq'), may hold values from -6 to 6
Outputs:
- layer_out: bfloat16 [4, 2048, 768], P('fsdp', 'seq')
- grad_tokens: bfloat16 [4, 2048, 768], P('fsdp', 'seq')
- grad_norm_one_gain: float32 [768], P('fsdp')
- grad_norm_one_bias: float32 [768], P('fsdp')
- grad_query_weight: float32 [768, 768], P('fsdp')
- grad_query_bias: float32 [768], P('fsdp')
- grad_key_weight: float32 [768, 64], P('fsdp')
- grad_key_bias: float32 [16], P('fsdp')
- grad_value_weight: float32 [768, 64], P('fsdp')
- grad_value_bias: float32 [64], P('fsdp')
- grad_out_weight: float32 [768, 768], P('fsdp')
- grad_out_bias: float32 [768], P('fsdp')
- grad_norm_two_gain: float32 [768], P('fsdp')
- grad_norm_two_bias: float32 [768], P('fsdp')
- grad_up_weight: float32 [3072, 768], P('fsdp')
- grad_up_bias: float32 [3072], P('fsdp')
- grad_down_weight: float32 [3072, 768], P('fsdp')
- grad_down_bias: float32 [768], P('fsdp')
The draws below stay inside these ranges and needn't reach their ends.
Inputs may be any that keep to these rules, and one draw needn't show every extreme that they name: `block_order`: for every index i of seq, entries 2i and 2i+1 are two blocks b and 15 - b; every block appears once. `doc_lengths`: each sequence's lengths sum to 2048.
All inputs are finite; a program needn't handle non-finite values.
Results may differ from the reference program's by a relative error of at most 0.012.
The reference program's roundings to bfloat16 on the way count: a program that leaves them out, or rounds other values in their place, can miss the bound.
Values may be sent and summed in bfloat16 or wider, within the bound.
No kernel may reach another device: no remote copies, remote signals or barrier semaphores. Data moves between devices by JAX's collectives and lax.ppermute only.
A program may use at most 128 MiB of HBM per device.

```python
import math
import jax
import jax.numpy as jnp
import numpy as np
from jax import lax

D = 768
HEADS = 12
HDIM = 64
ROT = 16
FF = 3072
DOCS = 4
NBLK = 16
LENGTH = 2048
SEQS = 4


def draw_block_order(key, part):
    key = jax.random.fold_in(key, 7)
    pair_count = NBLK // 2
    key_perm, key_flip = jax.random.split(key)
    ordering = jax.random.permutation(key_perm, pair_count).astype(jnp.int32)
    flipped = jax.random.randint(key_flip, (pair_count,), 0, 2, dtype=jnp.int32)
    first_slot = jnp.where(flipped == 1, NBLK - 1 - ordering, ordering)
    second = NBLK - 1 - first_slot
    return jnp.stack([first_slot, second], axis=1).reshape(NBLK).astype(jnp.int32)


def block_levels(stream_key, shape, cuts, smallest, high):
    loudness, own = 1.0, jax.random.fold_in(stream_key, 6)
    for axis_at, blocks in cuts:
        steps = jnp.exp(jax.random.uniform(jax.random.fold_in(own, axis_at), (blocks,), jnp.float32, smallest / len(cuts), high / len(cuts)))
        loudness = loudness * jnp.repeat(steps, shape[axis_at] // blocks).reshape([-1 if axis == axis_at else 1 for axis in range(len(shape))])
    return loudness


def split_up(number_of, total, reach, lean):
    portions = [(1 << 20) // math.isqrt(standing ** lean) + 1 for standing in range(2, number_of + 1)]
    rest, holding = total - reach - (number_of - 1), [1] * (number_of - 1)
    while rest > 0:
        free = [i for i in range(number_of - 1) if holding[i] < reach]
        mass, left = sum([portions[i] for i in free]), rest
        for i in free:
            extra = min(reach - holding[i], max(1, left * portions[i] // mass), rest)
            holding[i] = holding[i] + extra
            rest = rest - extra
    return np.array([reach] + holding)


def ragged_sizes(stream_key, number_of, total, most, lean):
    if number_of == 2:
        one = jax.random.randint(stream_key, (), max(1, total - most), min(most, total - 1) + 1)
        return jnp.stack([one, total - one])
    lengths = jnp.asarray(split_up(number_of, total, most, lean), jnp.int32)
    twos = (number_of - 1) // 2
    donor, receiver = lengths[1:1 + 2 * twos:2], lengths[2:2 + 2 * twos:2]
    room = jnp.minimum(donor - 1, most - receiver)
    shifted = jax.random.randint(jax.random.fold_in(stream_key, 1), (twos,), 0, 1 << 20) % (room + 1)
    lengths = lengths.at[1:1 + 2 * twos:2].set(donor - shifted).at[2:2 + 2 * twos:2].set(receiver + shifted)
    return lengths[jax.random.permutation(jax.random.fold_in(stream_key, 2), number_of)]


def noise(stream_key, shape, spread, bound, cuts=(), held_as=jnp.bfloat16):
    drawn = jax.random.normal(stream_key, shape, jnp.float32) * spread
    if len(cuts) > 0:
        drawn = block_levels(stream_key, shape, cuts, -0.22, 0.18) * drawn
    return jnp.clip(drawn, min=-bound, max=bound).astype(held_as)


def setup_inputs(seed: int = 0) -> dict:
    arg_keys = jax.random.split(jax.random.key(seed), 21)
    return {
        "tokens": noise(arg_keys[0], (SEQS, LENGTH, D), 1.0, 6.0, ((0, 4), (1, 8))),
        "block_order": draw_block_order(jax.random.fold_in(arg_keys[20], 71), 0),
        "doc_lengths": jax.vmap(lambda own: ragged_sizes(own, DOCS, LENGTH, LENGTH // 2, 1))(jax.random.split(arg_keys[2], SEQS)).reshape((SEQS, DOCS)).astype(jnp.int32),
        "norm_one_gain": jnp.clip(1.0 + 0.18 * jax.random.normal(arg_keys[3], (D,), jnp.float32), 0.099609375, 1.8984375).astype(jnp.bfloat16),
        "norm_one_bias": noise(arg_keys[4], (D,), 0.3, 4.0, ((0, 4),)),
        "query_weight": noise(arg_keys[5], (D, D), D ** -0.5, 0.21875, ((0, 4),)),
        "query_bias": noise(arg_keys[6], (D,), 0.5, 6.0, ((0, 4),)),
        "key_weight": noise(arg_keys[7], (D, HDIM), D ** -0.5, 0.21875, ((0, 4),)),
        "key_bias": noise(arg_keys[8], (ROT,), 0.5, 6.0, ((0, 4),)),
        "value_weight": noise(arg_keys[9], (D, HDIM), D ** -0.5, 0.21875, ((0, 4),)),
        "value_bias": noise(arg_keys[10], (HDIM,), 0.5, 6.0, ((0, 4),)),
        "out_weight": noise(arg_keys[11], (D, D), (D // 64) ** -0.5, 1.75, ((0, 4),)),
        "out_bias": noise(arg_keys[12], (D,), 1.0, 6.0, ((0, 4),)),
        "norm_two_gain": jnp.clip(1.0 + 0.18 * jax.random.normal(arg_keys[13], (D,), jnp.float32), 0.099609375, 1.8984375).astype(jnp.bfloat16),
        "norm_two_bias": noise(arg_keys[14], (D,), 0.3, 4.0, ((0, 4),)),
        "up_weight": noise(arg_keys[15], (FF, D), D ** -0.5, 0.21875, ((0, 4),)),
        "up_bias": noise(arg_keys[16], (FF,), 0.5, 6.0, ((0, 4),)),
        "down_weight": noise(arg_keys[17], (FF, D), FF ** -0.5, 0.109375, ((0, 4),)),
        "down_bias": noise(arg_keys[18], (D,), 1.0, 6.0, ((0, 4),)),
        "cotangent": noise(arg_keys[19], (SEQS, LENGTH, D), 1.0, 6.0, ((0, 4), (1, 8))),
    }


@jax.custom_vjp
def low(v):
    return lax.optimization_barrier(v.astype(jnp.bfloat16)).astype(jnp.float32)

@jax.custom_vjp
def low_back(v):
    return v

def low_keep(v):
    return (low(v), None)

def low_pass(kept, grad):
    return (grad,)

def back_keep(v):
    return (v, None)

def back_low(kept, grad):
    return (low(grad),)
low.defvjp(low_keep, low_pass)
low_back.defvjp(back_keep, back_low)
HIGHEST = lax.Precision.HIGHEST
NEGATIVE = -1e+30
EPSILON = 1e-05

def layer_norm(values, gain_vector, shift_vector):
    center = values - lax.optimization_barrier(jnp.mean(values, -1, keepdims=True))
    return center * lax.rsqrt(lax.optimization_barrier(jnp.mean(center * center, -1, keepdims=True)) + EPSILON) * gain_vector + shift_vector

def rotary_tables(positions):
    half_rot = ROT // 2
    frequencies = 10000.0 ** (-2.0 * jnp.arange(half_rot, dtype=jnp.float32) / ROT)
    angles = positions.astype(jnp.float32)[:, None] * frequencies[None, :]
    return (jnp.cos(angles), jnp.sin(angles))

def rotate(values, cosine_table, sine_table):
    half_rot = ROT // 2
    first_half = values[..., :half_rot]
    second_half = values[..., half_rot:ROT]
    return jnp.concatenate([first_half * cosine_table - second_half * sine_table, second_half * cosine_table + first_half * sine_table, values[..., ROT:]], -1)

def sequence_layer(params, tokens_seq, positions, documents):
    norm_one_gain, norm_one_bias, query_weight, query_bias, key_weight, key_bias, value_weight, value_bias, out_weight, out_bias, norm_two_gain, norm_two_bias, up_weight, up_bias, down_weight, down_bias = params
    length = tokens_seq.shape[0]
    normed_one = low(layer_norm(tokens_seq, norm_one_gain, norm_one_bias))
    normed_two = low(layer_norm(tokens_seq, norm_two_gain, norm_two_bias))
    cosine_table, sine_table = rotary_tables(positions)
    query_pre = low_back(jnp.dot(normed_one, query_weight, precision=HIGHEST) + query_bias).reshape(length, HEADS, HDIM)
    queries = low(rotate(query_pre, cosine_table[:, None, :], sine_table[:, None, :]))
    key_bias_full = jnp.concatenate([key_bias, jnp.zeros((HDIM - ROT,), key_bias.dtype)])
    key_pre = low_back(jnp.dot(normed_one, key_weight, precision=HIGHEST) + key_bias_full)
    keys_all = low(rotate(key_pre, cosine_table, sine_table))
    values_all = low(low_back(jnp.dot(normed_one, value_weight, precision=HIGHEST) + value_bias))
    rows_block = min(512, length)
    block_count = length // rows_block

    def attend(block_items):
        query_block, query_pos, query_doc = block_items
        scores = low_back(jnp.einsum('qhd,kd->hqk', query_block, keys_all, precision=HIGHEST) * HDIM ** (-0.5))
        allowed = (positions[None, :] <= query_pos[:, None]) & (documents[None, :] == query_doc[:, None])
        scores = jnp.where(allowed[None], scores, NEGATIVE)
        probabilities = jax.nn.softmax(scores, axis=-1)
        return jnp.einsum('hqk,kd->qhd', low(probabilities), values_all, precision=HIGHEST)
    mixed = lax.map(jax.checkpoint(attend), (queries.reshape(block_count, rows_block, HEADS, HDIM), positions.reshape(block_count, rows_block), documents.reshape(block_count, rows_block)))
    attn_low = low(low_back(mixed.reshape(length, HEADS * HDIM)))
    attention = jnp.dot(attn_low, out_weight, precision=HIGHEST) + out_bias
    pre_act = low_back(jnp.dot(normed_two, up_weight.T, precision=HIGHEST) + up_bias)
    hidden = low(jax.nn.gelu(pre_act, approximate=False))
    feed_forward = jnp.dot(hidden, down_weight, precision=HIGHEST) + down_bias
    return tokens_seq + attention + feed_forward

def reference(tokens, block_order, doc_lengths, norm_one_gain, norm_one_bias, query_weight, query_bias, key_weight, key_bias, value_weight, value_bias, out_weight, out_bias, norm_two_gain, norm_two_bias, up_weight, up_bias, down_weight, down_bias, cotangent):
    seq_count = tokens.shape[0]
    length = tokens.shape[1]
    model_width = tokens.shape[2]
    block_len = length // NBLK
    slot_index = jnp.arange(NBLK, dtype=jnp.int32)
    inverse = lax.optimization_barrier(jnp.sum(jnp.where(block_order[None, :] == slot_index[:, None], slot_index[None, :], 0), axis=1)).astype(jnp.int32)

    def to_true(tensor_in):
        return jnp.take(tensor_in.reshape(seq_count, NBLK, block_len, model_width), inverse, axis=1).reshape(seq_count, length, model_width)

    def to_store(tensor_in):
        return jnp.take(tensor_in.reshape(seq_count, NBLK, block_len, model_width), block_order, axis=1).reshape(seq_count, length, model_width)
    positions = jnp.arange(length, dtype=jnp.int32)
    doc_ends = jnp.cumsum(doc_lengths, axis=1).astype(jnp.int32)[:, :-1]
    documents = lax.optimization_barrier(jnp.sum((positions[None, :, None] >= doc_ends[:, None, :]).astype(jnp.int32), axis=2)).astype(jnp.int32)
    params = (norm_one_gain.astype(jnp.float32), norm_one_bias.astype(jnp.float32), query_weight.astype(jnp.float32), query_bias.astype(jnp.float32), key_weight.astype(jnp.float32), key_bias.astype(jnp.float32), value_weight.astype(jnp.float32), value_bias.astype(jnp.float32), out_weight.astype(jnp.float32), out_bias.astype(jnp.float32), norm_two_gain.astype(jnp.float32), norm_two_bias.astype(jnp.float32), up_weight.astype(jnp.float32), up_bias.astype(jnp.float32), down_weight.astype(jnp.float32), down_bias.astype(jnp.float32))
    tokens_true = to_true(tokens.astype(jnp.float32))
    cotangent_true = to_true(cotangent.astype(jnp.float32))

    def whole_layer(params_in, tokens_in):

        def one_sequence(carry_state, inputs):
            return (carry_state, sequence_layer(params_in, inputs[0], positions, inputs[1]))
        return lax.scan(one_sequence, jnp.zeros((), jnp.float32), (tokens_in, documents))[1]
    layer_true, pullback = jax.vjp(whole_layer, params, tokens_true)
    grad_params, grad_true = pullback(cotangent_true)
    layer_out = to_store(layer_true).astype(jnp.bfloat16)
    grad_tokens = to_store(grad_true).astype(jnp.bfloat16)
    return (layer_out, grad_tokens, grad_params[0], grad_params[1], grad_params[2], grad_params[3], grad_params[4], grad_params[5], grad_params[6], grad_params[7], grad_params[8], grad_params[9], grad_params[10], grad_params[11], grad_params[12], grad_params[13], grad_params[14], grad_params[15])
```

```python
import functools

import jax
import jax.numpy as jnp
from jax import lax
from jax.experimental import pallas as pl
from jax.experimental.pallas import tpu as pltpu
from jax.sharding import PartitionSpec as P

HEADS = 12
HDIM = 64
ROT = 16
HALF = ROT // 2
BLOCK = 128

NEGATIVE = -1e30
EPSILON = 1e-05
SQRT_HALF = 0.7071067811865476
GAUSS_FACTOR = 0.3989422804014327
SCALE = HDIM ** (-0.5)
BF = jnp.bfloat16
F32 = jnp.float32
MIB = 1024 * 1024
VMEM = pl.BlockSpec(memory_space=pltpu.VMEM)
SMEM = pl.BlockSpec(memory_space=pltpu.SMEM)

NN = (((1,), (0,)), ((), ()))
NT = (((1,), (1,)), ((), ()))
TN = (((0,), (0,)), ((), ()))


def dot(left, right, dims=NN):
    return lax.dot_general(left, right, dims, preferred_element_type=F32)


def shape(dims, dtype):
    return jax.ShapeDtypeStruct(dims, dtype)


def params(limit=48):
    return pltpu.CompilerParams(vmem_limit_bytes=limit * MIB)


def cost(flops, data, special=0):
    return pl.CostEstimate(flops=flops, bytes_accessed=data, transcendentals=special)


def swap(value, axis, bit):
    size = lax.axis_size(axis)
    return lax.ppermute(value, axis, [(i, i ^ bit) for i in range(size)])


def bits_of(size):
    return [1 << i for i in range(size.bit_length() - 1)]


def normalize(values):
    center = values - jnp.mean(values, -1, keepdims=True)
    inverse_std = lax.rsqrt(jnp.mean(center * center, -1, keepdims=True) + EPSILON)
    return (center * inverse_std, inverse_std)


def pick(pieces, index):
    result = pieces[-1]
    for i in range(len(pieces) - 2, -1, -1):
        result = jnp.where(index == i, pieces[i], result)
    return result


def rel_order(size):
    order = [0]
    for bit in reversed(bits_of(size)):
        order = order + [r ^ bit for r in order]
    return order


def front_kernel(rels, x_ref, *refs):
    count = len(rels)
    packs = refs[:count]
    cs_ref, n1_ref, kv_ref, vec_ref, wkv_ref, pieces = refs[count:]
    me = lax.axis_index("fsdp")
    part = packs[0].shape[0] - 16
    for rel, pack in zip(rels, packs):
        wkv_ref[pl.ds((rel ^ me) * part, part), :] = pack[:part, : 2 * HDIM]
        pieces[rel ^ me] = pack[part:, :].astype(F32)
    vec = jnp.concatenate([pieces[p] for p in range(count)], axis=1)
    vec_ref[...] = vec
    normal, _ = normalize(x_ref[...].astype(F32))
    n1 = (normal * vec[0:1] + vec[1:2]).astype(BF)
    n1_ref[...] = n1
    key_part, value_part = ROT // count, HDIM // count
    key_bias = jnp.concatenate([pieces[p][7:8, :key_part] for p in range(count)], axis=1)
    value_bias = jnp.concatenate(
        [pieces[p][7:8, key_part : key_part + value_part] for p in range(count)], axis=1
    )
    bias = jnp.concatenate([key_bias, jnp.zeros((1, HDIM - ROT), F32), value_bias], axis=1)
    turned = (dot(n1, wkv_ref[...]) + bias).T
    cosine, sine = cs_ref[:HALF], cs_ref[HALF:]
    first, second = turned[:HALF], turned[HALF:ROT]
    turned = jnp.concatenate(
        [first * cosine - second * sine, second * cosine + first * sine, turned[ROT:]], axis=0
    )
    kv_ref[...] = turned.T.astype(BF)


def query_kernel(n1_ref, dy_ref, wq_ref, wo_ref, vec_ref, cs_ref, qt_ref, dot_ref):
    width = wq_ref.shape[1]
    turned = (dot(n1_ref[...], wq_ref[...]) + vec_ref[4:5]).T
    cosine, sine = cs_ref[:HALF], cs_ref[HALF:]
    for h in range(HEADS):
        base = h * HDIM
        first, second = turned[base : base + HALF], turned[base + HALF : base + ROT]
        head = jnp.concatenate(
            [
                first * cosine - second * sine,
                second * cosine + first * sine,
                turned[base + ROT : base + HDIM],
            ],
            axis=0,
        )
        qt_ref[base : base + HDIM, :] = (head.astype(BF).astype(F32) * SCALE).astype(BF)
    dot_ref[...] = dot(dy_ref[...], wo_ref[...], NT).T.astype(BF)


def mlp_kernel(rels, seq_orders, shards, *refs):
    count = len(rels)
    xs = refs[:count]
    dys = refs[count : 2 * count]
    (
        up_ref,
        down_ref,
        ub_ref,
        vec_ref,
        keep_ref,
        send_ref,
        n1c_ref,
        upk_ref,
        ups_ref,
        dnk_ref,
        dns_ref,
        sums_ref,
        x_s,
        dy_s,
        acc_up,
        acc_dn,
        acc_v,
    ) = refs[2 * count :]
    step = pl.program_id(0)
    me = lax.axis_index("fsdp")
    seq_me = lax.axis_index("seq")
    width = up_ref.shape[1]
    hidden = up_ref.shape[0]
    sequence = rels[count // 2 :] + rels[: count // 2]
    for g, rel in enumerate(sequence):
        index = rels.index(rel)

        @pl.when(step == g)
        def _():
            x_s[...] = xs[index][...].astype(F32)
            dy_s[...] = dys[index][...]

    @pl.when(step == 0)
    def _():
        acc_up[...] = jnp.zeros_like(acc_up)
        acc_dn[...] = jnp.zeros_like(acc_dn)
        acc_v[...] = jnp.zeros_like(acc_v)

    rel_now = pick([jnp.int32(r) for r in sequence], step)
    normal, _ = normalize(x_s[...])
    part = width // count
    n1 = (normal * vec_ref[0:1] + vec_ref[1:2])
    n1c_ref[rel_now ^ me] = pick(
        [n1[:, p * part : (p + 1) * part] for p in range(count)], me
    ).astype(BF)
    n2 = (normal * vec_ref[2:3] + vec_ref[3:4]).astype(BF)
    dy = dy_s[...]
    out = None
    dn2 = None
    tile = 256
    for c in range(hidden // tile):
        rows = slice(c * tile, (c + 1) * tile)
        up_c, down_c = up_ref[rows, :], down_ref[rows, :]
        u = dot(n2, up_c, NT) + ub_ref[:, rows].astype(F32)
        dg = dot(dy, down_c, NT)
        phi = 0.5 * (1.0 + lax.erf(u * SQRT_HALF))
        g = (u * phi).astype(BF)
        du = (dg * (phi + u * jnp.exp(-0.5 * u * u) * GAUSS_FACTOR)).astype(BF)
        out_c = dot(g, down_c)
        dn2_c = dot(du, up_c)
        out = out_c if out is None else out + out_c
        dn2 = dn2_c if dn2 is None else dn2 + dn2_c
        acc_dn[rows, :] += dot(g, dy, TN)
        acc_up[rows, :] += dot(du, n2, TN)
        acc_v[2:3, rows] += jnp.sum(du.astype(F32), axis=0, keepdims=True)
    acc_v[0:1, :width] += jnp.sum(dn2 * normal, axis=0, keepdims=True)
    acc_v[1:2, :width] += jnp.sum(dn2, axis=0, keepdims=True)
    out_low = out.astype(BF)
    h_low = (dn2 * vec_ref[2:3]).astype(BF)

    @pl.when(step < count // 2)
    def _():
        send_ref[0, 0] = out_low
        send_ref[0, 1] = h_low

    @pl.when(step >= count // 2)
    def _():
        keep_ref[0, 0] = out_low
        keep_ref[0, 1] = h_low

    @pl.when(step == count - 1)
    def _():
        sums_ref[...] = acc_v[...]
        rows = hidden // shards
        for acc, order, near, far in (
            (acc_up, seq_orders[0], upk_ref, ups_ref),
            (acc_dn, seq_orders[1], dnk_ref, dns_ref),
        ):
            for m in range(shards):
                source = (order[m] ^ seq_me) & (shards - 1)
                value = acc[pl.ds(pl.multiple_of(source * rows, rows), rows), :].astype(BF)
                half = shards // 2
                target = near if m < half else far
                target[(m % half) * rows : (m % half + 1) * rows, :] = value


def attend_kernel(
    per_group,
    chunk_blocks,
    most,
    order_ref,
    len_ref,
    qt_ref,
    dot_ref,
    kv_ref,
    cs_ref,
    o_ref,
    dq_ref,
    dkv_ref,
    s_scr,
    p_scr,
    pb_scr,
    ds_scr,
    bias_scr,
    kv_scr,
    dkv_scr,
    qs,
    dos,
    ot,
    dqt,
    inverse,
):
    side, group = pl.program_id(0), pl.program_id(1)
    seq_me = lax.axis_index("seq")
    slots = kv_ref.shape[0] // BLOCK
    chunk = chunk_blocks * BLOCK
    lanes = per_group * BLOCK
    first_step = jnp.logical_and(side == 0, group == 0)
    last_step = jnp.logical_and(
        side == pl.num_programs(0) - 1, group == pl.num_programs(1) - 1
    )

    @pl.when(first_step)
    def _():
        dkv_scr[...] = jnp.zeros_like(dkv_scr)

        @pl.loop(0, slots)
        def _(i):
            rel = (i // 2) ^ seq_me
            place = jnp.int32(0)
            for bit in bits_of(slots // 2):
                place = place * 2 + (rel // bit) % 2
            inverse[order_ref[i]] = place * 2 + i % 2

    block = order_ref[2 * seq_me + side]
    base = block * BLOCK
    end_1 = len_ref[0, 0]
    end_2 = end_1 + len_ref[0, 1]
    end_3 = end_2 + len_ref[0, 2]

    def start_of(position):
        low = jnp.where(position >= end_1, end_1, 0)
        low = jnp.where(position >= end_2, end_2, low)
        return jnp.where(position >= end_3, end_3, low)

    q_pos = base + lax.broadcasted_iota(jnp.int32, (1, BLOCK), 1)
    q_start = start_of(q_pos)
    low_block = jnp.maximum(start_of(base) // BLOCK, block - (most - 1))
    chunks = (block - low_block + chunk_blocks) // chunk_blocks

    def slot_of(j):
        return inverse[jnp.minimum(low_block + j, block)]

    @pl.loop(0, chunks * chunk_blocks)
    def _(j):
        kv_scr[pl.ds(j * BLOCK, BLOCK), :] = kv_ref[pl.ds(slot_of(j) * BLOCK, BLOCK), :]

    for h in range(per_group):
        cols = slice(h * BLOCK, (h + 1) * BLOCK)
        qs[:, cols] = qt_ref[h * HDIM : (h + 1) * HDIM, :]
        dos[:, cols] = dot_ref[h * HDIM : (h + 1) * HDIM, :]

    def score_step(c, top):
        kv = kv_scr[pl.ds(c * chunk, chunk), :]
        s_scr[c] = dot(kv[:, :HDIM], qs[...])
        p_scr[c] = dot(kv[:, HDIM:], dos[...])
        k_pos = (low_block + c * chunk_blocks) * BLOCK + lax.broadcasted_iota(
            jnp.int32, (chunk, BLOCK), 0
        )
        allowed = jnp.logical_and(k_pos <= q_pos, k_pos >= q_start)
        bias_scr[...] = jnp.where(allowed, 0.0, NEGATIVE)
        tops = []
        for h in range(per_group):
            cols = slice(h * BLOCK, (h + 1) * BLOCK)
            s = s_scr[c, :, cols] + bias_scr[...]
            s_scr[c, :, cols] = s
            tops.append(jnp.max(s, axis=0, keepdims=True))
        return jnp.maximum(top, jnp.concatenate(tops, axis=1))

    top = lax.fori_loop(0, chunks, score_step, jnp.full((1, lanes), NEGATIVE, F32))

    def weight_step(c, carry):
        total, delta = carry
        totals, deltas = [], []
        for h in range(per_group):
            cols = slice(h * BLOCK, (h + 1) * BLOCK)
            e = jnp.exp(s_scr[c, :, cols] - top[:, cols])
            s_scr[c, :, cols] = e
            totals.append(jnp.sum(e, axis=0, keepdims=True))
            deltas.append(jnp.sum(e * p_scr[c, :, cols], axis=0, keepdims=True))
        return (
            total + jnp.concatenate(totals, axis=1),
            delta + jnp.concatenate(deltas, axis=1),
        )

    zero = jnp.zeros((1, lanes), F32)
    total, delta = lax.fori_loop(0, chunks, weight_step, (zero, zero))
    shrink = 1.0 / total
    delta = delta * shrink
    ot[...] = jnp.zeros_like(ot)
    dqt[...] = jnp.zeros_like(dqt)

    def grad_step(c, _):
        for h in range(per_group):
            cols = slice(h * BLOCK, (h + 1) * BLOCK)
            p = s_scr[c, :, cols] * shrink[:, cols]
            pb_scr[:, cols] = p.astype(BF)
            ds_scr[:, cols] = (p * (p_scr[c, :, cols] - delta[:, cols])).astype(BF)
        kv = kv_scr[pl.ds(c * chunk, chunk), :]
        ot[...] += dot(kv[:, HDIM:], pb_scr[...], TN)
        dqt[...] += dot(kv[:, :HDIM], ds_scr[...], TN)
        dk = dot(ds_scr[...], qs[...], NT)
        dv = dot(pb_scr[...], dos[...], NT)
        both = jnp.concatenate([dk, dv], axis=1)
        for b in range(chunk_blocks):

            @pl.when(low_block + c * chunk_blocks + b <= block)
            def _():
                place = slot_of(c * chunk_blocks + b) * BLOCK
                dkv_scr[pl.ds(pl.multiple_of(place, BLOCK), BLOCK), :] += both[
                    b * BLOCK : (b + 1) * BLOCK
                ]

        return 0

    lax.fori_loop(0, chunks, grad_step, 0)
    cosine, sine = cs_ref[:HALF], cs_ref[HALF:]
    outs, grads = [], []
    for h in range(per_group):
        cols = slice(h * BLOCK, (h + 1) * BLOCK)
        outs.append(ot[:, cols])
        grad = dqt[:, cols] * SCALE
        first, second = grad[:HALF], grad[HALF:ROT]
        grads.append(first * cosine + second * sine)
        grads.append(second * cosine - first * sine)
        grads.append(grad[ROT:])
    o_ref[...] = jnp.concatenate(outs, axis=0).T.astype(BF)
    dq_ref[...] = jnp.concatenate(grads, axis=0).T.astype(BF)

    @pl.when(last_step)
    def _():
        dkv_ref[...] = dkv_scr[...].astype(dkv_ref.dtype)


def output_kernel(x_ref, o_ref, wo_ref, vec_ref, near_ref, far_ref, layer_ref):
    mlp = near_ref[...].astype(F32) + far_ref[...].astype(F32)
    attention = dot(o_ref[...], wo_ref[...]) + vec_ref[5:6]
    layer_ref[...] = (x_ref[...].astype(F32) + attention + mlp + vec_ref[6:7]).astype(BF)


def weight_kernel(rels, n1c_ref, dq_ref, o_ref, *refs):
    count = len(rels)
    dys = refs[:count]
    (grad_ref,) = refs[count:]
    me = lax.axis_index("fsdp")
    part = n1c_ref.shape[2]
    rows = dys[0].shape[0]
    grad_q = None
    grad_o = None
    for p in range(count):
        term = dot(n1c_ref[p], dq_ref[p * rows : (p + 1) * rows, :], TN)
        grad_q = term if grad_q is None else grad_q + term
    for rel, dy_ref in zip(rels, dys):
        start = pl.multiple_of((rel ^ me) * rows, rows)
        o = o_ref[pl.ds(start, rows), :]
        cols = pick([o[:, p * part : (p + 1) * part] for p in range(count)], me)
        term = dot(cols, dy_ref[...], TN)
        grad_o = term if grad_o is None else grad_o + term
    grad_ref[:part] = grad_q.astype(BF)
    grad_ref[part:] = grad_o.astype(BF)


def tail_kernel(
    rels,
    x_ref,
    dy_ref,
    n1_ref,
    dq_ref,
    wq_ref,
    wkv_ref,
    vec_ref,
    cs_ref,
    near_ref,
    far_ref,
    dkvn_ref,
    dkvf_ref,
    sums_ref,
    grad_ref,
    keep_ref,
    send_ref,
    wg_s,
    vs,
):
    count = len(rels)
    me = lax.axis_index("fsdp")
    dkv = (dkvn_ref[...].astype(F32) + dkvf_ref[...].astype(F32)).T
    cosine, sine = cs_ref[:HALF], cs_ref[HALF:]
    first, second = dkv[:HALF], dkv[HALF:ROT]
    dkv = jnp.concatenate(
        [first * cosine + second * sine, second * cosine - first * sine, dkv[ROT:]], axis=0
    )
    dkv = dkv.T.astype(BF)
    dq = dq_ref[...]
    dn1 = dot(dq, wq_ref[...], NT) + dot(dkv, wkv_ref[...], NT)
    normal, inverse_std = normalize(x_ref[...].astype(F32))
    dy = dy_ref[...].astype(F32)
    total = near_ref[...].astype(F32) + far_ref[...].astype(F32) + dn1 * vec_ref[0:1]
    grad_ref[...] = (
        dy
        + inverse_std
        * (
            total
            - jnp.mean(total, -1, keepdims=True)
            - normal * jnp.mean(total * normal, -1, keepdims=True)
        )
    ).astype(BF)
    wg_s[...] = dot(n1_ref[...], dkv, TN)
    width = x_ref.shape[1]
    part = width // count
    dkv_sum = jnp.sum(dkv.astype(F32), axis=0, keepdims=True)
    vec = jnp.concatenate(
        [
            jnp.sum(dn1 * normal, axis=0, keepdims=True),
            jnp.sum(dn1, axis=0, keepdims=True),
            sums_ref[0:1, :width],
            sums_ref[1:2, :width],
            jnp.sum(dq.astype(F32), axis=0, keepdims=True),
            jnp.sum(dy, axis=0, keepdims=True),
        ],
        axis=0,
    )
    lanes = 128
    chunks = -(-part // lanes)
    for p in range(count):
        piece = vec[:, p * part : (p + 1) * part]
        piece = jnp.concatenate([piece, jnp.zeros((6, chunks * lanes - part), F32)], axis=1)
        for c in range(chunks):
            vs[p, c * 8 : c * 8 + 6, :] = piece[:, c * lanes : (c + 1) * lanes]
            vs[p, c * 8 + 6 : c * 8 + 7, :] = dkv_sum
            vs[p, c * 8 + 7 : c * 8 + 8, :] = jnp.zeros((1, lanes), F32)
    half = count // 2
    extra = sums_ref.shape[1] // lanes
    top = part + 8 * chunks
    for m, rel in enumerate(rels):
        target = keep_ref if m < half else send_ref
        place = m % half
        target[place, :part] = wg_s[pl.ds(pl.multiple_of((rel ^ me) * part, part), part), :]
        target[place, part:top] = vs[rel ^ me]
        for e in range(target.shape[1] - top):
            if rel == 0 and e < extra:
                row = sums_ref[2:3, e * lanes : (e + 1) * lanes]
            else:
                row = jnp.zeros((1, lanes), F32)
            target[place, top + e : top + e + 1] = row


def final_kernel(seq_orders, shards, upn, upf, dnn, dnf, gup_ref, gdn_ref):
    step = pl.program_id(0)
    seq_me = lax.axis_index("seq")
    rows = gup_ref.shape[0]
    half = shards // 2
    for order, near, far, target in (
        (seq_orders[0], upn, upf, gup_ref),
        (seq_orders[1], dnn, dnf, gdn_ref),
    ):
        wanted = (step ^ seq_me) & (shards - 1)
        place = jnp.int32(0)
        for m, rel in enumerate(order):
            place = jnp.where(wanted == rel, m, place)

        @pl.when(place < half)
        def _():
            start = pl.multiple_of(place * rows, rows)
            target[...] = near[pl.ds(start, rows), :].astype(F32)

        @pl.when(place >= half)
        def _():
            start = pl.multiple_of((place - half) * rows, rows)
            target[...] = far[pl.ds(start, rows), :].astype(F32)


def shard_order(bits):
    order = [0]
    for bit in reversed(bits):
        order = order + [r ^ bit for r in order]
    return order


def reduce_shards(near, far, bits, rest):
    for index, bit in enumerate(bits):
        value = near + swap(far, "seq", bit)
        if index + 1 < len(bits):
            half = value.shape[0] // 2
            near, far = value[:half], value[half:]
    for bit in rest:
        value = value + swap(value, "seq", bit)
    for index, bit in enumerate(reversed(bits)):
        other = swap(value, "seq", bit)
        if index + 1 < len(bits):
            value = jnp.concatenate([value, other], axis=0)
    return (value, other)


def on_device(
    tokens,
    block_order,
    doc_lengths,
    norm_one_gain,
    norm_one_bias,
    query_weight,
    query_bias,
    key_weight,
    key_bias,
    value_weight,
    value_bias,
    out_weight,
    out_bias,
    norm_two_gain,
    norm_two_bias,
    up_weight,
    up_bias,
    down_weight,
    down_bias,
    cotangent,
):
    _, rows, width = tokens.shape
    hidden = up_weight.shape[0]
    part = query_weight.shape[0]
    fsdp = lax.axis_size("fsdp")
    seqs = lax.axis_size("seq")
    slots = 2 * seqs
    fbits = bits_of(fsdp)
    sbits = bits_of(seqs)
    rels = rel_order(fsdp)
    fsdp_me = lax.axis_index("fsdp")
    seq_me = lax.axis_index("seq")
    x_own = tokens.reshape(rows, width)
    dy_own = cotangent.reshape(rows, width)

    def spread(value):
        parts = [value]
        for bit in reversed(fbits):
            parts = parts + [swap(v, "fsdp", bit) for v in parts]
        return parts

    small = jnp.concatenate(
        [key_bias, value_bias, jnp.zeros((part - key_bias.shape[0] - value_bias.shape[0],), BF)]
    )
    vectors = jnp.stack(
        [
            norm_one_gain,
            norm_one_bias,
            norm_two_gain,
            norm_two_bias,
            query_bias,
            out_bias,
            down_bias,
            small,
        ]
        + [jnp.zeros((part,), BF)] * 8
    )
    weights = jnp.concatenate(
        [key_weight, value_weight, jnp.zeros((part, part - 2 * HDIM), BF)], axis=1
    )
    packs = spread(jnp.concatenate([weights, vectors], axis=0))
    xs = spread(x_own)
    dys = spread(dy_own)
    wq = lax.all_gather(query_weight, "fsdp", axis=0, tiled=True)
    wo = lax.all_gather(out_weight, "fsdp", axis=0, tiled=True)

    own_blocks = lax.dynamic_slice_in_dim(block_order, 2 * seq_me, 2)
    offsets = jnp.arange(BLOCK, dtype=jnp.int32)
    own_pos = (own_blocks[:, None] * BLOCK + offsets[None, :]).reshape(rows)
    frequencies = 10000.0 ** (-2.0 * jnp.arange(HALF, dtype=F32) / ROT)
    angles = own_pos.astype(F32)[None, :] * frequencies[:, None]
    cs = jnp.concatenate([jnp.cos(angles), jnp.sin(angles)], axis=0)

    n1, kv_own, vec, wkv = pl.pallas_call(
        functools.partial(front_kernel, rels),
        out_shape=(
            shape((rows, width), BF),
            shape((rows, 2 * HDIM), BF),
            shape((16, width), F32),
            shape((width, 2 * HDIM), BF),
        ),
        in_specs=[VMEM] * (2 + fsdp),
        out_specs=(VMEM,) * 4,
        scratch_shapes=[pltpu.VMEM((fsdp, 16, part), F32)],
        compiler_params=params(),
        cost_estimate=cost(2 * rows * width * 128, 3 * MIB // 2),
        name="front",
    )(x_own, *packs, cs)

    kv = kv_own[None]
    for bit in reversed(sbits):
        kv = jnp.concatenate([kv, swap(kv, "seq", bit)], axis=0)
    kv_all = kv.reshape(seqs * rows, 2 * HDIM)

    shards = seqs
    while (hidden // shards) % 16:
        shards //= 2
    low_bits = [b for b in sbits if b < shards]
    rest_bits = [b for b in sbits if b >= shards]
    up_bits = low_bits
    down_bits = low_bits[1:] + low_bits[:1]
    seq_orders = (shard_order(up_bits), shard_order(down_bits))
    half = fsdp // 2
    mlp_flops = 12 * fsdp * rows * width * hidden
    keep, send, n1c, upk, ups, dnk, dns, sums = pl.pallas_call(
        functools.partial(mlp_kernel, rels, seq_orders, shards),
        grid=(fsdp,),
        out_shape=(
            shape((half, 2, rows, width), BF),
            shape((half, 2, rows, width), BF),
            shape((fsdp, rows, part), BF),
            shape((hidden // 2, width), BF),
            shape((hidden // 2, width), BF),
            shape((hidden // 2, width), BF),
            shape((hidden // 2, width), BF),
            shape((8, max(hidden, width)), F32),
        ),
        in_specs=[VMEM] * (2 * fsdp + 4),
        out_specs=(
            pl.BlockSpec((1, 2, rows, width), lambda g: (jnp.maximum(g - half, 0), 0, 0, 0)),
            pl.BlockSpec((1, 2, rows, width), lambda g: (jnp.minimum(g, half - 1), 0, 0, 0)),
        )
        + (VMEM,) * 6,
        scratch_shapes=[
            pltpu.VMEM((rows, width), F32),
            pltpu.VMEM((rows, width), BF),
            pltpu.VMEM((hidden, width), F32),
            pltpu.VMEM((hidden, width), F32),
            pltpu.VMEM((8, max(hidden, width)), F32),
        ],
        compiler_params=params(),
        cost_estimate=cost(mlp_flops, 12 * MIB, 2 * fsdp * rows * hidden),
        name="mlp",
    )(*xs, *dys, up_weight, down_weight, up_bias.reshape(1, hidden), vec)

    qt, do_t = pl.pallas_call(
        query_kernel,
        out_shape=(shape((width, rows), BF), shape((width, rows), BF)),
        in_specs=[VMEM] * 6,
        out_specs=(VMEM, VMEM),
        compiler_params=params(),
        cost_estimate=cost(4 * rows * width * width, 4 * MIB),
        name="query",
    )(n1, dy_own, wq, wo, vec, cs)

    most = min(slots, slots // 2 + 1)
    chunk_blocks = 2
    most_chunks = -(-most // chunk_blocks)
    chunk = chunk_blocks * BLOCK
    per_group = HEADS
    while most_chunks * chunk * per_group * BLOCK * 8 > 20 * MIB and per_group > 2:
        per_group = {12: 6, 6: 4, 4: 2}[per_group]
    lanes = per_group * BLOCK
    span = per_group * HDIM
    own, dq, dkv = pl.pallas_call(
        functools.partial(attend_kernel, per_group, chunk_blocks, most),
        grid=(2, HEADS // per_group),
        out_shape=(
            shape((rows, width), BF),
            shape((rows, width), BF),
            shape((slots * BLOCK, 2 * HDIM), BF),
        ),
        in_specs=[
            SMEM,
            SMEM,
            pl.BlockSpec((span, BLOCK), lambda i, g: (g, i)),
            pl.BlockSpec((span, BLOCK), lambda i, g: (g, i)),
            VMEM,
            pl.BlockSpec((ROT, BLOCK), lambda i, g: (0, i)),
        ],
        out_specs=(
            pl.BlockSpec((BLOCK, span), lambda i, g: (i, g)),
            pl.BlockSpec((BLOCK, span), lambda i, g: (i, g)),
            VMEM,
        ),
        scratch_shapes=[
            pltpu.VMEM((most_chunks, chunk, lanes), F32),
            pltpu.VMEM((most_chunks, chunk, lanes), F32),
            pltpu.VMEM((chunk, lanes), BF),
            pltpu.VMEM((chunk, lanes), BF),
            pltpu.VMEM((chunk, BLOCK), F32),
            pltpu.VMEM((most_chunks * chunk, 2 * HDIM), BF),
            pltpu.VMEM((slots * BLOCK, 2 * HDIM), F32),
            pltpu.VMEM((HDIM, lanes), BF),
            pltpu.VMEM((HDIM, lanes), BF),
            pltpu.VMEM((HDIM, lanes), F32),
            pltpu.VMEM((HDIM, lanes), F32),
            pltpu.SMEM((slots,), jnp.int32),
        ],
        compiler_params=params(56),
        cost_estimate=cost(24 * slots * BLOCK * BLOCK * width, 8 * MIB, slots * BLOCK * BLOCK * 12),
        name="attend",
    )(block_order, doc_lengths, qt, do_t, kv_all, cs)

    near, far = keep, send
    for index, bit in enumerate(fbits):
        if index + 1 < len(fbits):
            value = near + swap(far, "fsdp", bit)
            near, far = value[: value.shape[0] // 2], value[value.shape[0] // 2 :]
        else:
            far = swap(far, "fsdp", bit)
    near, far = near[0], far[0]

    layer_out = pl.pallas_call(
        output_kernel,
        out_shape=shape((rows, width), BF),
        in_specs=[VMEM] * 6,
        out_specs=VMEM,
        compiler_params=params(),
        cost_estimate=cost(2 * rows * width * width, 3 * MIB),
        name="output",
    )(x_own, own, wo, vec, near[0], far[0])

    gup = reduce_shards(upk, ups, up_bits, rest_bits)
    gdn = reduce_shards(dnk, dns, down_bits, rest_bits)

    o_all = lax.all_gather(own, "fsdp", axis=0, tiled=True)
    dq_all = lax.all_gather(dq, "fsdp", axis=0, tiled=True)
    gqo = pl.pallas_call(
        functools.partial(weight_kernel, rels),
        out_shape=shape((2 * part, width), BF),
        in_specs=[VMEM] * (3 + fsdp),
        out_specs=VMEM,
        compiler_params=params(),
        cost_estimate=cost(4 * fsdp * rows * part * width, 6 * MIB),
        name="weight",
    )(n1c, dq_all, o_all, *dys)
    gqo = lax.psum(gqo, "seq").astype(F32)

    value = dkv
    for index, bit in enumerate(sbits):
        split = value.shape[0] // 2
        near_kv, far_kv = value[:split], swap(value[split:], "seq", bit)
        if index + 1 < len(sbits):
            value = near_kv + far_kv

    extra = -(-hidden // 128)
    chunks = -(-part // 128)
    height = part + 8 * chunks + -(-extra // 8) * 8
    grad_tokens, keep_t, send_t = pl.pallas_call(
        functools.partial(tail_kernel, rels),
        out_shape=(
            shape((rows, width), BF),
            shape((half, height, 128), F32),
            shape((half, height, 128), F32),
        ),
        in_specs=[VMEM] * 13,
        out_specs=(VMEM, VMEM, VMEM),
        scratch_shapes=[
            pltpu.VMEM((width, 2 * HDIM), F32),
            pltpu.VMEM((fsdp, 8 * chunks, 128), F32),
        ],
        compiler_params=params(),
        cost_estimate=cost(2 * rows * width * (width + 256), 5 * MIB),
        name="tail",
    )(x_own, dy_own, n1, dq, wq, wkv, vec, cs, near[1], far[1], near_kv, far_kv, sums)

    near_t, far_t = keep_t, send_t
    for index, bit in enumerate(fbits):
        value = near_t + swap(far_t, "fsdp", bit)
        near_t, far_t = value[: value.shape[0] // 2], value[value.shape[0] // 2 :]
    value = value[0]
    for bit in sbits:
        value = value + swap(value, "seq", bit)

    shard_rows = hidden // shards
    grad_up, grad_down = pl.pallas_call(
        functools.partial(final_kernel, seq_orders, shards),
        grid=(shards,),
        out_shape=(shape((hidden, width), F32), shape((hidden, width), F32)),
        in_specs=[VMEM] * 4,
        out_specs=(
            pl.BlockSpec((shard_rows, width), lambda g: (g, 0)),
            pl.BlockSpec((shard_rows, width), lambda g: (g, 0)),
        ),
        compiler_params=params(),
        cost_estimate=cost(0, 8 * MIB),
        name="final",
    )(*gup, *gdn)

    kv_grad = value[:part]
    lines = value[part : part + 8 * chunks].reshape(chunks, 8, 128)
    lines = jnp.moveaxis(lines, 0, 1).reshape(8, chunks * 128)
    dkv_line = value[part + 6]
    key_part, value_part = key_bias.shape[0], value_bias.shape[0]
    grad_up_bias = value[part + 8 * chunks :].reshape(-1)[:hidden]
    vec_out = [lines[i, :part] for i in range(6)]
    grad_key_bias = lax.dynamic_slice_in_dim(dkv_line, fsdp_me * key_part, key_part)
    grad_value_bias = lax.dynamic_slice_in_dim(dkv_line, HDIM + fsdp_me * value_part, value_part)
    return (
        layer_out.reshape(1, rows, width),
        grad_tokens.reshape(1, rows, width),
        vec_out[0],
        vec_out[1],
        gqo[:part],
        vec_out[4],
        kv_grad[:, :HDIM],
        grad_key_bias,
        kv_grad[:, HDIM:],
        grad_value_bias,
        gqo[part:],
        vec_out[5],
        vec_out[2],
        vec_out[3],
        grad_up,
        grad_up_bias,
        grad_down,
        vec_out[5],
    )


def solution(mesh):
    split = P("fsdp")
    matrix = P("fsdp", None)
    stream = P("fsdp", "seq", None)
    return jax.shard_map(
        on_device,
        mesh=mesh,
        in_specs=(
            stream,
            P(),
            matrix,
            split,
            split,
            matrix,
            split,
            matrix,
            split,
            matrix,
            split,
            matrix,
            split,
            split,
            split,
            matrix,
            split,
            matrix,
            split,
            stream,
        ),
        out_specs=(
            stream,
            stream,
            split,
            split,
            matrix,
            split,
            matrix,
            split,
            matrix,
            split,
            matrix,
            split,
            split,
            split,
            matrix,
            split,
            matrix,
            split,
        ),
        check_vma=False,
    )
```

```python
import functools

import jax
import jax.numpy as jnp
from jax import lax
from jax.experimental import pallas as pl
from jax.experimental.pallas import tpu as pltpu
from jax.sharding import PartitionSpec as P

HEADS = 12
HDIM = 64
ROT = 16
HALF = ROT // 2
BLOCK = 128

NEGATIVE = -1e30
EPSILON = 1e-05
SQRT_HALF = 0.7071067811865476
GAUSS_FACTOR = 0.3989422804014327
SCALE = HDIM ** (-0.5)
BF = jnp.bfloat16
F32 = jnp.float32
MIB = 1024 * 1024
VMEM = pl.BlockSpec(memory_space=pltpu.VMEM)
SMEM = pl.BlockSpec(memory_space=pltpu.SMEM)
ANY = pl.BlockSpec(memory_space=pl.ANY)
HBM = pl.BlockSpec(memory_space=pltpu.HBM)

NN = (((1,), (0,)), ((), ()))
NT = (((1,), (1,)), ((), ()))
TN = (((0,), (0,)), ((), ()))


def dot(left, right, dims=NN):
    return lax.dot_general(left, right, dims, preferred_element_type=F32)


def shape(dims, dtype):
    return jax.ShapeDtypeStruct(dims, dtype)


def params(limit=48):
    return pltpu.CompilerParams(vmem_limit_bytes=limit * MIB)


def micros(time):
    return pl.CostEstimate(flops=time * 1000000000, bytes_accessed=1000, transcendentals=0)


class Sequence:
    def __init__(self):
        self.last = ()

    def run(self, kernel, outs, ins, scratch=(), limit=16, name=None, after=(), time=1, **specs):
        single = isinstance(outs, jax.ShapeDtypeStruct)
        self.last = self.last + tuple(after)
        count, extra = len(ins), len(self.last)

        def body(*refs):
            kernel(*refs[:count], *refs[count + extra :])

        results = pl.pallas_call(
            body,
            out_shape=outs,
            in_specs=list(specs.get("in_specs", [VMEM] * count)) + [ANY] * extra,
            out_specs=specs.get("out_specs", VMEM if single else (VMEM,) * len(outs)),
            grid=specs.get("grid", ()),
            scratch_shapes=list(scratch),
            compiler_params=params(limit),
            cost_estimate=micros(time),
            name=name,
        )(*ins, *self.last)
        self.last = (min((results,) if single else results, key=lambda v: v.size),)
        return results

    def stage(self, *tasks):
        ins, outs, plan = [], [], []
        for kind, arrays, parts in tasks:
            rows = arrays[0].shape[0] if kind is not join_step else sum(v.shape[0] for v in arrays)
            plan.append((kind, len(arrays), parts))
            ins.extend(arrays)
            outs.extend([shape((rows // parts,) + arrays[0].shape[1:], BF)] * parts)

        def kernel(*refs):
            sources, targets = refs[: len(ins)], refs[len(ins) :]
            for kind, count, parts in plan:
                kind(sources[:count], targets[:parts])
                sources, targets = sources[count:], targets[parts:]

        results = list(self.run(kernel, tuple(outs), ins, name="stage"))
        grouped = []
        for _, _, parts in plan:
            grouped.append(results[:parts])
            results = results[parts:]
        return grouped


class Sum:
    def __init__(self, near, far, bits, rest):
        self.near, self.coming = near, swap(far, "seq", bits[0])
        self.plan = [(bit, 2) for bit in bits[1:]] + [(bit, 1) for bit in rest]
        self.plan += [(bits[-1], 0)] + [(bit, -1) for bit in reversed(bits[:-1])]

    def left(self):
        return len(self.plan)

    def task(self):
        parts = self.plan[0][1]
        if parts == -1:
            return (join_step, [self.near, self.coming], 1)
        return (merge_step, [self.near, self.coming], max(parts, 1))

    def give(self, results):
        bit = self.plan.pop(0)[0]
        self.near = results[0]
        self.coming = swap(results[-1], "seq", bit)

    def pair(self):
        return (self.near, self.coming)


class Reduce(Sum):
    def __init__(self, near, far, bits):
        Sum.__init__(self, near, far, bits, [])
        self.plan = self.plan[: len(bits) - 1]


class Mix(Sum):
    def __init__(self, near, far, fbits, sbits):
        self.near, self.coming = near, swap(far, "fsdp", fbits[0])
        self.plan = [("fsdp", bit, 2) for bit in fbits[1:]] + [("seq", bit, 1) for bit in sbits]

    def task(self):
        return (mix_step, [self.near, self.coming], self.plan[0][2])

    def give(self, results):
        axis, bit, _ = self.plan.pop(0)
        self.near = results[0]
        self.coming = swap(results[-1], axis, bit)


def advance(sequence, *items, extra=()):
    results = sequence.stage(*[item.task() for item in items], *extra)
    for item, result in zip(items, results):
        item.give(result)
    return [result[0] for result in results[len(items) :]]


def swap(value, axis, bit):
    size = lax.axis_size(axis)
    return lax.ppermute(value, axis, [(i, i ^ bit) for i in range(size)])


def bits_of(size):
    return [1 << i for i in range(size.bit_length() - 1)]


def normalize(values):
    center = values - jnp.mean(values, -1, keepdims=True)
    inverse_std = lax.rsqrt(jnp.mean(center * center, -1, keepdims=True) + EPSILON)
    return (center * inverse_std, inverse_std)


def pick(pieces, index):
    result = pieces[-1]
    for i in range(len(pieces) - 2, -1, -1):
        result = jnp.where(index == i, pieces[i], result)
    return result


def rel_order(size):
    order = [0]
    for bit in reversed(bits_of(size)):
        order = order + [r ^ bit for r in order]
    return order


def pack_kernel(*refs):
    count = len(refs) // 2
    pack_ref, both_ref, sems = refs[count], refs[count + 1], refs[-1]
    rows = refs[0].shape[0]
    held = (both_ref.at[:rows], both_ref.at[rows:]) + refs[count + 2 : -1]
    copies = [
        pltpu.make_async_copy(refs[i], held[i], sems.at[i]) for i in range(count)
    ]
    for copy in copies:
        copy.start()
    for copy in copies:
        copy.wait()
    g1, b1, g2, b2, qb, ob, db, kb, vb, wk_ref, wv_ref = held[2:]
    part = g1.shape[0]
    small = jnp.concatenate(
        [
            kb[...].astype(F32).reshape(1, kb.shape[0]),
            vb[...].astype(F32).reshape(1, vb.shape[0]),
            jnp.zeros((1, part - kb.shape[0] - vb.shape[0]), F32),
        ],
        axis=1,
    )
    lines = [ref[...].astype(F32).reshape(1, part) for ref in (g1, b1, g2, b2, qb, ob, db)]
    lines = jnp.concatenate(lines + [small, jnp.zeros((8, part), F32)], axis=0)
    pack_ref[:HDIM] = wk_ref[...]
    pack_ref[HDIM : 2 * HDIM] = wv_ref[...]
    pack_ref[2 * HDIM :] = lines.astype(BF)


def front_kernel(rels, x_ref, *refs):
    count = len(rels)
    packs = refs[:count]
    cs_ref, n1_ref, kv_ref, vec_ref, wkv_ref, pieces, weights = refs[count:]
    me = lax.axis_index("fsdp")
    for rel, pack in zip(rels, packs):
        weights[rel ^ me] = pack[: 2 * HDIM, :]
        pieces[rel ^ me] = pack[2 * HDIM :, :].astype(F32)
    wkv = jnp.concatenate([weights[p] for p in range(count)], axis=1)
    wkv_ref[...] = wkv
    vec = jnp.concatenate([pieces[p] for p in range(count)], axis=1)
    vec_ref[...] = vec
    normal, _ = normalize(x_ref[...].astype(F32))
    n1 = (normal * vec[0:1] + vec[1:2]).astype(BF)
    n1_ref[...] = n1
    key_part, value_part = ROT // count, HDIM // count
    key_bias = jnp.concatenate([pieces[p][7:8, :key_part] for p in range(count)], axis=1)
    value_bias = jnp.concatenate(
        [pieces[p][7:8, key_part : key_part + value_part] for p in range(count)], axis=1
    )
    bias = jnp.concatenate([key_bias, jnp.zeros((1, HDIM - ROT), F32), value_bias], axis=1)
    turned = (dot(n1, wkv, NT) + bias).T
    cosine, sine = cs_ref[:HALF], cs_ref[HALF:]
    first, second = turned[:HALF], turned[HALF:ROT]
    turned = jnp.concatenate(
        [first * cosine - second * sine, second * cosine + first * sine, turned[ROT:]], axis=0
    )
    kv_ref[...] = turned.T.astype(BF)


def query_kernel(rels, n1_ref, dy_ref, vec_ref, cs_ref, *refs):
    count = len(rels)
    packs = refs[:count]
    qt_ref, dot_ref, wq_ref, wo_ref = refs[count:]
    me = lax.axis_index("fsdp")
    part = packs[0].shape[0] // 2
    for rel, pack in zip(rels, packs):
        start = pl.multiple_of((rel ^ me) * part, part)
        wq_ref[pl.ds(start, part), :] = pack[:part]
        wo_ref[pl.ds(start, part), :] = pack[part:]
    turned = (dot(n1_ref[...], wq_ref[...]) + vec_ref[4:5]).T
    cosine, sine = cs_ref[:HALF], cs_ref[HALF:]
    for h in range(HEADS):
        base = h * HDIM
        first, second = turned[base : base + HALF], turned[base + HALF : base + ROT]
        head = jnp.concatenate(
            [
                first * cosine - second * sine,
                second * cosine + first * sine,
                turned[base + ROT : base + HDIM],
            ],
            axis=0,
        )
        qt_ref[base : base + HDIM, :] = (head.astype(BF).astype(F32) * SCALE).astype(BF)
    dot_ref[...] = dot(dy_ref[...], wo_ref[...], NT).T.astype(BF)


def mlp_kernel(seq_orders, last, *refs):
    both, refs = refs[:2], refs[2:]
    if last:
        up_ref, down_ref, ub_ref, vec_ref, early_up, early_dn, early_sums = refs[:7]
        keep_ref, send_ref, n1c_ref, upk_ref, ups_ref, dnk_ref, dns_ref, sums_ref = refs[7:15]
        normal_s, n2_s, dy_s, acc_up, acc_dn = refs[15:]
    else:
        up_ref, down_ref, ub_ref, vec_ref, wq_ref, wo_ref = refs[:6]
        keep_ref, send_ref, n1c_ref, acc_up, acc_dn, sums_ref, pack_ref = refs[6:13]
        normal_s, n2_s, dy_s = refs[13:]
        half = pack_ref.shape[0] // 2
        pack_ref[:half] = wq_ref[...]
        pack_ref[half:] = wo_ref[...]
    me = lax.axis_index("fsdp")
    seq_me = lax.axis_index("seq")
    hidden, width = up_ref.shape
    part = n1c_ref.shape[2]
    rows = n1c_ref.shape[1]
    for i in range(2):
        here = slice(i * rows, (i + 1) * rows)
        x, dy = both[i][:rows], both[i][rows:]
        dy_s[here] = dy
        normal, _ = normalize(x.astype(F32))
        normal_s[here] = normal
        n1 = normal * vec_ref[0:1] + vec_ref[1:2]
        n1c_ref[i] = pick(
            [n1[:, p * part : (p + 1) * part] for p in range(width // part)], me
        ).astype(BF)
        n2_s[here] = (normal * vec_ref[2:3] + vec_ref[3:4]).astype(BF)
    n2, dy = n2_s[...], dy_s[...]
    out = None
    dn2 = None
    tile = 256
    bias = ub_ref[...].astype(F32).reshape(1, hidden)
    sums = []
    for c in range(hidden // tile):
        here = slice(c * tile, (c + 1) * tile)
        up_c, down_c = up_ref[here, :], down_ref[here, :]
        u = dot(n2, up_c, NT) + bias[:, here]
        dg = dot(dy, down_c, NT)
        phi = 0.5 * (1.0 + lax.erf(u * SQRT_HALF))
        g = (u * phi).astype(BF)
        du = (dg * (phi + u * jnp.exp(-0.5 * u * u) * GAUSS_FACTOR)).astype(BF)
        out_c = dot(g, down_c)
        dn2_c = dot(du, up_c)
        out = out_c if out is None else out + out_c
        dn2 = dn2_c if dn2 is None else dn2 + dn2_c
        grad_down, grad_up = dot(g, dy, TN), dot(du, n2, TN)
        if last:
            grad_down, grad_up = grad_down + early_dn[here, :], grad_up + early_up[here, :]
        acc_dn[here, :] = grad_down
        acc_up[here, :] = grad_up
        sums.append(jnp.sum(du.astype(F32), axis=0, keepdims=True))
    lines = [
        jnp.sum(dn2 * normal_s[...], axis=0, keepdims=True),
        jnp.sum(dn2, axis=0, keepdims=True),
        jnp.concatenate(sums, axis=1),
    ]
    for i, line in enumerate(lines):
        size = line.shape[1]
        if last:
            line = line + early_sums[i : i + 1, :size]
        sums_ref[i : i + 1, :size] = line
    for i, target in enumerate((keep_ref, send_ref)):
        here = slice(i * rows, (i + 1) * rows)
        target[0] = out[here].astype(BF)
        target[1] = (dn2[here] * vec_ref[2:3]).astype(BF)
    if last:
        spread_shards(acc_up, seq_orders[0], seq_me, upk_ref, ups_ref)
        spread_shards(acc_dn, seq_orders[1], seq_me, dnk_ref, dns_ref)


def attend_kernel(
    per_group,
    chunk_blocks,
    most,
    order_ref,
    len_ref,
    qt_ref,
    dot_ref,
    kv_near,
    kv_far,
    cs_ref,
    o_ref,
    far_ref,
    near_ref,
    dkvn_ref,
    dkvf_ref,
    s_scr,
    p_scr,
    pb_scr,
    ds_scr,
    bias_scr,
    kv_scr,
    dkv_scr,
    qs,
    dos,
    ot,
    dqt,
    inverse,
):
    side, group = pl.program_id(0), pl.program_id(1)
    seq_me = lax.axis_index("seq")
    half = kv_near.shape[0]
    slots = 2 * half // BLOCK
    chunk = chunk_blocks * BLOCK
    lanes = per_group * BLOCK
    first_step = jnp.logical_and(side == 0, group == 0)
    last_step = jnp.logical_and(
        side == pl.num_programs(0) - 1, group == pl.num_programs(1) - 1
    )

    @pl.when(first_step)
    def _():
        dkv_scr[...] = jnp.zeros_like(dkv_scr)

        @pl.loop(0, slots)
        def _(i):
            rel = (i // 2) ^ seq_me
            place = jnp.int32(0)
            for bit in bits_of(slots // 2):
                place = place * 2 + (rel // bit) % 2
            inverse[order_ref[i]] = place * 2 + i % 2

    block = order_ref[2 * seq_me + side]
    base = block * BLOCK
    end_1 = len_ref[0, 0]
    end_2 = end_1 + len_ref[0, 1]
    end_3 = end_2 + len_ref[0, 2]

    def start_of(position):
        low = jnp.where(position >= end_1, end_1, 0)
        low = jnp.where(position >= end_2, end_2, low)
        return jnp.where(position >= end_3, end_3, low)

    q_pos = base + lax.broadcasted_iota(jnp.int32, (1, BLOCK), 1)
    q_start = start_of(q_pos)
    low_block = jnp.maximum(start_of(base) // BLOCK, block - (most - 1))
    chunks = (block - low_block + chunk_blocks) // chunk_blocks

    def slot_of(j):
        return inverse[jnp.minimum(low_block + j, block)]

    @pl.loop(0, chunks * chunk_blocks)
    def _(j):
        start = slot_of(j) * BLOCK
        here = pl.ds(pl.multiple_of(j * BLOCK, BLOCK), BLOCK)

        @pl.when(start < half)
        def _():
            kv_scr[here, :] = kv_near[pl.ds(pl.multiple_of(start, BLOCK), BLOCK), :]

        @pl.when(start >= half)
        def _():
            kv_scr[here, :] = kv_far[pl.ds(pl.multiple_of(start - half, BLOCK), BLOCK), :]

    for h in range(per_group):
        cols = slice(h * BLOCK, (h + 1) * BLOCK)
        qs[:, cols] = qt_ref[h * HDIM : (h + 1) * HDIM, :]
        dos[:, cols] = dot_ref[h * HDIM : (h + 1) * HDIM, :]

    def score_step(c, top):
        kv = kv_scr[pl.ds(c * chunk, chunk), :]
        s_scr[c] = dot(kv[:, :HDIM], qs[...])
        p_scr[c] = dot(kv[:, HDIM:], dos[...])
        k_pos = (low_block + c * chunk_blocks) * BLOCK + lax.broadcasted_iota(
            jnp.int32, (chunk, BLOCK), 0
        )
        allowed = jnp.logical_and(k_pos <= q_pos, k_pos >= q_start)
        bias_scr[...] = jnp.where(allowed, 0.0, NEGATIVE)
        tops = []
        for h in range(per_group):
            cols = slice(h * BLOCK, (h + 1) * BLOCK)
            s = s_scr[c, :, cols] + bias_scr[...]
            s_scr[c, :, cols] = s
            tops.append(jnp.max(s, axis=0, keepdims=True))
        return jnp.maximum(top, jnp.concatenate(tops, axis=1))

    top = lax.fori_loop(0, chunks, score_step, jnp.full((1, lanes), NEGATIVE, F32))

    def weight_step(c, carry):
        total, delta = carry
        totals, deltas = [], []
        for h in range(per_group):
            cols = slice(h * BLOCK, (h + 1) * BLOCK)
            e = jnp.exp(s_scr[c, :, cols] - top[:, cols])
            s_scr[c, :, cols] = e
            totals.append(jnp.sum(e, axis=0, keepdims=True))
            deltas.append(jnp.sum(e * p_scr[c, :, cols], axis=0, keepdims=True))
        return (
            total + jnp.concatenate(totals, axis=1),
            delta + jnp.concatenate(deltas, axis=1),
        )

    zero = jnp.zeros((1, lanes), F32)
    total, delta = lax.fori_loop(0, chunks, weight_step, (zero, zero))
    shrink = 1.0 / total
    delta = delta * shrink
    ot[...] = jnp.zeros_like(ot)
    dqt[...] = jnp.zeros_like(dqt)

    def grad_step(c, _):
        for h in range(per_group):
            cols = slice(h * BLOCK, (h + 1) * BLOCK)
            p = s_scr[c, :, cols] * shrink[:, cols]
            pb_scr[:, cols] = p.astype(BF)
            ds_scr[:, cols] = (p * (p_scr[c, :, cols] - delta[:, cols])).astype(BF)
        kv = kv_scr[pl.ds(c * chunk, chunk), :]
        ot[...] += dot(kv[:, HDIM:], pb_scr[...], TN)
        dqt[...] += dot(kv[:, :HDIM], ds_scr[...], TN)
        dk = dot(ds_scr[...], qs[...], NT)
        dv = dot(pb_scr[...], dos[...], NT)
        both = jnp.concatenate([dk, dv], axis=1)
        for b in range(chunk_blocks):

            @pl.when(low_block + c * chunk_blocks + b <= block)
            def _():
                place = slot_of(c * chunk_blocks + b) * BLOCK
                dkv_scr[pl.ds(pl.multiple_of(place, BLOCK), BLOCK), :] += both[
                    b * BLOCK : (b + 1) * BLOCK
                ]

        return 0

    lax.fori_loop(0, chunks, grad_step, 0)
    cosine, sine = cs_ref[:HALF], cs_ref[HALF:]
    outs, grads = [], []
    for h in range(per_group):
        cols = slice(h * BLOCK, (h + 1) * BLOCK)
        outs.append(ot[:, cols])
        grad = dqt[:, cols] * SCALE
        first, second = grad[:HALF], grad[HALF:ROT]
        grads.append(first * cosine + second * sine)
        grads.append(second * cosine - first * sine)
        grads.append(grad[ROT:])
    width = o_ref.shape[1]
    here = pl.ds(pl.multiple_of(side * BLOCK, BLOCK), BLOCK)
    span = per_group * HDIM
    across = pl.ds(0 if span == width else pl.multiple_of(group * span, span), span)
    o_ref[here, across] = jnp.concatenate(outs, axis=0).T.astype(BF)
    grad = jnp.concatenate(grads, axis=0).T.astype(BF)
    far_ref[here, across] = grad
    near_ref[here, across] = grad

    @pl.when(group == pl.num_programs(1) - 1)
    def _():
        me = lax.axis_index("fsdp")
        part = near_ref.shape[1] - width
        count = width // part
        o = o_ref[here, :].astype(F32)
        pieces = [o[:, p * part : (p + 1) * part] for p in range(count)]
        near_ref[here, width:] = pick(pieces, me ^ 1).astype(BF)
        far_ref[here, width:] = jnp.concatenate(
            [pick(pieces, me ^ 2), pick(pieces, me ^ 3)], axis=1
        ).astype(BF)

    @pl.when(last_step)
    def _():
        dkvn_ref[...] = dkv_scr[:half].astype(dkvn_ref.dtype)
        dkvf_ref[...] = dkv_scr[half:].astype(dkvf_ref.dtype)


def output_kernel(x_ref, o_ref, wo_ref, vec_ref, a_ref, b_ref, c_ref, layer_ref):
    mlp = a_ref[0].astype(F32) + b_ref[0].astype(F32) + c_ref[0].astype(F32)
    attention = dot(o_ref[...], wo_ref[...]) + vec_ref[5:6]
    layer_ref[...] = (x_ref[...].astype(F32) + attention + mlp + vec_ref[6:7]).astype(BF)


def spread_shards(source, order, seq_me, near, far):
    shards = len(order)
    rows = source.shape[0] // shards
    half = shards // 2
    for m in range(shards):
        start = pl.multiple_of(((order[m] ^ seq_me) & (shards - 1)) * rows, rows)
        target = near if m < half else far
        target[(m % half) * rows : (m % half + 1) * rows, :] = source[pl.ds(start, rows), :].astype(
            BF
        )


def weight_kernel(order, n1a_ref, n1b_ref, o_ref, own_ref, z1_ref, z2_ref, z3_ref, *refs):
    me = lax.axis_index("fsdp")
    rows, part = n1a_ref.shape[1:]
    dys = [ref.at[rows:] for ref in refs[:4]]
    near_ref, far_ref, grad = refs[4:]
    width = dys[0].shape[1]
    o = o_ref[...].astype(F32)
    own = pick([o[:, p * part : (p + 1) * part] for p in range(width // part)], me).astype(BF)
    items = (
        (n1a_ref[0], own_ref[:, :width], own, dys[0][...]),
        (n1a_ref[1], z1_ref[:, :width], z1_ref[:, width:], dys[1][...]),
        (n1b_ref[0], z2_ref[:, :width], z2_ref[:, width : width + part], dys[2][...]),
        (n1b_ref[1], z3_ref[:, :width], z3_ref[:, width + part :], dys[3][...]),
    )
    grad_q = None
    grad_o = None
    for n1, dq, cols, dy in items:
        term_q, term_o = dot(n1, dq, TN), dot(cols, dy, TN)
        grad_q = term_q if grad_q is None else grad_q + term_q
        grad_o = term_o if grad_o is None else grad_o + term_o
    grad[:part] = grad_q
    grad[part:] = grad_o
    spread_shards(grad, order, lax.axis_index("seq"), near_ref, far_ref)


def tail_kernel(
    rels,
    x_ref,
    dy_ref,
    n1_ref,
    dq_ref,
    wq_ref,
    wkv_ref,
    vec_ref,
    cs_ref,
    a_ref,
    b_ref,
    c_ref,
    dkvn_ref,
    dkvf_ref,
    sums_ref,
    grad_ref,
    keep_ref,
    send_ref,
    vs,
):
    count = len(rels)
    me = lax.axis_index("fsdp")
    width = x_ref.shape[1]
    part = width // count
    dkv = (dkvn_ref[...].astype(F32) + dkvf_ref[...].astype(F32)).T
    cosine, sine = cs_ref[:HALF], cs_ref[HALF:]
    first, second = dkv[:HALF], dkv[HALF:ROT]
    dkv = jnp.concatenate(
        [first * cosine + second * sine, second * cosine - first * sine, dkv[ROT:]], axis=0
    )
    dkv_sum = jnp.sum(dkv.astype(BF).T.astype(F32), axis=0, keepdims=True)
    dkv_t = dkv.astype(BF)
    dq = dq_ref[:, :width]
    dn1 = dot(dq, wq_ref[...], NT) + dot(dkv_t, wkv_ref[...], TN)
    normal, inverse_std = normalize(x_ref[...].astype(F32))
    dy = dy_ref[...].astype(F32)
    total = a_ref[1].astype(F32) + b_ref[1].astype(F32) + c_ref[1].astype(F32)
    total = total + dn1 * vec_ref[0:1]
    grad_ref[...] = (
        dy
        + inverse_std
        * (
            total
            - jnp.mean(total, -1, keepdims=True)
            - normal * jnp.mean(total * normal, -1, keepdims=True)
        )
    ).astype(BF)
    grad_kv = dot(dkv_t, n1_ref[...])
    lines = jnp.concatenate(
        [
            jnp.sum(dn1 * normal, axis=0, keepdims=True),
            jnp.sum(dn1, axis=0, keepdims=True),
            sums_ref[0:1, :width],
            sums_ref[1:2, :width],
            jnp.sum(dq.astype(F32), axis=0, keepdims=True),
            jnp.sum(dy, axis=0, keepdims=True),
            jnp.concatenate(
                [jnp.concatenate([dkv_sum, jnp.zeros((1, part - 2 * HDIM), F32)], axis=1)] * count,
                axis=1,
            ),
            jnp.zeros((1, width), F32),
        ],
        axis=0,
    )
    for p in range(count):
        cols = slice(p * part, (p + 1) * part)
        vs[p, : 2 * HDIM, :] = grad_kv[:, cols]
        vs[p, 2 * HDIM :, :] = lines[:, cols]
    half = count // 2
    extra = sums_ref.shape[1] // part
    up_bias = jnp.concatenate(
        [sums_ref[2:3, e * part : (e + 1) * part] for e in range(extra)]
        + [jnp.zeros((8 - extra, part), F32)],
        axis=0,
    )
    for m, rel in enumerate(rels):
        target = keep_ref if m < half else send_ref
        piece = vs[rel ^ me]
        last = up_bias if rel == 0 else jnp.zeros_like(up_bias)
        store_split(
            target, m % half, piece[: 2 * HDIM], jnp.concatenate([piece[2 * HDIM :], last], axis=0)
        )


def store_split(target, index, matrix, lines):
    top = matrix.shape[0]
    high = lines.astype(BF)
    target[index, :top] = matrix.astype(BF)
    target[index, top : top + 16] = high
    target[index, top + 16 : top + 32] = (lines - high.astype(F32)).astype(BF)


def load_split(value):
    top = 2 * HDIM
    value = value.astype(F32)
    return (value[:top], value[top : top + 16] + value[top + 16 : top + 32])


def mix_step(sources, targets):
    a_ref, b_ref = sources
    each = a_ref.shape[0] // len(targets)
    for i, target in enumerate(targets):
        for j in range(each):
            first, second = load_split(a_ref[i * each + j]), load_split(b_ref[i * each + j])
            store_split(target, j, first[0] + second[0], first[1] + second[1])


def merge_step(sources, targets):
    a_ref, b_ref = sources
    rows = a_ref.shape[0] // len(targets)
    for i, target in enumerate(targets):
        here = slice(i * rows, (i + 1) * rows)
        target[...] = (a_ref[here].astype(F32) + b_ref[here].astype(F32)).astype(BF)


def join_step(sources, targets):
    rows = 0
    for source in sources:
        targets[0][rows : rows + source.shape[0]] = source[...]
        rows += source.shape[0]


def matrix_kernel(order, near_ref, far_ref, *refs):
    outs, (held, sems) = refs[:-2], refs[-2:]
    seq_me = lax.axis_index("seq")
    shards = len(order)
    half = shards // 2
    rows = near_ref.shape[0] // half
    each = shards // len(outs)
    copies = []
    for t in range(shards):
        wanted = (t ^ seq_me) & (shards - 1)
        place = jnp.int32(0)
        for m, rel in enumerate(order):
            place = jnp.where(wanted == rel, m, place)
        start = pl.multiple_of((place & (half - 1)) * rows, rows)

        @pl.when(place < half)
        def _():
            held[t] = near_ref[pl.ds(start, rows), :].astype(F32)

        @pl.when(place >= half)
        def _():
            held[t] = far_ref[pl.ds(start, rows), :].astype(F32)

        first = (t % each) * rows
        copy = pltpu.make_async_copy(
            held.at[t], outs[t // each].at[first : first + rows, :], sems.at[t]
        )
        copy.start()
        copies.append(copy)
    for copy in copies:
        copy.wait()


def vector_kernel(a_ref, b_ref, g1, b1, qb, kb, vb, ob, g2, b2, ub, db, wk_ref, wv_ref):
    me = lax.axis_index("fsdp")
    first, second = load_split(a_ref[0]), load_split(b_ref[0])
    total, lines = first[0] + second[0], first[1] + second[1]
    part = total.shape[1]
    wk_ref[...] = total[:HDIM]
    wv_ref[...] = total[HDIM:]
    for i, targets in enumerate(((g1,), (b1,), (g2,), (b2,), (qb,), (ob, db))):
        for target in targets:
            target[...] = lines[i : i + 1].reshape(part)
    kp, vp = kb.shape[0], vb.shape[0]
    line = lines[6:7]
    count = HDIM // vp
    kb[...] = pick([line[:, p * kp : (p + 1) * kp] for p in range(count)], me).reshape(kp)
    vb[...] = pick(
        [line[:, HDIM + p * vp : HDIM + (p + 1) * vp] for p in range(count)], me
    ).reshape(vp)
    extra = ub.shape[0] // part
    ub[...] = jnp.concatenate([lines[8 + e : 9 + e] for e in range(extra)], axis=1).reshape(
        ub.shape[0]
    )


def shard_count(rows, devices):
    shards = devices
    while shards > 2 and (rows % shards or (rows // shards) % 16):
        shards //= 2
    return shards


def shard_order(bits):
    order = [0]
    for bit in reversed(bits):
        order = order + [r ^ bit for r in order]
    return order


def on_device(
    tokens,
    block_order,
    doc_lengths,
    norm_one_gain,
    norm_one_bias,
    query_weight,
    query_bias,
    key_weight,
    key_bias,
    value_weight,
    value_bias,
    out_weight,
    out_bias,
    norm_two_gain,
    norm_two_bias,
    up_weight,
    up_bias,
    down_weight,
    down_bias,
    cotangent,
):
    _, rows, width = tokens.shape
    hidden = up_weight.shape[0]
    part = query_weight.shape[0]
    fsdp = lax.axis_size("fsdp")
    seqs = lax.axis_size("seq")
    slots = 2 * seqs
    fbits = bits_of(fsdp)
    sbits = bits_of(seqs)
    rels = rel_order(fsdp)
    fsdp_me = lax.axis_index("fsdp")
    seq_me = lax.axis_index("seq")
    x_own = tokens.reshape(rows, width)
    dy_own = cotangent.reshape(rows, width)

    def spread(value):
        parts = [value]
        for bit in reversed(fbits):
            parts = parts + [swap(v, "fsdp", bit) for v in parts]
        return parts

    pieces = (
        x_own,
        dy_own,
        norm_one_gain,
        norm_one_bias,
        norm_two_gain,
        norm_two_bias,
        query_bias,
        out_bias,
        down_bias,
        key_bias,
        value_bias,
        key_weight.T,
        value_weight.T,
    )
    sequence = Sequence()
    run = sequence.run
    pack, both_0 = run(
        pack_kernel,
        (shape((2 * HDIM + 16, part), BF), shape((2 * rows, width), BF)),
        pieces,
        [pltpu.VMEM(v.shape, BF) for v in pieces[2:]] + [pltpu.SemaphoreType.DMA((len(pieces),))],
        limit=60,
        name="pack",
        time=2,
        in_specs=[HBM] * len(pieces),
    )
    packs = spread(pack)
    both_2 = swap(both_0, "fsdp", 2)
    both_1 = swap(both_0, "fsdp", 1)

    own_blocks = lax.dynamic_slice_in_dim(block_order, 2 * seq_me, 2)
    offsets = jnp.arange(BLOCK, dtype=jnp.int32)
    own_pos = (own_blocks[:, None] * BLOCK + offsets[None, :]).reshape(rows)
    frequencies = 10000.0 ** (-2.0 * jnp.arange(HALF, dtype=F32) / ROT)
    angles = own_pos.astype(F32)[None, :] * frequencies[:, None]
    cs = jnp.concatenate([jnp.cos(angles), jnp.sin(angles)], axis=0)

    n1, kv_own, vec, wkv = run(
        functools.partial(front_kernel, rels),
        (
            shape((rows, width), BF),
            shape((rows, 2 * HDIM), BF),
            shape((16, width), F32),
            shape((2 * HDIM, width), BF),
        ),
        (x_own, *packs, cs),
        [pltpu.VMEM((fsdp, 16, part), F32), pltpu.VMEM((fsdp, 2 * HDIM, part), BF)],
        name="front",
    )

    kv = kv_own
    for bit in reversed(sbits[3:]):
        ((kv,),) = sequence.stage((join_step, [kv, swap(kv, "seq", bit)], 1))
    kv_parts = [kv] + [swap(kv, "seq", bit) for bit in (sbits[2], sbits[1], sbits[1] + sbits[2])]

    shards = shard_count(hidden, seqs)
    low_bits = [b for b in sbits if b < shards]
    rest_bits = [b for b in sbits if b >= shards]
    up_bits = low_bits
    dn_bits = low_bits[1:] + low_bits[:1]
    seq_orders = (shard_order(up_bits), shard_order(dn_bits))
    chunk_out = shape((2, rows, width), BF)
    n1c_out = shape((2, rows, part), BF)
    sums_out = shape((8, max(hidden, width)), F32)
    mlp_scratch = [
        pltpu.VMEM((2 * rows, width), F32),
        pltpu.VMEM((2 * rows, width), BF),
        pltpu.VMEM((2 * rows, width), BF),
    ]
    keep_a, send_a, n1a, early_up, early_dn, early_sums, pack_qo = run(
        functools.partial(mlp_kernel, None, False),
        (
            chunk_out,
            chunk_out,
            n1c_out,
            shape((hidden, width), F32),
            shape((hidden, width), F32),
            sums_out,
            shape((2 * part, width), BF),
        ),
        (both_0, both_1, up_weight, down_weight, up_bias, vec, query_weight, out_weight),
        mlp_scratch,
        limit=24,
        name="mlp_near",
        time=7,
    )
    (kv_near,), (relay,) = sequence.stage((join_step, kv_parts, 1), (join_step, [both_2], 1))
    both_3 = swap(relay, "fsdp", 1)
    qo_1 = swap(pack_qo, "fsdp", 1)
    back_a = swap(send_a, "fsdp", 1)
    kv_far = swap(kv_near, "seq", sbits[0])
    qo_2 = swap(pack_qo, "fsdp", 2)
    keep_b, send_b, n1b, upk, ups, dnk, dns, sums = run(
        functools.partial(mlp_kernel, seq_orders, True),
        (chunk_out, chunk_out, n1c_out)
        + (shape((hidden // 2, width), BF),) * 4
        + (sums_out,),
        (both_2, both_3, up_weight, down_weight, up_bias, vec, early_up, early_dn, early_sums),
        mlp_scratch + [pltpu.VMEM((hidden, width), F32)] * 2,
        limit=28,
        name="mlp_far",
        time=8,
        after=(qo_1, back_a, kv_far),
    )
    up = Sum(upk, ups, up_bits, rest_bits)
    dn = Sum(dnk, dns, dn_bits, rest_bits)
    ((relay_qo,),) = sequence.stage((join_step, [qo_2], 1))
    qo_3 = swap(relay_qo, "fsdp", 1)
    back_b = swap(send_b, "fsdp", 1)
    qt, do_t, wq, wo = run(
        functools.partial(query_kernel, rels),
        (
            shape((width, rows), BF),
            shape((width, rows), BF),
            shape((width, width), BF),
            shape((width, width), BF),
        ),
        (n1, dy_own, vec, cs, pack_qo, qo_2, qo_1, qo_3),
        name="query",
    )
    ((back,),) = sequence.stage((merge_step, [keep_b, back_b], 1))
    back = swap(back, "fsdp", 2)
    mlp_parts = (keep_a, back_a, back)

    most = min(slots, slots // 2 + 1)
    chunk_blocks = 2
    most_chunks = -(-most // chunk_blocks)
    chunk = chunk_blocks * BLOCK
    per_group = HEADS
    while most_chunks * chunk * per_group * BLOCK * 8 > 20 * MIB and per_group > 2:
        per_group = {12: 6, 6: 4, 4: 2}[per_group]
    lanes = per_group * BLOCK
    span = per_group * HDIM
    own, z_far, z_near, dkv_near, dkv_far = run(
        functools.partial(attend_kernel, per_group, chunk_blocks, most),
        (
            shape((rows, width), BF),
            shape((rows, width + 2 * part), BF),
            shape((rows, width + part), BF),
            shape((seqs * BLOCK, 2 * HDIM), BF),
            shape((seqs * BLOCK, 2 * HDIM), BF),
        ),
        (block_order, doc_lengths, qt, do_t, kv_near, kv_far, cs),
        [
            pltpu.VMEM((most_chunks, chunk, lanes), F32),
            pltpu.VMEM((most_chunks, chunk, lanes), F32),
            pltpu.VMEM((chunk, lanes), BF),
            pltpu.VMEM((chunk, lanes), BF),
            pltpu.VMEM((chunk, BLOCK), F32),
            pltpu.VMEM((most_chunks * chunk, 2 * HDIM), BF),
            pltpu.VMEM((slots * BLOCK, 2 * HDIM), F32),
            pltpu.VMEM((HDIM, lanes), BF),
            pltpu.VMEM((HDIM, lanes), BF),
            pltpu.VMEM((HDIM, lanes), F32),
            pltpu.VMEM((HDIM, lanes), F32),
            pltpu.SMEM((slots,), jnp.int32),
        ],
        limit=40,
        name="attend",
        time=13,
        grid=(2, HEADS // per_group),
        in_specs=[
            SMEM,
            SMEM,
            pl.BlockSpec((span, BLOCK), lambda i, g: (g, i)),
            pl.BlockSpec((span, BLOCK), lambda i, g: (g, i)),
            VMEM,
            VMEM,
            pl.BlockSpec((ROT, BLOCK), lambda i, g: (0, i)),
        ],
    )

    dkv = Reduce(dkv_near, dkv_far, sbits)
    z2 = swap(z_far, "fsdp", 2)
    advance(sequence, up, dn)
    layer_out = run(
        output_kernel,
        shape((rows, width), BF),
        (x_own, own, wo, vec, *mlp_parts),
        name="output",
    )
    while dkv.left() > 1:
        advance(sequence, dkv)
    z1 = swap(z_near, "fsdp", 1)
    (relay_z,) = advance(sequence, dkv, up, dn, extra=[(join_step, [z2], 1)])
    z3 = swap(relay_z, "fsdp", 1)

    qo_shards = shard_count(2 * part, seqs)
    qo_bits = [b for b in sbits if b < qo_shards]
    qo_rest = [b for b in sbits if b >= qo_shards]
    qo_order = shard_order(qo_bits)
    qok, qos = run(
        functools.partial(weight_kernel, qo_order),
        (shape((part, width), BF), shape((part, width), BF)),
        (n1a, n1b, own, z_near, z1, z2, z3, both_0, both_1, both_2, both_3),
        [pltpu.VMEM((2 * part, width), F32)],
        name="weight",
    )
    qo = Sum(qok, qos, qo_bits, qo_rest)
    height = 2 * HDIM + 32
    half = fsdp // 2
    mixed = shape((half, height, part), BF)
    grad_tokens, near_t, far_t = run(
        functools.partial(tail_kernel, rels),
        (shape((rows, width), BF), mixed, mixed),
        (x_own, dy_own, n1, z_near, wq, wkv, vec, cs, *mlp_parts, *dkv.pair(), sums),
        [pltpu.VMEM((fsdp, 2 * HDIM + 8, part), F32)],
        name="tail",
        time=2,
    )
    mix = Mix(near_t, far_t, fbits, sbits)
    advance(sequence, up, dn, mix, qo)
    advance(sequence, up, dn, mix, qo)
    advance(sequence, mix, qo)
    advance(sequence, up, dn, mix, qo)
    while up.left() + dn.left() + mix.left() + qo.left():
        advance(sequence, *[item for item in (mix, qo, up, dn) if item.left()])

    def matrix(pair, order, count):
        each = 2 * pair[0].shape[0] // len(order)
        return run(
            functools.partial(matrix_kernel, order),
            (shape((2 * pair[0].shape[0] // count, width), F32),) * count,
            pair,
            [
                pltpu.VMEM((len(order), each, width), F32),
                pltpu.SemaphoreType.DMA((len(order),)),
            ],
            limit=16,
            name="matrix",
            out_specs=(ANY,) * count,
        )

    vector = shape((part,), F32)
    g1, b1, qb, kb, vb, ob, g2, b2, ub, db, wk, wv = run(
        vector_kernel,
        (
            vector,
            vector,
            vector,
            shape(key_bias.shape, F32),
            shape(value_bias.shape, F32),
            vector,
            vector,
            vector,
            shape((hidden,), F32),
            vector,
            shape((HDIM, part), F32),
            shape((HDIM, part), F32),
        ),
        mix.pair(),
        limit=16,
        name="vector",
    )
    grad_query, grad_out = matrix(qo.pair(), qo_order, 2)
    (grad_up,) = matrix(up.pair(), seq_orders[0], 1)
    (grad_down,) = matrix(dn.pair(), seq_orders[1], 1)
    return (
        layer_out.reshape(1, rows, width),
        grad_tokens.reshape(1, rows, width),
        g1,
        b1,
        grad_query,
        qb,
        wk.T,
        kb,
        wv.T,
        vb,
        grad_out,
        ob,
        g2,
        b2,
        grad_up,
        ub,
        grad_down,
        db,
    )


def solution(mesh):
    split = P("fsdp")
    matrix = P("fsdp", None)
    stream = P("fsdp", "seq", None)
    return jax.shard_map(
        on_device,
        mesh=mesh,
        in_specs=(
            stream,
            P(),
            matrix,
            split,
            split,
            matrix,
            split,
            matrix,
            split,
            matrix,
            split,
            matrix,
            split,
            split,
            split,
            matrix,
            split,
            matrix,
            split,
            stream,
        ),
        out_specs=(
            stream,
            stream,
            split,
            split,
            matrix,
            split,
            matrix,
            split,
            matrix,
            split,
            matrix,
            split,
            split,
            split,
            matrix,
            split,
            matrix,
            split,
        ),
        check_vma=False,
    )
```

```python
import functools

import jax
import jax.numpy as jnp
from jax import lax
from jax.experimental import pallas as pl
from jax.experimental.pallas import tpu as pltpu
from jax.sharding import PartitionSpec as P

HEADS = 12
HDIM = 64
ROT = 16
HALF = ROT // 2
BLOCK = 128

NEGATIVE = -1e30
EPSILON = 1e-05
SQRT_HALF = 0.7071067811865476
GAUSS_FACTOR = 0.3989422804014327
SCALE = HDIM ** (-0.5)
BF = jnp.bfloat16
F32 = jnp.float32
MIB = 1024 * 1024
VMEM = pl.BlockSpec(memory_space=pltpu.VMEM)
SMEM = pl.BlockSpec(memory_space=pltpu.SMEM)
ANY = pl.BlockSpec(memory_space=pl.ANY)
HBM = pl.BlockSpec(memory_space=pltpu.HBM)

NN = (((1,), (0,)), ((), ()))
NT = (((1,), (1,)), ((), ()))
TN = (((0,), (0,)), ((), ()))


def dot(left, right, dims=NN):
    return lax.dot_general(left, right, dims, preferred_element_type=F32)


def shape(dims, dtype):
    return jax.ShapeDtypeStruct(dims, dtype)


def params(limit=48):
    return pltpu.CompilerParams(vmem_limit_bytes=limit * MIB)


def micros(time):
    return pl.CostEstimate(flops=max(1, time * 1000000000), bytes_accessed=1000, transcendentals=0)


class Sequence:
    def __init__(self):
        self.last = ()

    def run(self, kernel, outs, ins, scratch=(), limit=16, name=None, after=(), time=0, token=True, **specs):
        single = isinstance(outs, jax.ShapeDtypeStruct)
        self.last = self.last + tuple(after)
        count, extra = len(ins), len(self.last)

        def body(*refs):
            kernel(*refs[:count], *refs[count + extra :])

        results = pl.pallas_call(
            body,
            out_shape=outs,
            in_specs=list(specs.get("in_specs", [VMEM] * count)) + [ANY] * extra,
            out_specs=specs.get("out_specs", VMEM if single else (VMEM,) * len(outs)),
            grid=specs.get("grid", ()),
            scratch_shapes=list(scratch),
            compiler_params=params(limit),
            cost_estimate=micros(time),
            name=name,
        )(*ins, *self.last)
        if token:
            self.last = (min((results,) if single else results, key=lambda v: v.size),)
        return results

    def stage(self, tasks, bundles=(), after=()):
        bundles = [list(bundle) for bundle in bundles]
        placed = {key for bundle in bundles for key in bundle}
        for t, (_, _, parts) in enumerate(tasks):
            bundles += [[(t, p)] for p in range(parts) if (t, p) not in placed]
        sizes = {}
        for t, (kind, views, parts) in enumerate(tasks):
            rows = sum(v.rows for v in views) if kind is join_step else views[0].rows
            for p in range(parts):
                sizes[t, p] = rows // parts
        ins, outs, spots = [], [], {}
        for index, bundle in enumerate(bundles):
            start = 0
            for key in bundle:
                spots[key] = (index, start, sizes[key])
                start += sizes[key]
            like = tasks[bundle[0][0]][1][0].array
            outs.append(shape((start,) + like.shape[1:], BF))
        plan = []
        for t, (kind, views, parts) in enumerate(tasks):
            sources = []
            for view in views:
                at = next((i for i, v in enumerate(ins) if v is view.array), len(ins))
                if at == len(ins):
                    ins.append(view.array)
                sources.append((at, view.start, view.rows))
            plan.append((kind, sources, [spots[t, p] for p in range(parts)]))

        def kernel(*refs):
            def pieces(found, offset):
                return [refs[offset + i].at[start : start + size] for i, start, size in found]

            for kind, sources, targets in plan:
                kind(pieces(sources, 0), pieces(targets, len(ins)))

        results = self.run(kernel, tuple(outs), ins, name="stage", after=after)
        return {key: View(results[i], start, rows) for key, (i, start, rows) in spots.items()}


class View:
    def __init__(self, array, start=0, rows=None):
        self.array, self.start = array, start
        self.rows = array.shape[0] if rows is None else rows


class Sum:
    def __init__(self, near, far, bits, rest, small=False):
        self.small = small
        self.near, self.coming = View(near), View(swap(far, "seq", bits[0]))
        plan = [(bit, 2) for bit in bits[1:]] + [(bit, 1) for bit in rest]
        plan += [(bits[-1], 1)] + [(bit, -1) for bit in reversed(bits[:-1])]
        self.plan = [("seq", bit, parts) for bit, parts in plan]

    def left(self):
        return len(self.plan)

    def task(self):
        parts = self.plan[0][2]
        if parts == -1:
            return (join_step, [self.near, self.coming], 1)
        return (merge_step, [self.near, self.coming], parts)

    def pair(self):
        return (self.near, self.coming)


class Reduce(Sum):
    def __init__(self, near, far, bits):
        Sum.__init__(self, near, far, bits, [])
        self.plan = self.plan[: len(bits) - 1]


class Mix(Sum):
    def __init__(self, near, far, fbits, sbits):
        self.small = True
        self.near, self.coming = View(near), View(swap(far, "fsdp", fbits[0]))
        self.plan = [("fsdp", bit, 2) for bit in fbits[1:]] + [("seq", bit, 1) for bit in sbits]

    def task(self):
        return (mix_step, [self.near, self.coming], self.plan[0][2])


def join_all(sequence, *arrays, after=()):
    task = (join_step, [View(v) for v in arrays], 1)
    return sequence.stage([task], after=after)[0, 0].array


def flow(sequence, *items, extra=(), after=(), together=False):
    tasks = [item.task() for item in items] + list(extra)
    groups = {}
    for t, item in enumerate(items):
        axis, bit, _ = item.plan[0]
        key = (axis, bit, 0 if item.small or together else 1 + t)
        groups.setdefault(key, []).append((t, tasks[t][2] - 1))
    views = sequence.stage(tasks, groups.values(), after)
    for (axis, bit, _), keys in groups.items():
        sent = swap(views[keys[0]].array, axis, bit)
        for t, part in keys:
            view = views[t, part]
            items[t].near = views[t, 0]
            items[t].coming = View(sent, view.start, view.rows)
            items[t].plan.pop(0)
    return [views[len(items) + i, 0].array for i in range(len(extra))]


def swap(value, axis, bit):
    size = lax.axis_size(axis)
    return lax.ppermute(value, axis, [(i, i ^ bit) for i in range(size)])


def bits_of(size):
    return [1 << i for i in range(size.bit_length() - 1)]


def normalize(values):
    center = values - jnp.mean(values, -1, keepdims=True)
    inverse_std = lax.rsqrt(jnp.mean(center * center, -1, keepdims=True) + EPSILON)
    return (center * inverse_std, inverse_std)


def pick(pieces, index):
    result = pieces[-1]
    for i in range(len(pieces) - 2, -1, -1):
        result = jnp.where(index == i, pieces[i], result)
    return result


def rel_order(size):
    order = [0]
    for bit in reversed(bits_of(size)):
        order = order + [r ^ bit for r in order]
    return order


def pack_kernel(*refs):
    count = len(refs) // 2
    pack_ref, both_ref, qo_ref, bulk_ref = refs[count : count + 4]
    sems = refs[-1]
    rows, part = refs[0].shape[0], refs[2].shape[0]
    held = (both_ref.at[:rows], both_ref.at[rows:], qo_ref.at[:part], qo_ref.at[part:])
    held += refs[count + 4 : -1]
    start = 0
    pairs = [(refs[i], held[i]) for i in range(count)]
    for ref in refs[:4]:
        size = ref.shape[0]
        pairs.append((ref, bulk_ref.at[start : start + size]))
        start += size
    copies = [pltpu.make_async_copy(*pair, sems.at[i]) for i, pair in enumerate(pairs)]
    for copy in copies:
        copy.start()
    for copy in copies:
        copy.wait()
    g1, b1, g2, b2, qb, ob, db, kb, vb, wk_ref, wv_ref = held[4:]
    small = jnp.concatenate(
        [
            kb[...].astype(F32).reshape(1, kb.shape[0]),
            vb[...].astype(F32).reshape(1, vb.shape[0]),
            jnp.zeros((1, part - kb.shape[0] - vb.shape[0]), F32),
        ],
        axis=1,
    )
    lines = [ref[...].astype(F32).reshape(1, part) for ref in (g1, b1, g2, b2, qb, ob, db)]
    lines = jnp.concatenate(lines + [small, jnp.zeros((8, part), F32)], axis=0)
    pack_ref[:HDIM] = wk_ref[...]
    pack_ref[HDIM : 2 * HDIM] = wv_ref[...]
    pack_ref[2 * HDIM :] = lines.astype(BF)


def table_kernel(cosine, sine, out):
    out[:HALF] = cosine[...]
    out[HALF:] = sine[...]


def front_kernel(rels, x_ref, *refs):
    count = len(rels)
    packs = refs[:count]
    cs_ref, n1_ref, kv_ref, vec_ref, wkv_ref, pieces, weights = refs[count:]
    me = lax.axis_index("fsdp")
    for rel, pack in zip(rels, packs):
        weights[rel ^ me] = pack[: 2 * HDIM, :]
        pieces[rel ^ me] = pack[2 * HDIM :, :].astype(F32)
    wkv = jnp.concatenate([weights[p] for p in range(count)], axis=1)
    wkv_ref[...] = wkv
    vec = jnp.concatenate([pieces[p] for p in range(count)], axis=1)
    vec_ref[...] = vec
    normal, _ = normalize(x_ref[...].astype(F32))
    n1 = (normal * vec[0:1] + vec[1:2]).astype(BF)
    n1_ref[...] = n1
    key_part, value_part = ROT // count, HDIM // count
    key_bias = jnp.concatenate([pieces[p][7:8, :key_part] for p in range(count)], axis=1)
    value_bias = jnp.concatenate(
        [pieces[p][7:8, key_part : key_part + value_part] for p in range(count)], axis=1
    )
    bias = jnp.concatenate([key_bias, jnp.zeros((1, HDIM - ROT), F32), value_bias], axis=1)
    turned = (dot(n1, wkv, NT) + bias).T
    cosine, sine = cs_ref[:HALF], cs_ref[HALF:]
    first, second = turned[:HALF], turned[HALF:ROT]
    turned = jnp.concatenate(
        [first * cosine - second * sine, second * cosine + first * sine, turned[ROT:]], axis=0
    )
    kv_ref[...] = turned.T.astype(BF)


def query_kernel(rels, n1_ref, both_ref, vec_ref, cs_ref, *refs):
    count = len(rels) - 1
    part = refs[0].shape[0] // 2
    tops = [pack.shape[0] - 2 * part for pack in refs[:count]]
    pairs = [
        (pack.at[top : top + part], pack.at[top + part : top + 2 * part])
        for pack, top in zip(refs[:count], tops)
    ]
    pairs.append(refs[count : count + 2])
    qt_ref, dot_ref, wq_ref, wo_ref = refs[count + 2 :]
    me = lax.axis_index("fsdp")
    for rel, (near, far) in zip(rels, pairs):
        start = pl.multiple_of((rel ^ me) * part, part)
        wq_ref[pl.ds(start, part), :] = near[...]
        wo_ref[pl.ds(start, part), :] = far[...]
    turned = (dot(n1_ref[...], wq_ref[...]) + vec_ref[4:5]).T
    cosine, sine = cs_ref[:HALF], cs_ref[HALF:]
    for h in range(HEADS):
        base = h * HDIM
        first, second = turned[base : base + HALF], turned[base + HALF : base + ROT]
        head = jnp.concatenate(
            [
                first * cosine - second * sine,
                second * cosine + first * sine,
                turned[base + ROT : base + HDIM],
            ],
            axis=0,
        )
        qt_ref[base : base + HDIM, :] = (head.astype(BF).astype(F32) * SCALE).astype(BF)
    dy = both_ref[n1_ref.shape[0] :]
    dot_ref[...] = dot(dy, wo_ref[...], NT).T.astype(BF)


def mlp_kernel(seq_orders, last, *refs):
    both, refs = refs[:2], refs[2:]
    if last:
        up_ref, down_ref, ub_ref, vec_ref, early_up, early_dn, early_sums = refs[:7]
        keep_ref, send_ref, n1c_ref, upk_ref, ups_ref, dnk_ref, dns_ref, sums_ref = refs[7:15]
        normal_s, n2_s, dy_s, acc_up, acc_dn = refs[15:]
    else:
        up_ref, down_ref, ub_ref, vec_ref = refs[:4]
        keep_ref, send_ref, n1c_ref, acc_up, acc_dn, sums_ref = refs[4:10]
        normal_s, n2_s, dy_s = refs[10:]
    me = lax.axis_index("fsdp")
    seq_me = lax.axis_index("seq")
    hidden, width = up_ref.shape
    part = n1c_ref.shape[2]
    rows = n1c_ref.shape[1]
    for i in range(2):
        here = slice(i * rows, (i + 1) * rows)
        x, dy = both[i][:rows], both[i][rows : 2 * rows]
        dy_s[here] = dy
        normal, _ = normalize(x.astype(F32))
        normal_s[here] = normal
        n1 = normal * vec_ref[0:1] + vec_ref[1:2]
        n1c_ref[i] = pick(
            [n1[:, p * part : (p + 1) * part] for p in range(width // part)], me
        ).astype(BF)
        n2_s[here] = (normal * vec_ref[2:3] + vec_ref[3:4]).astype(BF)
    n2, dy = n2_s[...], dy_s[...]
    out = None
    dn2 = None
    tile = 256
    bias = ub_ref[...].astype(F32).reshape(1, hidden)
    sums = []
    for c in range(hidden // tile):
        here = slice(c * tile, (c + 1) * tile)
        up_c, down_c = up_ref[here, :], down_ref[here, :]
        u = dot(n2, up_c, NT) + bias[:, here]
        dg = dot(dy, down_c, NT)
        phi = 0.5 * (1.0 + lax.erf(u * SQRT_HALF))
        g = (u * phi).astype(BF)
        du = (dg * (phi + u * jnp.exp(-0.5 * u * u) * GAUSS_FACTOR)).astype(BF)
        out_c = dot(g, down_c)
        dn2_c = dot(du, up_c)
        out = out_c if out is None else out + out_c
        dn2 = dn2_c if dn2 is None else dn2 + dn2_c
        grad_down, grad_up = dot(g, dy, TN), dot(du, n2, TN)
        if last:
            grad_down, grad_up = grad_down + early_dn[here, :], grad_up + early_up[here, :]
        acc_dn[here, :] = grad_down
        acc_up[here, :] = grad_up
        sums.append(jnp.sum(du.astype(F32), axis=0, keepdims=True))
    lines = [
        jnp.sum(dn2 * normal_s[...], axis=0, keepdims=True),
        jnp.sum(dn2, axis=0, keepdims=True),
        jnp.concatenate(sums, axis=1),
    ]
    for i, line in enumerate(lines):
        size = line.shape[1]
        if last:
            line = line + early_sums[i : i + 1, :size]
        sums_ref[i : i + 1, :size] = line
    for i, target in enumerate((keep_ref, send_ref)):
        here = slice(i * rows, (i + 1) * rows)
        target[0] = out[here].astype(BF)
        target[1] = (dn2[here] * vec_ref[2:3]).astype(BF)
    if last:
        spread_shards(acc_up, seq_orders[0], seq_me, upk_ref, ups_ref)
        spread_shards(acc_dn, seq_orders[1], seq_me, dnk_ref, dns_ref)


def attend_kernel(kv_bits, dkv_bits, side, per_group, chunk_blocks, most, order_ref, len_ref, *refs):
    qt_ref, dot_ref, *kv_refs, cs_ref = refs[:5]
    refs = refs[5:]
    if side == 1:
        early, refs = refs[:3], refs[3:]
    else:
        early = ()
    count = 4 if side == 0 else 5
    attend_side(
        (kv_bits, dkv_bits),
        side,
        per_group,
        chunk_blocks,
        most,
        order_ref,
        len_ref,
        qt_ref,
        dot_ref,
        kv_refs,
        cs_ref,
        early,
        refs[:count],
        *refs[count:],
    )


def attend_side(
    orders,
    side,
    per_group,
    chunk_blocks,
    most,
    order_ref,
    len_ref,
    qt_ref,
    dot_ref,
    kv_refs,
    cs_ref,
    early,
    outs_refs,
    s_scr,
    p_scr,
    pb_scr,
    ds_scr,
    bias_scr,
    kv_scr,
    kvt_scr,
    dkv_scr,
    qs,
    dos,
    ot,
    dqt,
    inverse,
):
    group = pl.program_id(0)
    o_ref, far_ref, near_ref = outs_refs[:3]
    seq_me = lax.axis_index("seq")
    half = held = kv_refs[0].shape[0]
    slots = 2 * held // BLOCK
    chunk = chunk_blocks * BLOCK
    lanes = per_group * BLOCK
    @pl.when(group == 0)
    def _():
        if side == 0:
            dkv_scr[...] = jnp.zeros_like(dkv_scr)
        else:
            dkv_scr[...] = early[2][...]
            for source, target in zip(early[:2], (o_ref, near_ref)):
                target[:BLOCK] = source[...]

        @pl.loop(0, slots)
        def _(i):
            rel = (i // 2) ^ seq_me
            for at, bits in enumerate(orders):
                place = jnp.int32(0)
                for bit in bits:
                    place = place * 2 + (rel // bit) % 2
                inverse[at, order_ref[i]] = place * 2 + i % 2

    block = order_ref[2 * seq_me + side]
    base = block * BLOCK
    end_1 = len_ref[0, 0]
    end_2 = end_1 + len_ref[0, 1]
    end_3 = end_2 + len_ref[0, 2]

    def start_of(position):
        low = jnp.where(position >= end_1, end_1, 0)
        low = jnp.where(position >= end_2, end_2, low)
        return jnp.where(position >= end_3, end_3, low)

    q_pos = base + lax.broadcasted_iota(jnp.int32, (1, BLOCK), 1)
    q_start = start_of(q_pos)
    low_block = jnp.maximum(start_of(base) // BLOCK, block - (most - 1))
    chunks = (block - low_block + chunk_blocks) // chunk_blocks

    def slot_of(j, at):
        return inverse[at, jnp.minimum(low_block + j, block)]

    @pl.loop(0, chunks * chunk_blocks)
    def _(j):
        start = slot_of(j, 0) * BLOCK
        here = pl.ds(pl.multiple_of(j * BLOCK, BLOCK), BLOCK)
        for i, kv_ref in enumerate(kv_refs):

            @pl.when(start // held == i)
            def _():
                there = pl.multiple_of(start - i * held, BLOCK)
                kv_scr[here, :] = kv_ref[pl.ds(there, BLOCK), :]

    for h in range(per_group):
        cols = slice(h * BLOCK, (h + 1) * BLOCK)
        qs[:, cols] = qt_ref[h * HDIM : (h + 1) * HDIM, :]
        dos[:, cols] = dot_ref[h * HDIM : (h + 1) * HDIM, :]

    pairs = per_group // 2

    def columns(h):
        return slice(h * BLOCK, (h + 1) * BLOCK)

    def score_step(c, top):
        keys = kv_scr[pl.ds(c * chunk, chunk), :HDIM]
        k_pos = (low_block + c * chunk_blocks) * BLOCK + lax.broadcasted_iota(
            jnp.int32, (chunk, BLOCK), 0
        )
        allowed = jnp.logical_and(k_pos <= q_pos, k_pos >= q_start)
        bias_scr[c] = jnp.where(allowed, 0.0, NEGATIVE)
        tops = []
        for pair in range(pairs):
            s = dot(keys, qs[:, pair * 2 * BLOCK : (pair + 1) * 2 * BLOCK])
            for half_at in range(2):
                part = s[:, columns(half_at)] + bias_scr[c]
                s_scr[c, :, columns(2 * pair + half_at)] = part
                tops.append(jnp.max(part, axis=0, keepdims=True))
        return jnp.maximum(top, jnp.concatenate(tops, axis=1))

    top = lax.fori_loop(0, chunks, score_step, jnp.full((1, lanes), NEGATIVE, F32))

    def weight_step(c, carry):
        total, delta = carry
        totals, deltas = [], []
        values = kv_scr[pl.ds(c * chunk, chunk), HDIM:]
        for pair in range(pairs):
            dp = dot(values, dos[:, pair * 2 * BLOCK : (pair + 1) * 2 * BLOCK])
            for half_at in range(2):
                cols = columns(2 * pair + half_at)
                part = dp[:, columns(half_at)]
                p_scr[c, :, cols] = part
                e = jnp.exp(s_scr[c, :, cols] - top[:, cols])
                s_scr[c, :, cols] = e
                totals.append(jnp.sum(e, axis=0, keepdims=True))
                deltas.append(jnp.sum(e * part, axis=0, keepdims=True))
        return (
            total + jnp.concatenate(totals, axis=1),
            delta + jnp.concatenate(deltas, axis=1),
        )

    zero = jnp.zeros((1, lanes), F32)
    total, delta = lax.fori_loop(0, chunks, weight_step, (zero, zero))
    shrink = 1.0 / total
    delta = delta * shrink
    ot[...] = jnp.zeros_like(ot)
    dqt[...] = jnp.zeros_like(dqt)

    def grad_step(c, _):
        kvt = kvt_scr[c]
        for pair in range(pairs):
            both = slice(pair * 2 * BLOCK, (pair + 1) * 2 * BLOCK)
            for half_at in range(2):
                cols = columns(2 * pair + half_at)
                p = s_scr[c, :, cols] * shrink[:, cols]
                pb_scr[:, cols] = p.astype(BF)
                ds_scr[:, cols] = (p * (p_scr[c, :, cols] - delta[:, cols])).astype(BF)
            ot[:, both] += dot(kvt[HDIM:], pb_scr[:, both])
            dqt[:, both] += dot(kvt[:HDIM], ds_scr[:, both])
        dk = dot(ds_scr[...], qs[...], NT)
        dv = dot(pb_scr[...], dos[...], NT)
        both = jnp.concatenate([dk, dv], axis=1)
        for b in range(chunk_blocks):

            @pl.when(low_block + c * chunk_blocks + b <= block)
            def _():
                place = slot_of(c * chunk_blocks + b, 1) * BLOCK
                dkv_scr[pl.ds(pl.multiple_of(place, BLOCK), BLOCK), :] += both[
                    b * BLOCK : (b + 1) * BLOCK
                ]

        return 0

    @pl.loop(0, chunks)
    def _(c):
        kvt_scr[c] = kv_scr[pl.ds(c * chunk, chunk), :].astype(F32).T.astype(BF)

    lax.fori_loop(0, chunks, grad_step, 0)
    cosine, sine = cs_ref[:HALF], cs_ref[HALF:]
    outs, grads = [], []
    for h in range(per_group):
        cols = slice(h * BLOCK, (h + 1) * BLOCK)
        outs.append(ot[:, cols])
        grad = dqt[:, cols] * SCALE
        first, second = grad[:HALF], grad[HALF:ROT]
        grads.append(first * cosine + second * sine)
        grads.append(second * cosine - first * sine)
        grads.append(grad[ROT:])
    width = o_ref.shape[1]
    here = slice(side * BLOCK, (side + 1) * BLOCK)
    span = per_group * HDIM
    across = pl.ds(0 if span == width else pl.multiple_of(group * span, span), span)
    o_ref[here, across] = jnp.concatenate(outs, axis=0).T.astype(BF)
    grad = jnp.concatenate(grads, axis=0).T.astype(BF)
    far_ref[:, across] = grad
    near_ref[here, across] = grad

    @pl.when(group == pl.num_programs(0) - 1)
    def _():
        me = lax.axis_index("fsdp")
        part = near_ref.shape[1] - width
        count = width // part
        o = o_ref[here, :].astype(F32)
        pieces = [o[:, p * part : (p + 1) * part] for p in range(count)]
        near_ref[here, width:] = pick(pieces, me ^ 1).astype(BF)
        far_ref[:, width:] = jnp.concatenate(
            [pick(pieces, me ^ 2), pick(pieces, me ^ 3)], axis=1
        ).astype(BF)

        if side == 0:
            outs_refs[3][...] = dkv_scr[...]
        else:
            outs_refs[3][...] = dkv_scr[:half].astype(BF)
            outs_refs[4][...] = dkv_scr[half:].astype(BF)


def output_kernel(both_ref, o_ref, wo_ref, vec_ref, dn1_ref, a_ref, b_ref, c_ref, *outs):
    layer_ref, grad_ref = outs
    rows = o_ref.shape[0]
    x, dy = both_ref[:rows].astype(F32), both_ref[rows:].astype(F32)
    mlp = a_ref[0].astype(F32) + b_ref[0].astype(F32) + c_ref[0].astype(F32)
    attention = dot(o_ref[...], wo_ref[...]) + vec_ref[5:6]
    layer_ref[...] = (x + attention + mlp + vec_ref[6:7]).astype(BF)
    normal, inverse_std = normalize(x)
    total = a_ref[1].astype(F32) + b_ref[1].astype(F32) + c_ref[1].astype(F32)
    total = total + dn1_ref[...] * vec_ref[0:1]
    grad_ref[...] = (
        dy
        + inverse_std
        * (
            total
            - jnp.mean(total, -1, keepdims=True)
            - normal * jnp.mean(total * normal, -1, keepdims=True)
        )
    ).astype(BF)


def shard_at(order, m, seq_me):
    return (order[m] ^ seq_me) & order[-1]


def spread_shards(source, order, seq_me, near, far):
    shards = len(order)
    rows = source.shape[0] // shards
    half = shards // 2
    for m in range(shards):
        start = pl.multiple_of(shard_at(order, m, seq_me) * rows, rows)
        target = near if m < half else far
        target[(m % half) * rows : (m % half + 1) * rows, :] = source[pl.ds(start, rows), :].astype(
            BF
        )


def weight_kernel(order, n1a_ref, n1b_ref, o_ref, own_ref, z1_ref, z2_ref, z3_ref, *refs):
    me = lax.axis_index("fsdp")
    rows, part = n1a_ref.shape[1:]
    dys = [ref.at[rows : 2 * rows] for ref in refs[:4]]
    near_ref, far_ref, grad = refs[4:]
    width = dys[0].shape[1]
    o = o_ref[...].astype(F32)
    own = pick([o[:, p * part : (p + 1) * part] for p in range(width // part)], me).astype(BF)
    items = (
        (n1a_ref[0], own_ref[:, :width], own, dys[0][...]),
        (n1a_ref[1], z1_ref[:, :width], z1_ref[:, width:], dys[1][...]),
        (n1b_ref[0], z2_ref[:, :width], z2_ref[:, width:], dys[2][...]),
        (n1b_ref[1], z3_ref[:, :width], z3_ref[:, width:], dys[3][...]),
    )
    grad_q = None
    grad_o = None
    for n1, dq, cols, dy in items:
        term_q, term_o = dot(n1, dq, TN), dot(cols, dy, TN)
        grad_q = term_q if grad_q is None else grad_q + term_q
        grad_o = term_o if grad_o is None else grad_o + term_o
    grad[:part] = grad_q
    grad[part:] = grad_o
    spread_shards(grad, order, lax.axis_index("seq"), near_ref, far_ref)


def tail_kernel(
    rels,
    both_ref,
    n1_ref,
    dq_ref,
    wq_ref,
    wkv_ref,
    vec_ref,
    cs_ref,
    dkvn_ref,
    dkvf_ref,
    sums_ref,
    dn1_ref,
    keep_ref,
    send_ref,
    vs,
):
    count = len(rels)
    me = lax.axis_index("fsdp")
    rows, width = n1_ref.shape
    part = width // count
    dkv = (dkvn_ref[...].astype(F32) + dkvf_ref[...].astype(F32)).T
    cosine, sine = cs_ref[:HALF], cs_ref[HALF:]
    first, second = dkv[:HALF], dkv[HALF:ROT]
    dkv = jnp.concatenate(
        [first * cosine + second * sine, second * cosine - first * sine, dkv[ROT:]], axis=0
    )
    dkv_sum = jnp.sum(dkv.astype(BF).T.astype(F32), axis=0, keepdims=True)
    dkv_t = dkv.astype(BF)
    dq = dq_ref[:, :width]
    dn1 = dot(dq, wq_ref[...], NT) + dot(dkv_t, wkv_ref[...], TN)
    dn1_ref[...] = dn1
    normal, _ = normalize(both_ref[:rows].astype(F32))
    dy = both_ref[rows:].astype(F32)
    grad_kv = dot(dkv_t, n1_ref[...])
    lines = jnp.concatenate(
        [
            jnp.sum(dn1 * normal, axis=0, keepdims=True),
            jnp.sum(dn1, axis=0, keepdims=True),
            sums_ref[0:1, :width],
            sums_ref[1:2, :width],
            jnp.sum(dq.astype(F32), axis=0, keepdims=True),
            jnp.sum(dy, axis=0, keepdims=True),
            jnp.concatenate(
                [jnp.concatenate([dkv_sum, jnp.zeros((1, part - 2 * HDIM), F32)], axis=1)] * count,
                axis=1,
            ),
            jnp.zeros((1, width), F32),
        ],
        axis=0,
    )
    for p in range(count):
        cols = slice(p * part, (p + 1) * part)
        vs[p, : 2 * HDIM, :] = grad_kv[:, cols]
        vs[p, 2 * HDIM :, :] = lines[:, cols]
    half = count // 2
    extra = sums_ref.shape[1] // part
    up_bias = jnp.concatenate(
        [sums_ref[2:3, e * part : (e + 1) * part] for e in range(extra)]
        + [jnp.zeros((8 - extra, part), F32)],
        axis=0,
    )
    size = keep_ref.shape[0] // half
    for m, rel in enumerate(rels):
        target = keep_ref if m < half else send_ref
        piece = vs[rel ^ me]
        last = up_bias if rel == 0 else jnp.zeros_like(up_bias)
        lines = jnp.concatenate([piece[2 * HDIM :], last], axis=0)
        target[(m % half) * size : (m % half + 1) * size] = join_split(
            fold(piece[: 2 * HDIM], count), fold(lines, count)
        )


def join_split(matrix, lines):
    high = lines.astype(BF).astype(F32)
    rest = jnp.zeros((8, matrix.shape[1]), F32)
    return jnp.concatenate([matrix, high, lines - high, rest], axis=0).astype(BF)


def load_split(value):
    value = value.astype(F32)
    return (value[:32], value[32:36] + value[36:40])


def fold(value, count):
    rows = value.shape[0] // count
    return jnp.concatenate([value[i * rows : (i + 1) * rows] for i in range(count)], axis=1)


def unfold(value, part):
    return jnp.concatenate(
        [value[:, i : i + part] for i in range(0, value.shape[1], part)], axis=0
    )


def mix_step(sources, targets):
    each = sources[0].shape[0] // len(targets)
    for i, target in enumerate(targets):
        here = slice(i * each, (i + 1) * each)
        first, second = load_split(sources[0][here]), load_split(sources[1][here])
        target[...] = join_split(first[0] + second[0], first[1] + second[1])


def merge_step(sources, targets):
    a_ref, b_ref = sources
    rows = a_ref.shape[0] // len(targets)
    for i, target in enumerate(targets):
        here = slice(i * rows, (i + 1) * rows)
        target[...] = (a_ref[here].astype(F32) + b_ref[here].astype(F32)).astype(BF)


def relay_kernel(part, first_ref, second_ref, own_ref, next_ref):
    width = own_ref.shape[1] - part
    for i, ref in enumerate((first_ref, second_ref)):
        here = slice(i * BLOCK, (i + 1) * BLOCK)
        own_ref[here] = ref[:, : width + part]
        next_ref[here, :width] = ref[:, :width]
        next_ref[here, width:] = ref[:, width + part :]


def join_step(sources, targets):
    rows = 0
    for source in sources:
        targets[0][rows : rows + source.shape[0]] = source[...]
        rows += source.shape[0]


def matrix_kernel(order, near_view, far_view, near_ref, far_ref, *refs):
    outs, (held, sems) = refs[:-2], refs[-2:]
    seq_me = lax.axis_index("seq")
    shards = len(order)
    half = shards // 2
    near_ref = near_ref.at[near_view[0] : near_view[0] + near_view[1]]
    far_ref = far_ref.at[far_view[0] : far_view[0] + far_view[1]]
    rows = near_ref.shape[0] // half
    each = shards // len(outs)
    copies = []
    for t in range(shards):
        place = jnp.int32(0)
        for m in range(shards):
            place = jnp.where(shard_at(order, m, seq_me) == t, m, place)
        start = pl.multiple_of((place & (half - 1)) * rows, rows)

        @pl.when(place < half)
        def _():
            held[t] = near_ref[pl.ds(start, rows), :].astype(F32)

        @pl.when(place >= half)
        def _():
            held[t] = far_ref[pl.ds(start, rows), :].astype(F32)

        first = (t % each) * rows
        copy = pltpu.make_async_copy(
            held.at[t], outs[t // each].at[first : first + rows, :], sems.at[t]
        )
        copy.start()
        copies.append(copy)
    for copy in copies:
        copy.wait()


def vector_kernel(a_at, b_at, a_ref, b_ref, g1, b1, qb, kb, vb, ob, g2, b2, ub, db, wk_ref, wv_ref):
    me = lax.axis_index("fsdp")
    first, second = load_split(a_ref[a_at : a_at + 48]), load_split(b_ref[b_at : b_at + 48])
    part = g1.shape[0]
    total = unfold(first[0] + second[0], part)
    lines = unfold(first[1] + second[1], part)
    wk_ref[...] = total[:HDIM]
    wv_ref[...] = total[HDIM:]
    for i, targets in enumerate(((g1,), (b1,), (g2,), (b2,), (qb,), (ob, db))):
        for target in targets:
            target[...] = lines[i : i + 1].reshape(part)
    kp, vp = kb.shape[0], vb.shape[0]
    line = lines[6:7]
    count = HDIM // vp
    kb[...] = pick([line[:, p * kp : (p + 1) * kp] for p in range(count)], me).reshape(kp)
    vb[...] = pick(
        [line[:, HDIM + p * vp : HDIM + (p + 1) * vp] for p in range(count)], me
    ).reshape(vp)
    extra = ub.shape[0] // part
    ub[...] = jnp.concatenate([lines[8 + e : 9 + e] for e in range(extra)], axis=1).reshape(
        ub.shape[0]
    )


def shard_count(rows, devices):
    shards = devices
    while shards > 2 and (rows % shards or (rows // shards) % 16):
        shards //= 2
    return shards


def shard_order(bits):
    order = [0]
    for bit in reversed(bits):
        order = order + [r ^ bit for r in order]
    return order


def on_device(
    tokens,
    block_order,
    doc_lengths,
    norm_one_gain,
    norm_one_bias,
    query_weight,
    query_bias,
    key_weight,
    key_bias,
    value_weight,
    value_bias,
    out_weight,
    out_bias,
    norm_two_gain,
    norm_two_bias,
    up_weight,
    up_bias,
    down_weight,
    down_bias,
    cotangent,
):
    _, rows, width = tokens.shape
    hidden = up_weight.shape[0]
    part = query_weight.shape[0]
    fsdp = lax.axis_size("fsdp")
    seqs = lax.axis_size("seq")
    slots = 2 * seqs
    fbits = bits_of(fsdp)
    sbits = bits_of(seqs)
    rels = rel_order(fsdp)
    fsdp_me = lax.axis_index("fsdp")
    seq_me = lax.axis_index("seq")
    x_own = tokens.reshape(rows, width)
    dy_own = cotangent.reshape(rows, width)

    def spread(value):
        parts = [value]
        for bit in reversed(fbits):
            parts = parts + [swap(v, "fsdp", bit) for v in parts]
        return parts

    pieces = (
        x_own,
        dy_own,
        query_weight,
        out_weight,
        norm_one_gain,
        norm_one_bias,
        norm_two_gain,
        norm_two_bias,
        query_bias,
        out_bias,
        down_bias,
        key_bias,
        value_bias,
        key_weight.T,
        value_weight.T,
    )
    sequence = Sequence()
    run = sequence.run
    pack, both_0, qo_0, bulk_0 = run(
        pack_kernel,
        (
            shape((2 * HDIM + 16, part), BF),
            shape((2 * rows, width), BF),
            shape((2 * part, width), BF),
            shape((2 * rows + 2 * part, width), BF),
        ),
        pieces,
        [pltpu.VMEM(v.shape, BF) for v in pieces[4:]] + [pltpu.SemaphoreType.DMA((len(pieces) + 4,))],
        limit=60,
        name="pack",
        time=2,
        in_specs=[HBM] * len(pieces),
    )
    packs = spread(pack)
    qo_2 = swap(qo_0, "fsdp", 2)
    both_2 = swap(both_0, "fsdp", 2)
    bulk_1 = swap(bulk_0, "fsdp", 1)

    own_blocks = lax.dynamic_slice_in_dim(block_order, 2 * seq_me, 2)
    offsets = jnp.arange(BLOCK, dtype=jnp.int32)
    own_pos = (own_blocks[:, None] * BLOCK + offsets[None, :]).reshape(rows)
    frequencies = 10000.0 ** (-2.0 * jnp.arange(HALF, dtype=F32) / ROT)
    angles = own_pos.astype(F32)[None, :] * frequencies[:, None]
    cs = run(
        table_kernel,
        shape((ROT, rows), F32),
        (jnp.cos(angles), jnp.sin(angles)),
        name="tables",
        time=5,
    )

    n1, kv_own, vec, wkv = run(
        functools.partial(front_kernel, rels),
        (
            shape((rows, width), BF),
            shape((rows, 2 * HDIM), BF),
            shape((16, width), F32),
            shape((2 * HDIM, width), BF),
        ),
        (x_own, *packs, cs),
        [pltpu.VMEM((fsdp, 16, part), F32), pltpu.VMEM((fsdp, 2 * HDIM, part), BF)],
        name="front",
        time=1,
    )

    kv = kv_own
    for bit in reversed(sbits[3:]):
        kv = join_all(sequence, kv, swap(kv, "seq", bit))
    kv_parts = [kv] + [swap(kv, "seq", bit) for bit in (sbits[2], sbits[1], sbits[1] + sbits[2])]
    kv_bits = sbits

    up_bits, dn_bits = sbits[:2], [sbits[1], sbits[0]]
    seq_orders = (shard_order(up_bits), shard_order(dn_bits))

    def others(bits):
        return sorted((b for b in sbits if b not in bits), key=lambda b: (b > sbits[2], -b))

    chunk_out = shape((2, rows, width), BF)
    n1c_out = shape((2, rows, part), BF)
    sums_out = shape((8, max(hidden, width)), F32)
    mlp_scratch = [
        pltpu.VMEM((2 * rows, width), F32),
        pltpu.VMEM((2 * rows, width), BF),
        pltpu.VMEM((2 * rows, width), BF),
    ]
    most = min(slots, slots // 2 + 1)
    chunk_blocks = 2
    most_chunks = -(-most // chunk_blocks)
    chunk = chunk_blocks * BLOCK
    per_group = HEADS
    while most_chunks * chunk * per_group * BLOCK * 8 > 20 * MIB and per_group > 2:
        per_group = {12: 6, 6: 4, 4: 2}[per_group]
    lanes = per_group * BLOCK
    span = per_group * HDIM
    def attend(side, early, outs):
        return run(
            functools.partial(attend_kernel, kv_bits, sbits, side, per_group, chunk_blocks, most),
            outs,
            (block_order, doc_lengths, qt, do_t, *kv_parts, cs, *early),
            [
                pltpu.VMEM((most_chunks, chunk, lanes), F32),
                pltpu.VMEM((most_chunks, chunk, lanes), F32),
                pltpu.VMEM((chunk, lanes), BF),
                pltpu.VMEM((chunk, lanes), BF),
                pltpu.VMEM((most_chunks, chunk, BLOCK), F32),
                pltpu.VMEM((most_chunks * chunk, 2 * HDIM), BF),
                pltpu.VMEM((most_chunks, 2 * HDIM, chunk), BF),
                pltpu.VMEM((slots * BLOCK, 2 * HDIM), F32),
                pltpu.VMEM((HDIM, lanes), BF),
                pltpu.VMEM((HDIM, lanes), BF),
                pltpu.VMEM((HDIM, lanes), F32),
                pltpu.VMEM((HDIM, lanes), F32),
                pltpu.SMEM((2, slots), jnp.int32),
            ],
            limit=36 if slots <= 16 else 60,
            name="attend",
            time=(2, 10)[side],
            grid=(HEADS // per_group,),
            in_specs=[
                SMEM,
                SMEM,
                pl.BlockSpec((span, BLOCK), lambda g: (g, side)),
                pl.BlockSpec((span, BLOCK), lambda g: (g, side)),
                VMEM,
                VMEM,
                pl.BlockSpec((ROT, BLOCK), lambda g: (0, side)),
            ]
            + [VMEM] * len(early),
        )

    far_out = shape((BLOCK, width + 2 * part), BF)
    keep_a, send_a, n1a, early_up, early_dn, early_sums = run(
        functools.partial(mlp_kernel, None, False),
        (
            chunk_out,
            chunk_out,
            n1c_out,
            shape((hidden, width), F32),
            shape((hidden, width), F32),
            sums_out,
        ),
        (both_0, bulk_1, up_weight, down_weight, up_bias, vec),
        mlp_scratch,
        limit=24,
        name="mlp_near",
        time=0,
    )
    back_a = swap(send_a, "fsdp", 1)
    kv_near = join_all(sequence, *kv_parts)
    kv_parts = [kv_near, swap(kv_near, "seq", sbits[0])]
    task = (join_step, [View(qo_2, 0, part)], 1), (join_step, [View(qo_2, part, part)], 1)
    views = sequence.stage(task)
    qo_3 = [swap(views[t, 0].array, "fsdp", 1) for t in range(2)]
    qt, do_t, wq, wo = run(
        functools.partial(query_kernel, rels),
        (
            shape((width, rows), BF),
            shape((width, rows), BF),
            shape((width, width), BF),
            shape((width, width), BF),
        ),
        (n1, both_0, vec, cs, qo_0, qo_2, bulk_1, *qo_3),
        name="query",
    )

    own, far_0, near, dkv = attend(
        0,
        (),
        (
            shape((BLOCK, width), BF),
            far_out,
            shape((BLOCK, width + part), BF),
            shape((slots * BLOCK, 2 * HDIM), F32),
        ),
    )
    z2 = [swap(far_0, "fsdp", 2)]
    both_3 = swap(join_all(sequence, both_2), "fsdp", 1)
    keep_b, send_b, n1b, upk, ups, dnk, dns, sums = run(
        functools.partial(mlp_kernel, seq_orders, True),
        (chunk_out, chunk_out, n1c_out)
        + (shape((hidden // 2, width), BF),) * 4
        + (sums_out,),
        (both_2, both_3, up_weight, down_weight, up_bias, vec, early_up, early_dn, early_sums),
        mlp_scratch + [pltpu.VMEM((hidden, width), F32)] * 2,
        limit=28,
        name="mlp_far",
        time=8,
        after=(back_a,),
    )
    up = Sum(upk, ups, up_bits, others(up_bits))
    dn = Sum(dnk, dns, dn_bits, others(dn_bits))
    own, far_1, z_near, dkv_near, dkv_far = attend(
        1,
        (own, near, dkv),
        (shape((rows, width), BF), far_out, shape((rows, width + part), BF))
        + (shape((seqs * BLOCK, 2 * HDIM), BF),) * 2,
    )
    z2.append(swap(far_1, "fsdp", 2))
    dkv = Reduce(dkv_near, dkv_far, sbits)
    z1 = swap(z_near, "fsdp", 1)
    flow(sequence, up, dn)
    z2, relay_z = run(
        functools.partial(relay_kernel, part),
        (shape((rows, width + part), BF),) * 2,
        z2,
        name="relay",
    )
    z3 = swap(relay_z, "fsdp", 1)
    flow(sequence, up)
    qo_bits = sbits[:2]
    qo_order = shard_order(qo_bits)
    qok, qos = run(
        functools.partial(weight_kernel, qo_order),
        (shape((part, width), BF),) * 2,
        (n1a, n1b, own, z_near, z1, z2, z3, both_0, bulk_1, both_2, both_3),
        [pltpu.VMEM((2 * part, width), F32)],
        name="weight",
    )
    qo = Sum(qok, qos, qo_bits, others(qo_bits), small=True)
    flow(sequence, dkv)
    while dkv.left():
        flow(sequence, dkv)
    mixed = shape((48 * fsdp // 2, width), BF)
    dn1, near_t, far_t = run(
        functools.partial(tail_kernel, rels),
        (shape((rows, width), F32), mixed, mixed),
        (both_0, n1, z_near, wq, wkv, vec, cs, *[v.array for v in dkv.pair()], sums),
        [pltpu.VMEM((fsdp, 2 * HDIM + 8, part), F32)],
        name="tail",
    )
    mix = Mix(near_t, far_t, fbits, [sbits[1], sbits[0], sbits[2]] + sbits[3:])
    flow(sequence, qo)
    flow(sequence, dn)
    while up.left() > 2:
        flow(sequence, up)
    flow(sequence, up)
    flow(sequence, mix)
    flow(sequence, qo)
    flow(sequence, up)
    flow(sequence, mix)
    back_b = swap(send_b, "fsdp", 1)
    back = sequence.stage([(merge_step, [View(keep_b), View(back_b)], 1)])[0, 0].array
    back = swap(back, "fsdp", 2)
    flow(sequence, mix)
    while dn.left() > 2:
        flow(sequence, dn)
    flow(sequence, dn)
    flow(sequence, qo)
    flow(sequence, mix)
    flow(sequence, qo)
    flow(sequence, dn)
    layer_out, grad_tokens = run(
        output_kernel,
        (shape((rows, width), BF),) * 2,
        (both_0, own, wo, vec, dn1, keep_a, back_a, back),
        name="output",
        token=False,
    )
    while up.left() + dn.left() + qo.left() + mix.left():
        flow(sequence, *[item for item in (qo, mix, up, dn) if item.left()])

    def matrix(item, order, count):
        near, far = item.pair()
        each = 2 * near.rows // len(order)
        views = [(view.start, view.rows) for view in (near, far)]
        return run(
            functools.partial(matrix_kernel, order, *views),
            (shape((2 * near.rows // count, width), F32),) * count,
            (near.array, far.array),
            [
                pltpu.VMEM((len(order), each, width), F32),
                pltpu.SemaphoreType.DMA((len(order),)),
            ],
            name="matrix",
            token=False,
            out_specs=(HBM,) * count,
        )

    vector = shape((part,), F32)
    g1, b1, qb, kb, vb, ob, g2, b2, ub, db, wk, wv = run(
        functools.partial(vector_kernel, *[v.start for v in mix.pair()]),
        (
            vector,
            vector,
            vector,
            shape(key_bias.shape, F32),
            shape(value_bias.shape, F32),
            vector,
            vector,
            vector,
            shape((hidden,), F32),
            vector,
            shape((HDIM, part), F32),
            shape((HDIM, part), F32),
        ),
        tuple(v.array for v in mix.pair()),
        limit=16,
        token=False,
        name="vector",
    )
    grad_query, grad_out = matrix(qo, qo_order, 2)
    (grad_up,) = matrix(up, seq_orders[0], 1)
    (grad_down,) = matrix(dn, seq_orders[1], 1)
    return (
        layer_out.reshape(1, rows, width),
        grad_tokens.reshape(1, rows, width),
        g1,
        b1,
        grad_query,
        qb,
        wk.T,
        kb,
        wv.T,
        vb,
        grad_out,
        ob,
        g2,
        b2,
        grad_up,
        ub,
        grad_down,
        db,
    )


def solution(mesh):
    split = P("fsdp")
    matrix = P("fsdp", None)
    stream = P("fsdp", "seq", None)
    return jax.shard_map(
        on_device,
        mesh=mesh,
        in_specs=(
            stream,
            P(),
            matrix,
            split,
            split,
            matrix,
            split,
            matrix,
            split,
            matrix,
            split,
            matrix,
            split,
            split,
            split,
            matrix,
            split,
            matrix,
            split,
            stream,
        ),
        out_specs=(
            stream,
            stream,
            split,
            split,
            matrix,
            split,
            matrix,
            split,
            matrix,
            split,
            matrix,
            split,
            split,
            split,
            matrix,
            split,
            matrix,
            split,
        ),
        check_vma=False,
    )
```

```python
import functools

import jax
import jax.numpy as jnp
from jax import lax
from jax.experimental import pallas as pl
from jax.experimental.pallas import tpu as pltpu
from jax.sharding import PartitionSpec as P

HEADS = 12
HDIM = 64
ROT = 16
HALF = ROT // 2
BLOCK = 128

NEGATIVE = -1e30
EPSILON = 1e-05
SQRT_HALF = 0.7071067811865476
GAUSS_FACTOR = 0.3989422804014327
SCALE = HDIM ** (-0.5)
BF = jnp.bfloat16
F32 = jnp.float32
MIB = 1024 * 1024
VMEM = pl.BlockSpec(memory_space=pltpu.VMEM)
SMEM = pl.BlockSpec(memory_space=pltpu.SMEM)
ANY = pl.BlockSpec(memory_space=pl.ANY)
HBM = pl.BlockSpec(memory_space=pltpu.HBM)

NN = (((1,), (0,)), ((), ()))
NT = (((1,), (1,)), ((), ()))
TN = (((0,), (0,)), ((), ()))


def dot(left, right, dims=NN):
    return lax.dot_general(left, right, dims, preferred_element_type=F32)


def shape(dims, dtype):
    return jax.ShapeDtypeStruct(dims, dtype)


def params(limit=48):
    return pltpu.CompilerParams(vmem_limit_bytes=limit * MIB)


def micros(time):
    return pl.CostEstimate(flops=max(1, time * 1000000000), bytes_accessed=1000, transcendentals=0)


class Sequence:
    def __init__(self):
        self.last = ()

    def run(self, kernel, outs, ins, scratch=(), limit=16, name=None, after=(), time=0, token=True, **specs):
        single = isinstance(outs, jax.ShapeDtypeStruct)
        self.last = self.last + tuple(after)
        count, extra = len(ins), len(self.last)

        def body(*refs):
            kernel(*refs[:count], *refs[count + extra :])

        results = pl.pallas_call(
            body,
            out_shape=outs,
            in_specs=list(specs.get("in_specs", [VMEM] * count)) + [ANY] * extra,
            out_specs=specs.get("out_specs", VMEM if single else (VMEM,) * len(outs)),
            grid=specs.get("grid", ()),
            scratch_shapes=list(scratch),
            compiler_params=params(limit),
            cost_estimate=micros(time),
            name=name,
        )(*ins, *self.last)
        if token:
            self.last = (min((results,) if single else results, key=lambda v: v.size),)
        return results

    def stage(self, tasks, bundles=(), after=()):
        bundles = [list(bundle) for bundle in bundles]
        placed = {key for bundle in bundles for key in bundle}
        for t, (_, _, parts) in enumerate(tasks):
            bundles += [[(t, p)] for p in range(parts) if (t, p) not in placed]
        sizes = {}
        for t, (kind, views, parts) in enumerate(tasks):
            rows = sum(v.rows for v in views) if kind is join_step else views[0].rows
            for p in range(parts):
                sizes[t, p] = rows // parts
        ins, outs, spots = [], [], {}
        for index, bundle in enumerate(bundles):
            start = 0
            for key in bundle:
                spots[key] = (index, start, sizes[key])
                start += sizes[key]
            like = tasks[bundle[0][0]][1][0].array
            outs.append(shape((start,) + like.shape[1:], BF))
        plan = []
        for t, (kind, views, parts) in enumerate(tasks):
            sources = []
            for view in views:
                at = next((i for i, v in enumerate(ins) if v is view.array), len(ins))
                if at == len(ins):
                    ins.append(view.array)
                sources.append((at, view.start, view.rows))
            plan.append((kind, sources, [spots[t, p] for p in range(parts)]))

        def kernel(*refs):
            def pieces(found, offset):
                return [refs[offset + i].at[start : start + size] for i, start, size in found]

            for kind, sources, targets in plan:
                kind(pieces(sources, 0), pieces(targets, len(ins)))

        results = self.run(kernel, tuple(outs), ins, name="stage", after=after)
        return {key: View(results[i], start, rows) for key, (i, start, rows) in spots.items()}


class View:
    def __init__(self, array, start=0, rows=None):
        self.array, self.start = array, start
        self.rows = array.shape[0] if rows is None else rows


class Sum:
    def __init__(self, near, far, bits, rest, small=False):
        self.small = small
        self.near, self.coming = View(near), View(swap(far, "seq", bits[0]))
        plan = [(bit, 2) for bit in bits[1:]] + [(bit, 1) for bit in rest]
        plan += [(bits[-1], 1)] + [(bit, -1) for bit in reversed(bits[:-1])]
        self.plan = [("seq", bit, parts) for bit, parts in plan]

    def left(self):
        return len(self.plan)

    def task(self):
        parts = self.plan[0][2]
        if parts == -1:
            return (join_step, [self.near, self.coming], 1)
        return (merge_step, [self.near, self.coming], parts)

    def pair(self):
        return (self.near, self.coming)


class Reduce(Sum):
    def __init__(self, near, far, bits):
        Sum.__init__(self, near, far, bits, [])
        self.plan = self.plan[: len(bits) - 1]


class Mix(Sum):
    def __init__(self, near, far, fbits, sbits):
        self.small = True
        self.near, self.coming = View(near), View(swap(far, "fsdp", fbits[0]))
        self.plan = [("fsdp", bit, 2) for bit in fbits[1:]] + [("seq", bit, 1) for bit in sbits]

    def task(self):
        return (mix_step, [self.near, self.coming], self.plan[0][2])


def join_all(sequence, *arrays, after=()):
    task = (join_step, [View(v) for v in arrays], 1)
    return sequence.stage([task], after=after)[0, 0].array


def flow(sequence, *items, extra=(), after=(), together=False):
    tasks = [item.task() for item in items] + list(extra)
    groups = {}
    for t, item in enumerate(items):
        axis, bit, _ = item.plan[0]
        key = (axis, bit, 0 if item.small or together else 1 + t)
        groups.setdefault(key, []).append((t, tasks[t][2] - 1))
    views = sequence.stage(tasks, groups.values(), after)
    for (axis, bit, _), keys in groups.items():
        sent = swap(views[keys[0]].array, axis, bit)
        for t, part in keys:
            view = views[t, part]
            items[t].near = views[t, 0]
            items[t].coming = View(sent, view.start, view.rows)
            items[t].plan.pop(0)
    return [views[len(items) + i, 0].array for i in range(len(extra))]


def swap(value, axis, bit):
    size = lax.axis_size(axis)
    return lax.ppermute(value, axis, [(i, i ^ bit) for i in range(size)])


def bits_of(size):
    return [1 << i for i in range(size.bit_length() - 1)]


def normalize(values):
    center = values - jnp.mean(values, -1, keepdims=True)
    inverse_std = lax.rsqrt(jnp.mean(center * center, -1, keepdims=True) + EPSILON)
    return (center * inverse_std, inverse_std)


def pick(pieces, index):
    result = pieces[-1]
    for i in range(len(pieces) - 2, -1, -1):
        result = jnp.where(index == i, pieces[i], result)
    return result


def rel_order(size):
    order = [0]
    for bit in reversed(bits_of(size)):
        order = order + [r ^ bit for r in order]
    return order


def pack_kernel(*refs):
    count = len(refs) // 2
    pack_ref, both_ref, qo_ref, bulk_ref = refs[count : count + 4]
    sems = refs[-1]
    rows, part = refs[0].shape[0], refs[2].shape[0]
    held = (both_ref.at[:rows], both_ref.at[rows:], qo_ref.at[:part], qo_ref.at[part:])
    held += refs[count + 4 : -1]
    start = 0
    pairs = [(refs[i], held[i]) for i in range(count)]
    for ref in refs[:4]:
        size = ref.shape[0]
        pairs.append((ref, bulk_ref.at[start : start + size]))
        start += size
    copies = [pltpu.make_async_copy(*pair, sems.at[i]) for i, pair in enumerate(pairs)]
    for copy in copies:
        copy.start()
    for copy in copies:
        copy.wait()
    g1, b1, g2, b2, qb, ob, db, kb, vb, wk_ref, wv_ref = held[4:]
    small = jnp.concatenate(
        [
            kb[...].astype(F32).reshape(1, kb.shape[0]),
            vb[...].astype(F32).reshape(1, vb.shape[0]),
            jnp.zeros((1, part - kb.shape[0] - vb.shape[0]), F32),
        ],
        axis=1,
    )
    lines = [ref[...].astype(F32).reshape(1, part) for ref in (g1, b1, g2, b2, qb, ob, db)]
    lines = jnp.concatenate(lines + [small, jnp.zeros((8, part), F32)], axis=0)
    pack_ref[:HDIM] = wk_ref[...]
    pack_ref[HDIM : 2 * HDIM] = wv_ref[...]
    pack_ref[2 * HDIM :] = lines.astype(BF)


def table_kernel(cosine, sine, out):
    out[:HALF] = cosine[...]
    out[HALF:] = sine[...]


def front_kernel(rels, x_ref, *refs):
    count = len(rels)
    packs = refs[:count]
    cs_ref, n1_ref, kv_ref, vec_ref, wkv_ref, pieces, weights = refs[count:]
    me = lax.axis_index("fsdp")
    for rel, pack in zip(rels, packs):
        weights[rel ^ me] = pack[: 2 * HDIM, :]
        pieces[rel ^ me] = pack[2 * HDIM :, :].astype(F32)
    wkv = jnp.concatenate([weights[p] for p in range(count)], axis=1)
    wkv_ref[...] = wkv
    vec = jnp.concatenate([pieces[p] for p in range(count)], axis=1)
    vec_ref[...] = vec
    normal, _ = normalize(x_ref[...].astype(F32))
    n1 = (normal * vec[0:1] + vec[1:2]).astype(BF)
    n1_ref[...] = n1
    key_part, value_part = ROT // count, HDIM // count
    key_bias = jnp.concatenate([pieces[p][7:8, :key_part] for p in range(count)], axis=1)
    value_bias = jnp.concatenate(
        [pieces[p][7:8, key_part : key_part + value_part] for p in range(count)], axis=1
    )
    bias = jnp.concatenate([key_bias, jnp.zeros((1, HDIM - ROT), F32), value_bias], axis=1)
    turned = (dot(n1, wkv, NT) + bias).T
    cosine, sine = cs_ref[:HALF], cs_ref[HALF:]
    first, second = turned[:HALF], turned[HALF:ROT]
    turned = jnp.concatenate(
        [first * cosine - second * sine, second * cosine + first * sine, turned[ROT:]], axis=0
    )
    kv_ref[...] = turned.T.astype(BF)


def query_kernel(rels, n1_ref, both_ref, vec_ref, cs_ref, *refs):
    count = len(rels) - 1
    part = refs[0].shape[0] // 2
    tops = [pack.shape[0] - 2 * part for pack in refs[:count]]
    pairs = [
        (pack.at[top : top + part], pack.at[top + part : top + 2 * part])
        for pack, top in zip(refs[:count], tops)
    ]
    pairs.append(refs[count : count + 2])
    qt_ref, dot_ref, wq_ref, wo_ref = refs[count + 2 :]
    me = lax.axis_index("fsdp")
    for rel, (near, far) in zip(rels, pairs):
        start = pl.multiple_of((rel ^ me) * part, part)
        wq_ref[pl.ds(start, part), :] = near[...]
        wo_ref[pl.ds(start, part), :] = far[...]
    turned = (dot(n1_ref[...], wq_ref[...]) + vec_ref[4:5]).T
    cosine, sine = cs_ref[:HALF], cs_ref[HALF:]
    for h in range(HEADS):
        base = h * HDIM
        first, second = turned[base : base + HALF], turned[base + HALF : base + ROT]
        head = jnp.concatenate(
            [
                first * cosine - second * sine,
                second * cosine + first * sine,
                turned[base + ROT : base + HDIM],
            ],
            axis=0,
        )
        qt_ref[base : base + HDIM, :] = (head.astype(BF).astype(F32) * SCALE).astype(BF)
    dy = both_ref[n1_ref.shape[0] :]
    dot_ref[...] = dot(dy, wo_ref[...], NT).T.astype(BF)


def mlp_kernel(seq_orders, last, *refs):
    both, refs = refs[:2], refs[2:]
    if last:
        up_ref, down_ref, ub_ref, vec_ref, early_up, early_dn, early_sums = refs[:7]
        keep_ref, send_ref, n1c_ref, upk_ref, ups_ref, dnk_ref, dns_ref, sums_ref = refs[7:15]
        normal_s, n2_s, dy_s, acc_up, acc_dn = refs[15:]
    else:
        up_ref, down_ref, ub_ref, vec_ref = refs[:4]
        keep_ref, send_ref, n1c_ref, acc_up, acc_dn, sums_ref = refs[4:10]
        normal_s, n2_s, dy_s = refs[10:]
    me = lax.axis_index("fsdp")
    seq_me = lax.axis_index("seq")
    hidden, width = up_ref.shape
    part = n1c_ref.shape[2]
    rows = n1c_ref.shape[1]
    for i in range(2):
        here = slice(i * rows, (i + 1) * rows)
        x, dy = both[i][:rows], both[i][rows : 2 * rows]
        dy_s[here] = dy
        normal, _ = normalize(x.astype(F32))
        normal_s[here] = normal
        n1 = normal * vec_ref[0:1] + vec_ref[1:2]
        n1c_ref[i] = pick(
            [n1[:, p * part : (p + 1) * part] for p in range(width // part)], me
        ).astype(BF)
        n2_s[here] = (normal * vec_ref[2:3] + vec_ref[3:4]).astype(BF)
    n2, dy = n2_s[...], dy_s[...]
    out = None
    dn2 = None
    tile = 256
    bias = ub_ref[...].astype(F32).reshape(1, hidden)
    sums = []
    for c in range(hidden // tile):
        here = slice(c * tile, (c + 1) * tile)
        up_c, down_c = up_ref[here, :], down_ref[here, :]
        u = dot(n2, up_c, NT) + bias[:, here]
        dg = dot(dy, down_c, NT)
        phi = 0.5 * (1.0 + lax.erf(u * SQRT_HALF))
        g = (u * phi).astype(BF)
        du = (dg * (phi + u * jnp.exp(-0.5 * u * u) * GAUSS_FACTOR)).astype(BF)
        out_c = dot(g, down_c)
        dn2_c = dot(du, up_c)
        out = out_c if out is None else out + out_c
        dn2 = dn2_c if dn2 is None else dn2 + dn2_c
        grad_down, grad_up = dot(g, dy, TN), dot(du, n2, TN)
        if last:
            grad_down, grad_up = grad_down + early_dn[here, :], grad_up + early_up[here, :]
        acc_dn[here, :] = grad_down
        acc_up[here, :] = grad_up
        sums.append(jnp.sum(du.astype(F32), axis=0, keepdims=True))
    lines = [
        jnp.sum(dn2 * normal_s[...], axis=0, keepdims=True),
        jnp.sum(dn2, axis=0, keepdims=True),
        jnp.concatenate(sums, axis=1),
    ]
    for i, line in enumerate(lines):
        size = line.shape[1]
        if last:
            line = line + early_sums[i : i + 1, :size]
        sums_ref[i : i + 1, :size] = line
    for i, target in enumerate((keep_ref, send_ref)):
        here = slice(i * rows, (i + 1) * rows)
        target[0] = out[here].astype(BF)
        target[1] = (dn2[here] * vec_ref[2:3]).astype(BF)
    if last:
        spread_shards(acc_up, seq_orders[0], seq_me, upk_ref, ups_ref)
        spread_shards(acc_dn, seq_orders[1], seq_me, dnk_ref, dns_ref)


def attend_kernel(kv_bits, dkv_bits, side, per_group, chunk_blocks, most, order_ref, len_ref, *refs):
    qt_ref, dot_ref, *kv_refs, cs_ref = refs[:5]
    refs = refs[5:]
    if side == 1:
        early, refs = refs[:3], refs[3:]
    else:
        early = ()
    count = 4 if side == 0 else 5
    attend_side(
        (kv_bits, dkv_bits),
        side,
        per_group,
        chunk_blocks,
        most,
        order_ref,
        len_ref,
        qt_ref,
        dot_ref,
        kv_refs,
        cs_ref,
        early,
        refs[:count],
        *refs[count:],
    )


def attend_side(
    orders,
    side,
    per_group,
    chunk_blocks,
    most,
    order_ref,
    len_ref,
    qt_ref,
    dot_ref,
    kv_refs,
    cs_ref,
    early,
    outs_refs,
    s_scr,
    p_scr,
    pb_scr,
    ds_scr,
    bias_scr,
    kv_scr,
    kvt_scr,
    dkv_scr,
    qs,
    dos,
    ot,
    dqt,
    inverse,
):
    group = pl.program_id(0)
    o_ref, far_ref, near_ref = outs_refs[:3]
    seq_me = lax.axis_index("seq")
    half = held = kv_refs[0].shape[0]
    slots = 2 * held // BLOCK
    chunk = chunk_blocks * BLOCK
    lanes = per_group * BLOCK
    @pl.when(group == 0)
    def _():
        if side == 0:
            dkv_scr[...] = jnp.zeros_like(dkv_scr)
        else:
            dkv_scr[...] = early[2][...]
            for source, target in zip(early[:2], (o_ref, near_ref)):
                target[:BLOCK] = source[...]

        @pl.loop(0, slots)
        def _(i):
            rel = (i // 2) ^ seq_me
            for at, bits in enumerate(orders):
                place = jnp.int32(0)
                for bit in bits:
                    place = place * 2 + (rel // bit) % 2
                inverse[at, order_ref[i]] = place * 2 + i % 2

    block = order_ref[2 * seq_me + side]
    base = block * BLOCK
    end_1 = len_ref[0, 0]
    end_2 = end_1 + len_ref[0, 1]
    end_3 = end_2 + len_ref[0, 2]

    def start_of(position):
        low = jnp.where(position >= end_1, end_1, 0)
        low = jnp.where(position >= end_2, end_2, low)
        return jnp.where(position >= end_3, end_3, low)

    q_pos = base + lax.broadcasted_iota(jnp.int32, (1, BLOCK), 1)
    q_start = start_of(q_pos)
    low_block = jnp.maximum(start_of(base) // BLOCK, block - (most - 1))
    chunks = (block - low_block + chunk_blocks) // chunk_blocks

    def slot_of(j, at):
        return inverse[at, jnp.minimum(low_block + j, block)]

    @pl.loop(0, chunks * chunk_blocks)
    def _(j):
        start = slot_of(j, 0) * BLOCK
        here = pl.ds(pl.multiple_of(j * BLOCK, BLOCK), BLOCK)
        for i, kv_ref in enumerate(kv_refs):

            @pl.when(start // held == i)
            def _():
                there = pl.multiple_of(start - i * held, BLOCK)
                kv_scr[here, :] = kv_ref[pl.ds(there, BLOCK), :]

    for h in range(per_group):
        cols = slice(h * BLOCK, (h + 1) * BLOCK)
        qs[:, cols] = qt_ref[h * HDIM : (h + 1) * HDIM, :]
        dos[:, cols] = dot_ref[h * HDIM : (h + 1) * HDIM, :]

    pairs = per_group // 2

    def columns(h):
        return slice(h * BLOCK, (h + 1) * BLOCK)

    def score_step(c, top):
        keys = kv_scr[pl.ds(c * chunk, chunk), :HDIM]
        k_pos = (low_block + c * chunk_blocks) * BLOCK + lax.broadcasted_iota(
            jnp.int32, (chunk, BLOCK), 0
        )
        allowed = jnp.logical_and(k_pos <= q_pos, k_pos >= q_start)
        bias_scr[c] = jnp.where(allowed, 0.0, NEGATIVE)
        tops = []
        for pair in range(pairs):
            s = dot(keys, qs[:, pair * 2 * BLOCK : (pair + 1) * 2 * BLOCK])
            for half_at in range(2):
                part = s[:, columns(half_at)] + bias_scr[c]
                s_scr[c, :, columns(2 * pair + half_at)] = part
                tops.append(jnp.max(part, axis=0, keepdims=True))
        return jnp.maximum(top, jnp.concatenate(tops, axis=1))

    top = lax.fori_loop(0, chunks, score_step, jnp.full((1, lanes), NEGATIVE, F32))

    def weight_step(c, carry):
        total, delta = carry
        totals, deltas = [], []
        values = kv_scr[pl.ds(c * chunk, chunk), HDIM:]
        for pair in range(pairs):
            dp = dot(values, dos[:, pair * 2 * BLOCK : (pair + 1) * 2 * BLOCK])
            for half_at in range(2):
                cols = columns(2 * pair + half_at)
                part = dp[:, columns(half_at)]
                p_scr[c, :, cols] = part
                e = jnp.exp(s_scr[c, :, cols] - top[:, cols])
                s_scr[c, :, cols] = e
                totals.append(jnp.sum(e, axis=0, keepdims=True))
                deltas.append(jnp.sum(e * part, axis=0, keepdims=True))
        return (
            total + jnp.concatenate(totals, axis=1),
            delta + jnp.concatenate(deltas, axis=1),
        )

    zero = jnp.zeros((1, lanes), F32)
    total, delta = lax.fori_loop(0, chunks, weight_step, (zero, zero))
    shrink = 1.0 / total
    delta = delta * shrink
    ot[...] = jnp.zeros_like(ot)
    dqt[...] = jnp.zeros_like(dqt)

    def grad_step(c, _):
        kvt = kvt_scr[c]
        for pair in range(pairs):
            both = slice(pair * 2 * BLOCK, (pair + 1) * 2 * BLOCK)
            for half_at in range(2):
                cols = columns(2 * pair + half_at)
                p = s_scr[c, :, cols] * shrink[:, cols]
                pb_scr[:, cols] = p.astype(BF)
                ds_scr[:, cols] = (p * (p_scr[c, :, cols] - delta[:, cols])).astype(BF)
            ot[:, both] += dot(kvt[HDIM:], pb_scr[:, both])
            dqt[:, both] += dot(kvt[:HDIM], ds_scr[:, both])
        dk = dot(ds_scr[...], qs[...], NT)
        dv = dot(pb_scr[...], dos[...], NT)
        both = jnp.concatenate([dk, dv], axis=1)
        for b in range(chunk_blocks):

            @pl.when(low_block + c * chunk_blocks + b <= block)
            def _():
                place = slot_of(c * chunk_blocks + b, 1) * BLOCK
                dkv_scr[pl.ds(pl.multiple_of(place, BLOCK), BLOCK), :] += both[
                    b * BLOCK : (b + 1) * BLOCK
                ]

        return 0

    @pl.loop(0, chunks)
    def _(c):
        kvt_scr[c] = kv_scr[pl.ds(c * chunk, chunk), :].astype(F32).T.astype(BF)

    lax.fori_loop(0, chunks, grad_step, 0)
    cosine, sine = cs_ref[:HALF], cs_ref[HALF:]
    outs, grads = [], []
    for h in range(per_group):
        cols = slice(h * BLOCK, (h + 1) * BLOCK)
        outs.append(ot[:, cols])
        grad = dqt[:, cols] * SCALE
        first, second = grad[:HALF], grad[HALF:ROT]
        grads.append(first * cosine + second * sine)
        grads.append(second * cosine - first * sine)
        grads.append(grad[ROT:])
    width = o_ref.shape[1]
    here = slice(side * BLOCK, (side + 1) * BLOCK)
    span = per_group * HDIM
    across = pl.ds(0 if span == width else pl.multiple_of(group * span, span), span)
    o_ref[here, across] = jnp.concatenate(outs, axis=0).T.astype(BF)
    grad = jnp.concatenate(grads, axis=0).T.astype(BF)
    far_ref[:, across] = grad
    near_ref[here, across] = grad

    @pl.when(group == pl.num_programs(0) - 1)
    def _():
        me = lax.axis_index("fsdp")
        part = near_ref.shape[1] - width
        count = width // part
        o = o_ref[here, :].astype(F32)
        pieces = [o[:, p * part : (p + 1) * part] for p in range(count)]
        near_ref[here, width:] = pick(pieces, me ^ 1).astype(BF)
        far_ref[:, width:] = jnp.concatenate(
            [pick(pieces, me ^ 2), pick(pieces, me ^ 3)], axis=1
        ).astype(BF)

        if side == 0:
            outs_refs[3][...] = dkv_scr[...]
        else:
            outs_refs[3][...] = dkv_scr[:half].astype(BF)
            outs_refs[4][...] = dkv_scr[half:].astype(BF)


def output_kernel(both_ref, o_ref, wo_ref, vec_ref, dn1_ref, a_ref, b_ref, c_ref, *outs):
    layer_ref, grad_ref, mark = outs
    mark[...] = jnp.zeros_like(mark)
    rows = o_ref.shape[0]
    x, dy = both_ref[:rows].astype(F32), both_ref[rows:].astype(F32)
    mlp = a_ref[0].astype(F32) + b_ref[0].astype(F32) + c_ref[0].astype(F32)
    attention = dot(o_ref[...], wo_ref[...]) + vec_ref[5:6]
    layer_ref[...] = (x + attention + mlp + vec_ref[6:7]).astype(BF)
    normal, inverse_std = normalize(x)
    total = a_ref[1].astype(F32) + b_ref[1].astype(F32) + c_ref[1].astype(F32)
    total = total + dn1_ref[...] * vec_ref[0:1]
    grad_ref[...] = (
        dy
        + inverse_std
        * (
            total
            - jnp.mean(total, -1, keepdims=True)
            - normal * jnp.mean(total * normal, -1, keepdims=True)
        )
    ).astype(BF)


def shard_at(order, m, seq_me):
    return (order[m] ^ seq_me) & order[-1]


def spread_shards(source, order, seq_me, near, far):
    shards = len(order)
    rows = source.shape[0] // shards
    half = shards // 2
    for m in range(shards):
        start = pl.multiple_of(shard_at(order, m, seq_me) * rows, rows)
        target = near if m < half else far
        target[(m % half) * rows : (m % half + 1) * rows, :] = source[pl.ds(start, rows), :].astype(
            BF
        )


def weight_kernel(order, n1a_ref, n1b_ref, o_ref, own_ref, z1_ref, z2_ref, z3_ref, *refs):
    me = lax.axis_index("fsdp")
    rows, part = n1a_ref.shape[1:]
    dys = [ref.at[rows : 2 * rows] for ref in refs[:4]]
    near_ref, far_ref, grad = refs[4:]
    width = dys[0].shape[1]
    o = o_ref[...].astype(F32)
    own = pick([o[:, p * part : (p + 1) * part] for p in range(width // part)], me).astype(BF)
    items = (
        (n1a_ref[0], own_ref[:, :width], own, dys[0][...]),
        (n1a_ref[1], z1_ref[:, :width], z1_ref[:, width:], dys[1][...]),
        (n1b_ref[0], z2_ref[:, :width], z2_ref[:, width:], dys[2][...]),
        (n1b_ref[1], z3_ref[:, :width], z3_ref[:, width:], dys[3][...]),
    )
    grad_q = None
    grad_o = None
    for n1, dq, cols, dy in items:
        term_q, term_o = dot(n1, dq, TN), dot(cols, dy, TN)
        grad_q = term_q if grad_q is None else grad_q + term_q
        grad_o = term_o if grad_o is None else grad_o + term_o
    grad[:part] = grad_q
    grad[part:] = grad_o
    spread_shards(grad, order, lax.axis_index("seq"), near_ref, far_ref)


def tail_kernel(
    rels,
    both_ref,
    n1_ref,
    dq_ref,
    wq_ref,
    wkv_ref,
    vec_ref,
    cs_ref,
    dkvn_ref,
    dkvf_ref,
    sums_ref,
    dn1_ref,
    keep_ref,
    send_ref,
    vs,
):
    count = len(rels)
    me = lax.axis_index("fsdp")
    rows, width = n1_ref.shape
    part = width // count
    dkv = (dkvn_ref[...].astype(F32) + dkvf_ref[...].astype(F32)).T
    cosine, sine = cs_ref[:HALF], cs_ref[HALF:]
    first, second = dkv[:HALF], dkv[HALF:ROT]
    dkv = jnp.concatenate(
        [first * cosine + second * sine, second * cosine - first * sine, dkv[ROT:]], axis=0
    )
    dkv_sum = jnp.sum(dkv.astype(BF).T.astype(F32), axis=0, keepdims=True)
    dkv_t = dkv.astype(BF)
    dq = dq_ref[:, :width]
    dn1 = dot(dq, wq_ref[...], NT) + dot(dkv_t, wkv_ref[...], TN)
    dn1_ref[...] = dn1
    normal, _ = normalize(both_ref[:rows].astype(F32))
    dy = both_ref[rows:].astype(F32)
    grad_kv = dot(dkv_t, n1_ref[...])
    lines = jnp.concatenate(
        [
            jnp.sum(dn1 * normal, axis=0, keepdims=True),
            jnp.sum(dn1, axis=0, keepdims=True),
            sums_ref[0:1, :width],
            sums_ref[1:2, :width],
            jnp.sum(dq.astype(F32), axis=0, keepdims=True),
            jnp.sum(dy, axis=0, keepdims=True),
            jnp.concatenate(
                [jnp.concatenate([dkv_sum, jnp.zeros((1, part - 2 * HDIM), F32)], axis=1)] * count,
                axis=1,
            ),
            jnp.zeros((1, width), F32),
        ],
        axis=0,
    )
    for p in range(count):
        cols = slice(p * part, (p + 1) * part)
        vs[p, : 2 * HDIM, :] = grad_kv[:, cols]
        vs[p, 2 * HDIM :, :] = lines[:, cols]
    half = count // 2
    extra = sums_ref.shape[1] // part
    up_bias = jnp.concatenate(
        [sums_ref[2:3, e * part : (e + 1) * part] for e in range(extra)]
        + [jnp.zeros((8 - extra, part), F32)],
        axis=0,
    )
    size = keep_ref.shape[0] // half
    for m, rel in enumerate(rels):
        target = keep_ref if m < half else send_ref
        piece = vs[rel ^ me]
        last = up_bias if rel == 0 else jnp.zeros_like(up_bias)
        lines = jnp.concatenate([piece[2 * HDIM :], last], axis=0)
        target[(m % half) * size : (m % half + 1) * size] = join_split(
            fold(piece[: 2 * HDIM], count), fold(lines, count)
        )


def join_split(matrix, lines):
    high = lines.astype(BF).astype(F32)
    rest = jnp.zeros((8, matrix.shape[1]), F32)
    return jnp.concatenate([matrix, high, lines - high, rest], axis=0).astype(BF)


def load_split(value):
    value = value.astype(F32)
    return (value[:32], value[32:36] + value[36:40])


def fold(value, count):
    rows = value.shape[0] // count
    return jnp.concatenate([value[i * rows : (i + 1) * rows] for i in range(count)], axis=1)


def unfold(value, part):
    return jnp.concatenate(
        [value[:, i : i + part] for i in range(0, value.shape[1], part)], axis=0
    )


def mix_step(sources, targets):
    each = sources[0].shape[0] // len(targets)
    for i, target in enumerate(targets):
        here = slice(i * each, (i + 1) * each)
        first, second = load_split(sources[0][here]), load_split(sources[1][here])
        target[...] = join_split(first[0] + second[0], first[1] + second[1])


def merge_step(sources, targets):
    a_ref, b_ref = sources
    rows = a_ref.shape[0] // len(targets)
    for i, target in enumerate(targets):
        here = slice(i * rows, (i + 1) * rows)
        target[...] = (a_ref[here].astype(F32) + b_ref[here].astype(F32)).astype(BF)


def relay_kernel(part, first_ref, second_ref, own_ref, next_ref):
    width = own_ref.shape[1] - part
    for i, ref in enumerate((first_ref, second_ref)):
        here = slice(i * BLOCK, (i + 1) * BLOCK)
        own_ref[here] = ref[:, : width + part]
        next_ref[here, :width] = ref[:, :width]
        next_ref[here, width:] = ref[:, width + part :]


def join_step(sources, targets):
    rows = 0
    for source in sources:
        targets[0][rows : rows + source.shape[0]] = source[...]
        rows += source.shape[0]


def matrix_kernel(order, near_view, far_view, near_ref, far_ref, *refs):
    outs, (mark, held, sems) = refs[:-3], refs[-3:]
    mark[...] = jnp.zeros_like(mark)
    seq_me = lax.axis_index("seq")
    shards = len(order)
    half = shards // 2
    near_ref = near_ref.at[near_view[0] : near_view[0] + near_view[1]]
    far_ref = far_ref.at[far_view[0] : far_view[0] + far_view[1]]
    rows = near_ref.shape[0] // half
    each = shards // len(outs)
    copies = []
    for t in range(shards):
        place = jnp.int32(0)
        for m in range(shards):
            place = jnp.where(shard_at(order, m, seq_me) == t, m, place)
        start = pl.multiple_of((place & (half - 1)) * rows, rows)

        @pl.when(place < half)
        def _():
            held[t] = near_ref[pl.ds(start, rows), :].astype(F32)

        @pl.when(place >= half)
        def _():
            held[t] = far_ref[pl.ds(start, rows), :].astype(F32)

        first = (t % each) * rows
        copy = pltpu.make_async_copy(
            held.at[t], outs[t // each].at[first : first + rows, :], sems.at[t]
        )
        copy.start()
        copies.append(copy)
    for copy in copies:
        copy.wait()


def vector_kernel(a_at, b_at, a_ref, b_ref, g1, b1, qb, kb, vb, ob, g2, b2, ub, db, wk_ref, wv_ref):
    me = lax.axis_index("fsdp")
    first, second = load_split(a_ref[a_at : a_at + 48]), load_split(b_ref[b_at : b_at + 48])
    part = g1.shape[0]
    total = unfold(first[0] + second[0], part)
    lines = unfold(first[1] + second[1], part)
    wk_ref[...] = total[:HDIM]
    wv_ref[...] = total[HDIM:]
    for i, targets in enumerate(((g1,), (b1,), (g2,), (b2,), (qb,), (ob, db))):
        for target in targets:
            target[...] = lines[i : i + 1].reshape(part)
    kp, vp = kb.shape[0], vb.shape[0]
    line = lines[6:7]
    count = HDIM // vp
    kb[...] = pick([line[:, p * kp : (p + 1) * kp] for p in range(count)], me).reshape(kp)
    vb[...] = pick(
        [line[:, HDIM + p * vp : HDIM + (p + 1) * vp] for p in range(count)], me
    ).reshape(vp)
    extra = ub.shape[0] // part
    ub[...] = jnp.concatenate([lines[8 + e : 9 + e] for e in range(extra)], axis=1).reshape(
        ub.shape[0]
    )


def shard_count(rows, devices):
    shards = devices
    while shards > 2 and (rows % shards or (rows // shards) % 16):
        shards //= 2
    return shards


def shard_order(bits):
    order = [0]
    for bit in reversed(bits):
        order = order + [r ^ bit for r in order]
    return order


def on_device(
    tokens,
    block_order,
    doc_lengths,
    norm_one_gain,
    norm_one_bias,
    query_weight,
    query_bias,
    key_weight,
    key_bias,
    value_weight,
    value_bias,
    out_weight,
    out_bias,
    norm_two_gain,
    norm_two_bias,
    up_weight,
    up_bias,
    down_weight,
    down_bias,
    cotangent,
):
    _, rows, width = tokens.shape
    hidden = up_weight.shape[0]
    part = query_weight.shape[0]
    fsdp = lax.axis_size("fsdp")
    seqs = lax.axis_size("seq")
    slots = 2 * seqs
    fbits = bits_of(fsdp)
    sbits = bits_of(seqs)
    rels = rel_order(fsdp)
    fsdp_me = lax.axis_index("fsdp")
    seq_me = lax.axis_index("seq")
    x_own = tokens.reshape(rows, width)
    dy_own = cotangent.reshape(rows, width)

    def spread(value):
        parts = [value]
        for bit in reversed(fbits):
            parts = parts + [swap(v, "fsdp", bit) for v in parts]
        return parts

    pieces = (
        x_own,
        dy_own,
        query_weight,
        out_weight,
        norm_one_gain,
        norm_one_bias,
        norm_two_gain,
        norm_two_bias,
        query_bias,
        out_bias,
        down_bias,
        key_bias,
        value_bias,
        key_weight.T,
        value_weight.T,
    )
    sequence = Sequence()
    run = sequence.run
    pack, both_0, qo_0, bulk_0 = run(
        pack_kernel,
        (
            shape((2 * HDIM + 16, part), BF),
            shape((2 * rows, width), BF),
            shape((2 * part, width), BF),
            shape((2 * rows + 2 * part, width), BF),
        ),
        pieces,
        [pltpu.VMEM(v.shape, BF) for v in pieces[4:]] + [pltpu.SemaphoreType.DMA((len(pieces) + 4,))],
        limit=60,
        name="pack",
        time=2,
        in_specs=[HBM] * len(pieces),
    )
    packs = spread(pack)
    qo_2 = swap(qo_0, "fsdp", 2)
    both_2 = swap(both_0, "fsdp", 2)
    bulk_1 = swap(bulk_0, "fsdp", 1)

    own_blocks = lax.dynamic_slice_in_dim(block_order, 2 * seq_me, 2)
    offsets = jnp.arange(BLOCK, dtype=jnp.int32)
    own_pos = (own_blocks[:, None] * BLOCK + offsets[None, :]).reshape(rows)
    frequencies = 10000.0 ** (-2.0 * jnp.arange(HALF, dtype=F32) / ROT)
    angles = own_pos.astype(F32)[None, :] * frequencies[:, None]
    cs = run(
        table_kernel,
        shape((ROT, rows), F32),
        (jnp.cos(angles), jnp.sin(angles)),
        name="tables",
        time=5,
    )

    n1, kv_own, vec, wkv = run(
        functools.partial(front_kernel, rels),
        (
            shape((rows, width), BF),
            shape((rows, 2 * HDIM), BF),
            shape((16, width), F32),
            shape((2 * HDIM, width), BF),
        ),
        (x_own, *packs, cs),
        [pltpu.VMEM((fsdp, 16, part), F32), pltpu.VMEM((fsdp, 2 * HDIM, part), BF)],
        name="front",
        time=1,
    )

    kv = kv_own
    for bit in reversed(sbits[3:]):
        kv = join_all(sequence, kv, swap(kv, "seq", bit))
    kv_parts = [kv] + [swap(kv, "seq", bit) for bit in (sbits[2], sbits[1], sbits[1] + sbits[2])]
    kv_bits = sbits

    up_bits, dn_bits = sbits[:2], [sbits[1], sbits[0]]
    seq_orders = (shard_order(up_bits), shard_order(dn_bits))

    def others(bits):
        return sorted((b for b in sbits if b not in bits), key=lambda b: (b > sbits[2], -b))

    chunk_out = shape((2, rows, width), BF)
    n1c_out = shape((2, rows, part), BF)
    sums_out = shape((8, max(hidden, width)), F32)
    mlp_scratch = [
        pltpu.VMEM((2 * rows, width), F32),
        pltpu.VMEM((2 * rows, width), BF),
        pltpu.VMEM((2 * rows, width), BF),
    ]
    most = min(slots, slots // 2 + 1)
    chunk_blocks = 2
    most_chunks = -(-most // chunk_blocks)
    chunk = chunk_blocks * BLOCK
    per_group = HEADS
    while most_chunks * chunk * per_group * BLOCK * 8 > 20 * MIB and per_group > 2:
        per_group = {12: 6, 6: 4, 4: 2}[per_group]
    lanes = per_group * BLOCK
    span = per_group * HDIM
    def attend(side, early, outs):
        return run(
            functools.partial(attend_kernel, kv_bits, sbits, side, per_group, chunk_blocks, most),
            outs,
            (block_order, doc_lengths, qt, do_t, *kv_parts, cs, *early),
            [
                pltpu.VMEM((most_chunks, chunk, lanes), F32),
                pltpu.VMEM((most_chunks, chunk, lanes), F32),
                pltpu.VMEM((chunk, lanes), BF),
                pltpu.VMEM((chunk, lanes), BF),
                pltpu.VMEM((most_chunks, chunk, BLOCK), F32),
                pltpu.VMEM((most_chunks * chunk, 2 * HDIM), BF),
                pltpu.VMEM((most_chunks, 2 * HDIM, chunk), BF),
                pltpu.VMEM((slots * BLOCK, 2 * HDIM), F32),
                pltpu.VMEM((HDIM, lanes), BF),
                pltpu.VMEM((HDIM, lanes), BF),
                pltpu.VMEM((HDIM, lanes), F32),
                pltpu.VMEM((HDIM, lanes), F32),
                pltpu.SMEM((2, slots), jnp.int32),
            ],
            limit=36 if slots <= 16 else 60,
            name="attend",
            time=(2, 14)[side],
            grid=(HEADS // per_group,),
            in_specs=[
                SMEM,
                SMEM,
                pl.BlockSpec((span, BLOCK), lambda g: (g, side)),
                pl.BlockSpec((span, BLOCK), lambda g: (g, side)),
                VMEM,
                VMEM,
                pl.BlockSpec((ROT, BLOCK), lambda g: (0, side)),
            ]
            + [VMEM] * len(early),
        )

    far_out = shape((BLOCK, width + 2 * part), BF)
    def matrix(item, order, count):
        near, far = item.pair()
        each = 2 * near.rows // len(order)
        views = [(view.start, view.rows) for view in (near, far)]
        return run(
            functools.partial(matrix_kernel, order, *views),
            (shape((2 * near.rows // count, width), F32),) * count + (shape((8, 128), F32),),
            (near.array, far.array),
            [
                pltpu.VMEM((len(order), each, width), F32),
                pltpu.SemaphoreType.DMA((len(order),)),
            ],
            name="matrix",
            out_specs=(HBM,) * count + (VMEM,),
        )[:count]

    keep_a, send_a, n1a, early_up, early_dn, early_sums = run(
        functools.partial(mlp_kernel, None, False),
        (
            chunk_out,
            chunk_out,
            n1c_out,
            shape((hidden, width), F32),
            shape((hidden, width), F32),
            sums_out,
        ),
        (both_0, bulk_1, up_weight, down_weight, up_bias, vec),
        mlp_scratch,
        limit=24,
        name="mlp_near",
        time=0,
    )
    back_a = swap(send_a, "fsdp", 1)
    kv_near = join_all(sequence, *kv_parts)
    kv_parts = [kv_near, swap(kv_near, "seq", sbits[0])]
    task = (join_step, [View(qo_2, 0, part)], 1), (join_step, [View(qo_2, part, part)], 1)
    views = sequence.stage(task)
    qo_3 = [swap(views[t, 0].array, "fsdp", 1) for t in range(2)]
    qt, do_t, wq, wo = run(
        functools.partial(query_kernel, rels),
        (
            shape((width, rows), BF),
            shape((width, rows), BF),
            shape((width, width), BF),
            shape((width, width), BF),
        ),
        (n1, both_0, vec, cs, qo_0, qo_2, bulk_1, *qo_3),
        name="query",
    )

    own, far_0, near, dkv = attend(
        0,
        (),
        (
            shape((BLOCK, width), BF),
            far_out,
            shape((BLOCK, width + part), BF),
            shape((slots * BLOCK, 2 * HDIM), F32),
        ),
    )
    z2 = [swap(far_0, "fsdp", 2)]
    both_3 = swap(join_all(sequence, both_2), "fsdp", 1)
    keep_b, send_b, n1b, upk, ups, dnk, dns, sums = run(
        functools.partial(mlp_kernel, seq_orders, True),
        (chunk_out, chunk_out, n1c_out)
        + (shape((hidden // 2, width), BF),) * 4
        + (sums_out,),
        (both_2, both_3, up_weight, down_weight, up_bias, vec, early_up, early_dn, early_sums),
        mlp_scratch + [pltpu.VMEM((hidden, width), F32)] * 2,
        limit=28,
        name="mlp_far",
        time=14,
        after=(back_a,),
    )
    up = Sum(upk, ups, up_bits, others(up_bits))
    dn = Sum(dnk, dns, dn_bits, others(dn_bits))
    own, far_1, z_near, dkv_near, dkv_far = attend(
        1,
        (own, near, dkv),
        (shape((rows, width), BF), far_out, shape((rows, width + part), BF))
        + (shape((seqs * BLOCK, 2 * HDIM), BF),) * 2,
    )
    z2.append(swap(far_1, "fsdp", 2))
    dkv = Reduce(dkv_near, dkv_far, sbits)
    z1 = swap(z_near, "fsdp", 1)
    flow(sequence, up, dn)
    z2, relay_z = run(
        functools.partial(relay_kernel, part),
        (shape((rows, width + part), BF),) * 2,
        z2,
        name="relay",
    )
    z3 = swap(relay_z, "fsdp", 1)
    flow(sequence, dkv)
    flow(sequence, up)
    qo_bits = sbits[:2]
    qo_order = shard_order(qo_bits)
    qok, qos = run(
        functools.partial(weight_kernel, qo_order),
        (shape((part, width), BF),) * 2,
        (n1a, n1b, own, z_near, z1, z2, z3, both_0, bulk_1, both_2, both_3),
        [pltpu.VMEM((2 * part, width), F32)],
        name="weight",
    )
    qo = Sum(qok, qos, qo_bits, others(qo_bits), small=True)
    while dkv.left():
        flow(sequence, dkv)
    flow(sequence, dn)
    mixed = shape((48 * fsdp // 2, width), BF)
    dn1, near_t, far_t = run(
        functools.partial(tail_kernel, rels),
        (shape((rows, width), F32), mixed, mixed),
        (both_0, n1, z_near, wq, wkv, vec, cs, *[v.array for v in dkv.pair()], sums),
        [pltpu.VMEM((fsdp, 2 * HDIM + 8, part), F32)],
        name="tail",
    )
    mix = Mix(near_t, far_t, fbits, [sbits[1], sbits[0], sbits[2]] + sbits[3:])
    while up.left() > 2:
        flow(sequence, up)
    flow(sequence, up)
    flow(sequence, qo)
    flow(sequence, mix)
    flow(sequence, qo, up)
    flow(sequence, mix)
    back_b = swap(send_b, "fsdp", 1)
    back = sequence.stage([(merge_step, [View(keep_b), View(back_b)], 1)])[0, 0].array
    back = swap(back, "fsdp", 2)
    flow(sequence, mix)
    while dn.left() > 2:
        flow(sequence, dn)
    flow(sequence, dn)
    flow(sequence, qo)
    while mix.left() > 1:
        flow(sequence, mix)
    flow(sequence, mix)
    while qo.left() > 1:
        flow(sequence, qo)
    flow(sequence, qo)
    flow(sequence, dn)
    layer_out, grad_tokens, _ = run(
        output_kernel,
        (shape((rows, width), BF),) * 2 + (shape((8, 128), F32),),
        (both_0, own, wo, vec, dn1, keep_a, back_a, back),
        name="output",
    )
    (grad_up,) = matrix(up, seq_orders[0], 1)
    vector = shape((part,), F32)
    g1, b1, qb, kb, vb, ob, g2, b2, ub, db, wk, wv = run(
        functools.partial(vector_kernel, *[v.start for v in mix.pair()]),
        (
            vector,
            vector,
            vector,
            shape(key_bias.shape, F32),
            shape(value_bias.shape, F32),
            vector,
            vector,
            vector,
            shape((hidden,), F32),
            vector,
            shape((HDIM, part), F32),
            shape((HDIM, part), F32),
        ),
        tuple(v.array for v in mix.pair()),
        limit=16,
        name="vector",
    )
    grad_query, grad_out = matrix(qo, qo_order, 2)
    (grad_down,) = matrix(dn, seq_orders[1], 1)
    return (
        layer_out.reshape(1, rows, width),
        grad_tokens.reshape(1, rows, width),
        g1,
        b1,
        grad_query,
        qb,
        wk.T,
        kb,
        wv.T,
        vb,
        grad_out,
        ob,
        g2,
        b2,
        grad_up,
        ub,
        grad_down,
        db,
    )


def solution(mesh):
    split = P("fsdp")
    matrix = P("fsdp", None)
    stream = P("fsdp", "seq", None)
    return jax.shard_map(
        on_device,
        mesh=mesh,
        in_specs=(
            stream,
            P(),
            matrix,
            split,
            split,
            matrix,
            split,
            matrix,
            split,
            matrix,
            split,
            matrix,
            split,
            split,
            split,
            matrix,
            split,
            matrix,
            split,
            stream,
        ),
        out_specs=(
            stream,
            stream,
            split,
            split,
            matrix,
            split,
            matrix,
            split,
            matrix,
            split,
            matrix,
            split,
            split,
            split,
            matrix,
            split,
            matrix,
            split,
        ),
        check_vma=False,
    )
```

```python
import functools

import jax
import jax.numpy as jnp
from jax import lax
from jax.experimental import pallas as pl
from jax.experimental.pallas import tpu as pltpu
from jax.sharding import PartitionSpec as P

HEADS = 12
HDIM = 64
ROT = 16
HALF = ROT // 2
BLOCK = 128

NEGATIVE = -1e30
EPSILON = 1e-05
SQRT_HALF = 0.7071067811865476
GAUSS_FACTOR = 0.3989422804014327
SCALE = HDIM ** (-0.5)
BF = jnp.bfloat16
F32 = jnp.float32
MIB = 1024 * 1024
VMEM = pl.BlockSpec(memory_space=pltpu.VMEM)
SMEM = pl.BlockSpec(memory_space=pltpu.SMEM)
ANY = pl.BlockSpec(memory_space=pl.ANY)
HBM = pl.BlockSpec(memory_space=pltpu.HBM)

NN = (((1,), (0,)), ((), ()))
NT = (((1,), (1,)), ((), ()))
TN = (((0,), (0,)), ((), ()))


def dot(left, right, dims=NN):
    return lax.dot_general(left, right, dims, preferred_element_type=F32)


def shape(dims, dtype):
    return jax.ShapeDtypeStruct(dims, dtype)


def params(limit=48):
    return pltpu.CompilerParams(vmem_limit_bytes=limit * MIB)


def micros(time):
    return pl.CostEstimate(flops=max(1, time * 1000000000), bytes_accessed=1000, transcendentals=0)


class Sequence:
    def __init__(self):
        self.last = ()

    def run(self, kernel, outs, ins, scratch=(), limit=16, name=None, after=(), time=0, token=True, **specs):
        single = isinstance(outs, jax.ShapeDtypeStruct)
        self.last = self.last + tuple(after)
        count, extra = len(ins), len(self.last)

        def body(*refs):
            kernel(*refs[:count], *refs[count + extra :])

        results = pl.pallas_call(
            body,
            out_shape=outs,
            in_specs=list(specs.get("in_specs", [VMEM] * count)) + [ANY] * extra,
            out_specs=specs.get("out_specs", VMEM if single else (VMEM,) * len(outs)),
            grid=specs.get("grid", ()),
            scratch_shapes=list(scratch),
            compiler_params=params(limit),
            cost_estimate=micros(time),
            name=name,
        )(*ins, *self.last)
        if token:
            self.last = (min((results,) if single else results, key=lambda v: v.size),)
        return results

    def stage(self, tasks, bundles=(), after=()):
        bundles = [list(bundle) for bundle in bundles]
        placed = {key for bundle in bundles for key in bundle}
        for t, (_, _, parts) in enumerate(tasks):
            bundles += [[(t, p)] for p in range(parts) if (t, p) not in placed]
        sizes = {}
        for t, (kind, views, parts) in enumerate(tasks):
            rows = sum(v.rows for v in views) if kind is join_step else views[0].rows
            for p in range(parts):
                sizes[t, p] = rows // parts
        ins, outs, spots = [], [], {}
        for index, bundle in enumerate(bundles):
            start = 0
            for key in bundle:
                spots[key] = (index, start, sizes[key])
                start += sizes[key]
            like = tasks[bundle[0][0]][1][0].array
            outs.append(shape((start,) + like.shape[1:], BF))
        plan = []
        for t, (kind, views, parts) in enumerate(tasks):
            sources = []
            for view in views:
                at = next((i for i, v in enumerate(ins) if v is view.array), len(ins))
                if at == len(ins):
                    ins.append(view.array)
                sources.append((at, view.start, view.rows))
            plan.append((kind, sources, [spots[t, p] for p in range(parts)]))

        def kernel(*refs):
            def pieces(found, offset):
                return [refs[offset + i].at[start : start + size] for i, start, size in found]

            for kind, sources, targets in plan:
                kind(pieces(sources, 0), pieces(targets, len(ins)))

        results = self.run(kernel, tuple(outs), ins, name="stage", after=after)
        return {key: View(results[i], start, rows) for key, (i, start, rows) in spots.items()}


class View:
    def __init__(self, array, start=0, rows=None):
        self.array, self.start = array, start
        self.rows = array.shape[0] if rows is None else rows


class Sum:
    def __init__(self, near, far, bits, rest, small=False):
        self.small = small
        self.near, self.coming = View(near), View(swap(far, "seq", bits[0]))
        plan = [(bit, 2) for bit in bits[1:]] + [(bit, 1) for bit in rest]
        plan += [(bits[-1], 1)] + [(bit, -1) for bit in reversed(bits[:-1])]
        self.plan = [("seq", bit, parts) for bit, parts in plan]

    def left(self):
        return len(self.plan)

    def task(self):
        parts = self.plan[0][2]
        if parts == -1:
            return (join_step, [self.near, self.coming], 1)
        return (merge_step, [self.near, self.coming], parts)

    def pair(self):
        return (self.near, self.coming)


class Reduce(Sum):
    def __init__(self, near, far, bits):
        Sum.__init__(self, near, far, bits, [])
        self.plan = self.plan[: len(bits) - 1]


class Mix(Sum):
    def __init__(self, near, far, fbits, sbits):
        self.small = True
        self.near, self.coming = View(near), View(swap(far, "fsdp", fbits[0]))
        self.plan = [("fsdp", bit, 2) for bit in fbits[1:]] + [("seq", bit, 1) for bit in sbits]

    def task(self):
        return (mix_step, [self.near, self.coming], self.plan[0][2])


def join_all(sequence, *arrays, after=()):
    task = (join_step, [View(v) for v in arrays], 1)
    return sequence.stage([task], after=after)[0, 0].array


def flow(sequence, *items, extra=(), after=(), together=False):
    tasks = [item.task() for item in items] + list(extra)
    groups = {}
    for t, item in enumerate(items):
        axis, bit, _ = item.plan[0]
        key = (axis, bit, 0 if item.small or together else 1 + t)
        groups.setdefault(key, []).append((t, tasks[t][2] - 1))
    views = sequence.stage(tasks, groups.values(), after)
    for (axis, bit, _), keys in groups.items():
        sent = swap(views[keys[0]].array, axis, bit)
        for t, part in keys:
            view = views[t, part]
            items[t].near = views[t, 0]
            items[t].coming = View(sent, view.start, view.rows)
            items[t].plan.pop(0)
    return [views[len(items) + i, 0].array for i in range(len(extra))]


def swap(value, axis, bit):
    size = lax.axis_size(axis)
    return lax.ppermute(value, axis, [(i, i ^ bit) for i in range(size)])


def bits_of(size):
    return [1 << i for i in range(size.bit_length() - 1)]


def normalize(values):
    center = values - jnp.mean(values, -1, keepdims=True)
    inverse_std = lax.rsqrt(jnp.mean(center * center, -1, keepdims=True) + EPSILON)
    return (center * inverse_std, inverse_std)


def pick(pieces, index):
    result = pieces[-1]
    for i in range(len(pieces) - 2, -1, -1):
        result = jnp.where(index == i, pieces[i], result)
    return result


def rel_order(size):
    order = [0]
    for bit in reversed(bits_of(size)):
        order = order + [r ^ bit for r in order]
    return order


def pack_kernel(*refs):
    count = len(refs) // 2
    pack_ref, both_ref, qo_ref, bulk_ref = refs[count : count + 4]
    sems = refs[-1]
    rows, part = refs[0].shape[0], refs[2].shape[0]
    held = (both_ref.at[:rows], both_ref.at[rows:], qo_ref.at[:part], qo_ref.at[part:])
    held += refs[count + 4 : -1]
    start = 0
    pairs = [(refs[i], held[i]) for i in range(count)]
    for ref in refs[:4]:
        size = ref.shape[0]
        pairs.append((ref, bulk_ref.at[start : start + size]))
        start += size
    copies = [pltpu.make_async_copy(*pair, sems.at[i]) for i, pair in enumerate(pairs)]
    for copy in copies:
        copy.start()
    for copy in copies:
        copy.wait()
    g1, b1, g2, b2, qb, ob, db, kb, vb, wk_ref, wv_ref = held[4:]
    small = jnp.concatenate(
        [
            kb[...].astype(F32).reshape(1, kb.shape[0]),
            vb[...].astype(F32).reshape(1, vb.shape[0]),
            jnp.zeros((1, part - kb.shape[0] - vb.shape[0]), F32),
        ],
        axis=1,
    )
    lines = [ref[...].astype(F32).reshape(1, part) for ref in (g1, b1, g2, b2, qb, ob, db)]
    lines = jnp.concatenate(lines + [small, jnp.zeros((8, part), F32)], axis=0)
    pack_ref[:HDIM] = wk_ref[...]
    pack_ref[HDIM : 2 * HDIM] = wv_ref[...]
    pack_ref[2 * HDIM :] = lines.astype(BF)


def table_kernel(cosine, sine, out):
    out[:HALF] = cosine[...]
    out[HALF:] = sine[...]


def front_kernel(rels, x_ref, *refs):
    count = len(rels)
    packs = refs[:count]
    cs_ref, n1_ref, kv_ref, vec_ref, wkv_ref, pieces, weights = refs[count:]
    me = lax.axis_index("fsdp")
    for rel, pack in zip(rels, packs):
        weights[rel ^ me] = pack[: 2 * HDIM, :]
        pieces[rel ^ me] = pack[2 * HDIM :, :].astype(F32)
    wkv = jnp.concatenate([weights[p] for p in range(count)], axis=1)
    wkv_ref[...] = wkv
    vec = jnp.concatenate([pieces[p] for p in range(count)], axis=1)
    vec_ref[...] = vec
    normal, _ = normalize(x_ref[...].astype(F32))
    n1 = (normal * vec[0:1] + vec[1:2]).astype(BF)
    n1_ref[...] = n1
    key_part, value_part = ROT // count, HDIM // count
    key_bias = jnp.concatenate([pieces[p][7:8, :key_part] for p in range(count)], axis=1)
    value_bias = jnp.concatenate(
        [pieces[p][7:8, key_part : key_part + value_part] for p in range(count)], axis=1
    )
    bias = jnp.concatenate([key_bias, jnp.zeros((1, HDIM - ROT), F32), value_bias], axis=1)
    turned = (dot(n1, wkv, NT) + bias).T
    cosine, sine = cs_ref[:HALF], cs_ref[HALF:]
    first, second = turned[:HALF], turned[HALF:ROT]
    turned = jnp.concatenate(
        [first * cosine - second * sine, second * cosine + first * sine, turned[ROT:]], axis=0
    )
    kv_ref[...] = turned.T.astype(BF)


def query_kernel(rels, n1_ref, both_ref, vec_ref, cs_ref, *refs):
    count = len(rels) - 1
    part = refs[0].shape[0] // 2
    tops = [pack.shape[0] - 2 * part for pack in refs[:count]]
    pairs = [
        (pack.at[top : top + part], pack.at[top + part : top + 2 * part])
        for pack, top in zip(refs[:count], tops)
    ]
    pairs.append(refs[count : count + 2])
    qt_ref, dot_ref, wq_ref, wo_ref = refs[count + 2 :]
    me = lax.axis_index("fsdp")
    for rel, (near, far) in zip(rels, pairs):
        start = pl.multiple_of((rel ^ me) * part, part)
        wq_ref[pl.ds(start, part), :] = near[...]
        wo_ref[pl.ds(start, part), :] = far[...]
    turned = (dot(n1_ref[...], wq_ref[...]) + vec_ref[4:5]).T
    cosine, sine = cs_ref[:HALF], cs_ref[HALF:]
    for h in range(HEADS):
        base = h * HDIM
        first, second = turned[base : base + HALF], turned[base + HALF : base + ROT]
        head = jnp.concatenate(
            [
                first * cosine - second * sine,
                second * cosine + first * sine,
                turned[base + ROT : base + HDIM],
            ],
            axis=0,
        )
        qt_ref[base : base + HDIM, :] = (head.astype(BF).astype(F32) * SCALE).astype(BF)
    dy = both_ref[n1_ref.shape[0] :]
    dot_ref[...] = dot(dy, wo_ref[...], NT).T.astype(BF)


def mlp_kernel(seq_orders, last, *refs):
    both, refs = refs[:2], refs[2:]
    if last:
        up_ref, down_ref, ub_ref, vec_ref, early_up, early_dn, early_sums = refs[:7]
        keep_ref, send_ref, n1c_ref, upk_ref, ups_ref, dnk_ref, dns_ref, sums_ref = refs[7:15]
        normal_s, n2_s, dy_s, acc_up, acc_dn = refs[15:]
    else:
        up_ref, down_ref, ub_ref, vec_ref = refs[:4]
        keep_ref, send_ref, n1c_ref, acc_up, acc_dn, sums_ref = refs[4:10]
        normal_s, n2_s, dy_s = refs[10:]
    me = lax.axis_index("fsdp")
    seq_me = lax.axis_index("seq")
    hidden, width = up_ref.shape
    part = n1c_ref.shape[2]
    rows = n1c_ref.shape[1]
    for i in range(2):
        here = slice(i * rows, (i + 1) * rows)
        x, dy = both[i][:rows], both[i][rows : 2 * rows]
        dy_s[here] = dy
        normal, _ = normalize(x.astype(F32))
        normal_s[here] = normal
        n1 = normal * vec_ref[0:1] + vec_ref[1:2]
        n1c_ref[i] = pick(
            [n1[:, p * part : (p + 1) * part] for p in range(width // part)], me
        ).astype(BF)
        n2_s[here] = (normal * vec_ref[2:3] + vec_ref[3:4]).astype(BF)
    n2, dy = n2_s[...], dy_s[...]
    out = None
    dn2 = None
    tile = 256
    bias = ub_ref[...].astype(F32).reshape(1, hidden)
    sums = []
    for c in range(hidden // tile):
        here = slice(c * tile, (c + 1) * tile)
        up_c, down_c = up_ref[here, :], down_ref[here, :]
        u = dot(n2, up_c, NT) + bias[:, here]
        dg = dot(dy, down_c, NT)
        phi = 0.5 * (1.0 + lax.erf(u * SQRT_HALF))
        g = (u * phi).astype(BF)
        du = (dg * (phi + u * jnp.exp(-0.5 * u * u) * GAUSS_FACTOR)).astype(BF)
        out_c = dot(g, down_c)
        dn2_c = dot(du, up_c)
        out = out_c if out is None else out + out_c
        dn2 = dn2_c if dn2 is None else dn2 + dn2_c
        grad_down, grad_up = dot(g, dy, TN), dot(du, n2, TN)
        if last:
            grad_down, grad_up = grad_down + early_dn[here, :], grad_up + early_up[here, :]
        acc_dn[here, :] = grad_down
        acc_up[here, :] = grad_up
        sums.append(jnp.sum(du.astype(F32), axis=0, keepdims=True))
    lines = [
        jnp.sum(dn2 * normal_s[...], axis=0, keepdims=True),
        jnp.sum(dn2, axis=0, keepdims=True),
        jnp.concatenate(sums, axis=1),
    ]
    for i, line in enumerate(lines):
        size = line.shape[1]
        if last:
            line = line + early_sums[i : i + 1, :size]
        sums_ref[i : i + 1, :size] = line
    for i, target in enumerate((keep_ref, send_ref)):
        here = slice(i * rows, (i + 1) * rows)
        target[0] = out[here].astype(BF)
        target[1] = (dn2[here] * vec_ref[2:3]).astype(BF)
    if last:
        spread_shards(acc_up, seq_orders[0], seq_me, upk_ref, ups_ref)
        spread_shards(acc_dn, seq_orders[1], seq_me, dnk_ref, dns_ref)


def attend_kernel(kv_bits, dkv_bits, side, per_group, chunk_blocks, most, order_ref, len_ref, *refs):
    qt_ref, dot_ref, *kv_refs, cs_ref = refs[:5]
    refs = refs[5:]
    if side == 1:
        early, refs = refs[:3], refs[3:]
    else:
        early = ()
    count = 4 if side == 0 else 5
    attend_side(
        (kv_bits, dkv_bits),
        side,
        per_group,
        chunk_blocks,
        most,
        order_ref,
        len_ref,
        qt_ref,
        dot_ref,
        kv_refs,
        cs_ref,
        early,
        refs[:count],
        *refs[count:],
    )


def attend_side(
    orders,
    side,
    per_group,
    chunk_blocks,
    most,
    order_ref,
    len_ref,
    qt_ref,
    dot_ref,
    kv_refs,
    cs_ref,
    early,
    outs_refs,
    s_scr,
    p_scr,
    pb_scr,
    ds_scr,
    bias_scr,
    kv_scr,
    kvt_scr,
    dkv_scr,
    qs,
    dos,
    ot,
    dqt,
    inverse,
):
    group = pl.program_id(0)
    o_ref, far_ref, near_ref = outs_refs[:3]
    seq_me = lax.axis_index("seq")
    half = held = kv_refs[0].shape[0]
    slots = 2 * held // BLOCK
    chunk = chunk_blocks * BLOCK
    lanes = per_group * BLOCK
    @pl.when(group == 0)
    def _():
        if side == 0:
            dkv_scr[...] = jnp.zeros_like(dkv_scr)
        else:
            dkv_scr[...] = early[2][...]
            for source, target in zip(early[:2], (o_ref, near_ref)):
                target[:BLOCK] = source[...]

        @pl.loop(0, slots)
        def _(i):
            rel = (i // 2) ^ seq_me
            for at, bits in enumerate(orders):
                place = jnp.int32(0)
                for bit in bits:
                    place = place * 2 + (rel // bit) % 2
                inverse[at, order_ref[i]] = place * 2 + i % 2

    block = order_ref[2 * seq_me + side]
    base = block * BLOCK
    end_1 = len_ref[0, 0]
    end_2 = end_1 + len_ref[0, 1]
    end_3 = end_2 + len_ref[0, 2]

    def start_of(position):
        low = jnp.where(position >= end_1, end_1, 0)
        low = jnp.where(position >= end_2, end_2, low)
        return jnp.where(position >= end_3, end_3, low)

    q_pos = base + lax.broadcasted_iota(jnp.int32, (1, BLOCK), 1)
    q_start = start_of(q_pos)
    low_block = jnp.maximum(start_of(base) // BLOCK, block - (most - 1))
    chunks = (block - low_block + chunk_blocks) // chunk_blocks

    def slot_of(j, at):
        return inverse[at, jnp.minimum(low_block + j, block)]

    @pl.loop(0, chunks * chunk_blocks)
    def _(j):
        start = slot_of(j, 0) * BLOCK
        here = pl.ds(pl.multiple_of(j * BLOCK, BLOCK), BLOCK)
        for i, kv_ref in enumerate(kv_refs):

            @pl.when(start // held == i)
            def _():
                there = pl.multiple_of(start - i * held, BLOCK)
                kv_scr[here, :] = kv_ref[pl.ds(there, BLOCK), :]

    for h in range(per_group):
        cols = slice(h * BLOCK, (h + 1) * BLOCK)
        qs[:, cols] = qt_ref[h * HDIM : (h + 1) * HDIM, :]
        dos[:, cols] = dot_ref[h * HDIM : (h + 1) * HDIM, :]

    pairs = per_group // 2

    def columns(h):
        return slice(h * BLOCK, (h + 1) * BLOCK)

    def score_step(c, top):
        keys = kv_scr[pl.ds(c * chunk, chunk), :HDIM]
        k_pos = (low_block + c * chunk_blocks) * BLOCK + lax.broadcasted_iota(
            jnp.int32, (chunk, BLOCK), 0
        )
        allowed = jnp.logical_and(k_pos <= q_pos, k_pos >= q_start)
        bias_scr[c] = jnp.where(allowed, 0.0, NEGATIVE)
        tops = []
        for pair in range(pairs):
            s = dot(keys, qs[:, pair * 2 * BLOCK : (pair + 1) * 2 * BLOCK])
            for half_at in range(2):
                part = s[:, columns(half_at)] + bias_scr[c]
                s_scr[c, :, columns(2 * pair + half_at)] = part
                tops.append(jnp.max(part, axis=0, keepdims=True))
        return jnp.maximum(top, jnp.concatenate(tops, axis=1))

    top = lax.fori_loop(0, chunks, score_step, jnp.full((1, lanes), NEGATIVE, F32))

    def weight_step(c, carry):
        total, delta = carry
        totals, deltas = [], []
        values = kv_scr[pl.ds(c * chunk, chunk), HDIM:]
        for pair in range(pairs):
            dp = dot(values, dos[:, pair * 2 * BLOCK : (pair + 1) * 2 * BLOCK])
            for half_at in range(2):
                cols = columns(2 * pair + half_at)
                part = dp[:, columns(half_at)]
                p_scr[c, :, cols] = part
                e = jnp.exp(s_scr[c, :, cols] - top[:, cols])
                s_scr[c, :, cols] = e
                totals.append(jnp.sum(e, axis=0, keepdims=True))
                deltas.append(jnp.sum(e * part, axis=0, keepdims=True))
        return (
            total + jnp.concatenate(totals, axis=1),
            delta + jnp.concatenate(deltas, axis=1),
        )

    zero = jnp.zeros((1, lanes), F32)
    total, delta = lax.fori_loop(0, chunks, weight_step, (zero, zero))
    shrink = 1.0 / total
    delta = delta * shrink
    ot[...] = jnp.zeros_like(ot)
    dqt[...] = jnp.zeros_like(dqt)

    def grad_step(c, _):
        kvt = kvt_scr[c]
        for pair in range(pairs):
            both = slice(pair * 2 * BLOCK, (pair + 1) * 2 * BLOCK)
            for half_at in range(2):
                cols = columns(2 * pair + half_at)
                p = s_scr[c, :, cols] * shrink[:, cols]
                pb_scr[:, cols] = p.astype(BF)
                ds_scr[:, cols] = (p * (p_scr[c, :, cols] - delta[:, cols])).astype(BF)
            ot[:, both] += dot(kvt[HDIM:], pb_scr[:, both])
            dqt[:, both] += dot(kvt[:HDIM], ds_scr[:, both])
        dk = dot(ds_scr[...], qs[...], NT)
        dv = dot(pb_scr[...], dos[...], NT)
        both = jnp.concatenate([dk, dv], axis=1)
        for b in range(chunk_blocks):

            @pl.when(low_block + c * chunk_blocks + b <= block)
            def _():
                place = slot_of(c * chunk_blocks + b, 1) * BLOCK
                dkv_scr[pl.ds(pl.multiple_of(place, BLOCK), BLOCK), :] += both[
                    b * BLOCK : (b + 1) * BLOCK
                ]

        return 0

    @pl.loop(0, chunks)
    def _(c):
        kvt_scr[c] = kv_scr[pl.ds(c * chunk, chunk), :].astype(F32).T.astype(BF)

    lax.fori_loop(0, chunks, grad_step, 0)
    cosine, sine = cs_ref[:HALF], cs_ref[HALF:]
    outs, grads = [], []
    for h in range(per_group):
        cols = slice(h * BLOCK, (h + 1) * BLOCK)
        outs.append(ot[:, cols])
        grad = dqt[:, cols] * SCALE
        first, second = grad[:HALF], grad[HALF:ROT]
        grads.append(first * cosine + second * sine)
        grads.append(second * cosine - first * sine)
        grads.append(grad[ROT:])
    width = o_ref.shape[1]
    here = slice(side * BLOCK, (side + 1) * BLOCK)
    span = per_group * HDIM
    across = pl.ds(0 if span == width else pl.multiple_of(group * span, span), span)
    o_ref[here, across] = jnp.concatenate(outs, axis=0).T.astype(BF)
    grad = jnp.concatenate(grads, axis=0).T.astype(BF)
    far_ref[:, across] = grad
    near_ref[here, across] = grad

    @pl.when(group == pl.num_programs(0) - 1)
    def _():
        me = lax.axis_index("fsdp")
        part = near_ref.shape[1] - width
        count = width // part
        o = o_ref[here, :].astype(F32)
        pieces = [o[:, p * part : (p + 1) * part] for p in range(count)]
        near_ref[here, width:] = pick(pieces, me ^ 1).astype(BF)
        far_ref[:, width:] = jnp.concatenate(
            [pick(pieces, me ^ 2), pick(pieces, me ^ 3)], axis=1
        ).astype(BF)

        if side == 0:
            outs_refs[3][...] = dkv_scr[...]
        else:
            outs_refs[3][...] = dkv_scr[:half].astype(BF)
            outs_refs[4][...] = dkv_scr[half:].astype(BF)


def output_kernel(both_ref, o_ref, wo_ref, vec_ref, dn1_ref, a_ref, b_ref, c_ref, *outs):
    layer_ref, grad_ref, mark = outs
    mark[...] = jnp.zeros_like(mark)
    rows = o_ref.shape[0]
    x, dy = both_ref[:rows].astype(F32), both_ref[rows:].astype(F32)
    mlp = a_ref[0].astype(F32) + b_ref[0].astype(F32) + c_ref[0].astype(F32)
    attention = dot(o_ref[...], wo_ref[...]) + vec_ref[5:6]
    layer_ref[...] = (x + attention + mlp + vec_ref[6:7]).astype(BF)
    normal, inverse_std = normalize(x)
    total = a_ref[1].astype(F32) + b_ref[1].astype(F32) + c_ref[1].astype(F32)
    total = total + dn1_ref[...] * vec_ref[0:1]
    grad_ref[...] = (
        dy
        + inverse_std
        * (
            total
            - jnp.mean(total, -1, keepdims=True)
            - normal * jnp.mean(total * normal, -1, keepdims=True)
        )
    ).astype(BF)


def shard_at(order, m, seq_me):
    return (order[m] ^ seq_me) & order[-1]


def spread_shards(source, order, seq_me, near, far):
    shards = len(order)
    rows = source.shape[0] // shards
    half = shards // 2
    for m in range(shards):
        start = pl.multiple_of(shard_at(order, m, seq_me) * rows, rows)
        target = near if m < half else far
        target[(m % half) * rows : (m % half + 1) * rows, :] = source[pl.ds(start, rows), :].astype(
            BF
        )


def weight_kernel(order, n1a_ref, n1b_ref, o_ref, own_ref, z1_ref, z2_ref, z3_ref, *refs):
    me = lax.axis_index("fsdp")
    rows, part = n1a_ref.shape[1:]
    dys = [ref.at[rows : 2 * rows] for ref in refs[:4]]
    near_ref, far_ref, grad = refs[4:]
    width = dys[0].shape[1]
    o = o_ref[...].astype(F32)
    own = pick([o[:, p * part : (p + 1) * part] for p in range(width // part)], me).astype(BF)
    items = (
        (n1a_ref[0], own_ref[:, :width], own, dys[0][...]),
        (n1a_ref[1], z1_ref[:, :width], z1_ref[:, width:], dys[1][...]),
        (n1b_ref[0], z2_ref[:, :width], z2_ref[:, width:], dys[2][...]),
        (n1b_ref[1], z3_ref[:, :width], z3_ref[:, width:], dys[3][...]),
    )
    grad_q = None
    grad_o = None
    for n1, dq, cols, dy in items:
        term_q, term_o = dot(n1, dq, TN), dot(cols, dy, TN)
        grad_q = term_q if grad_q is None else grad_q + term_q
        grad_o = term_o if grad_o is None else grad_o + term_o
    grad[:part] = grad_q
    grad[part:] = grad_o
    spread_shards(grad, order, lax.axis_index("seq"), near_ref, far_ref)


def tail_kernel(
    rels,
    both_ref,
    n1_ref,
    dq_ref,
    wq_ref,
    wkv_ref,
    vec_ref,
    cs_ref,
    dkvn_ref,
    dkvf_ref,
    sums_ref,
    dn1_ref,
    keep_ref,
    send_ref,
    vs,
):
    count = len(rels)
    me = lax.axis_index("fsdp")
    rows, width = n1_ref.shape
    part = width // count
    dkv = (dkvn_ref[...].astype(F32) + dkvf_ref[...].astype(F32)).T
    cosine, sine = cs_ref[:HALF], cs_ref[HALF:]
    first, second = dkv[:HALF], dkv[HALF:ROT]
    dkv = jnp.concatenate(
        [first * cosine + second * sine, second * cosine - first * sine, dkv[ROT:]], axis=0
    )
    dkv_sum = jnp.sum(dkv.astype(BF).T.astype(F32), axis=0, keepdims=True)
    dkv_t = dkv.astype(BF)
    dq = dq_ref[:, :width]
    dn1 = dot(dq, wq_ref[...], NT) + dot(dkv_t, wkv_ref[...], TN)
    dn1_ref[...] = dn1
    normal, _ = normalize(both_ref[:rows].astype(F32))
    dy = both_ref[rows:].astype(F32)
    grad_kv = dot(dkv_t, n1_ref[...])
    lines = jnp.concatenate(
        [
            jnp.sum(dn1 * normal, axis=0, keepdims=True),
            jnp.sum(dn1, axis=0, keepdims=True),
            sums_ref[0:1, :width],
            sums_ref[1:2, :width],
            jnp.sum(dq.astype(F32), axis=0, keepdims=True),
            jnp.sum(dy, axis=0, keepdims=True),
            jnp.concatenate(
                [jnp.concatenate([dkv_sum, jnp.zeros((1, part - 2 * HDIM), F32)], axis=1)] * count,
                axis=1,
            ),
            jnp.zeros((1, width), F32),
        ],
        axis=0,
    )
    for p in range(count):
        cols = slice(p * part, (p + 1) * part)
        vs[p, : 2 * HDIM, :] = grad_kv[:, cols]
        vs[p, 2 * HDIM :, :] = lines[:, cols]
    half = count // 2
    extra = sums_ref.shape[1] // part
    up_bias = jnp.concatenate(
        [sums_ref[2:3, e * part : (e + 1) * part] for e in range(extra)]
        + [jnp.zeros((8 - extra, part), F32)],
        axis=0,
    )
    size = keep_ref.shape[0] // half
    for m, rel in enumerate(rels):
        target = keep_ref if m < half else send_ref
        piece = vs[rel ^ me]
        last = up_bias if rel == 0 else jnp.zeros_like(up_bias)
        lines = jnp.concatenate([piece[2 * HDIM :], last], axis=0)
        target[(m % half) * size : (m % half + 1) * size] = join_split(
            fold(piece[: 2 * HDIM], count), fold(lines, count)
        )


def join_split(matrix, lines):
    high = lines.astype(BF).astype(F32)
    rest = jnp.zeros((8, matrix.shape[1]), F32)
    return jnp.concatenate([matrix, high, lines - high, rest], axis=0).astype(BF)


def load_split(value):
    value = value.astype(F32)
    return (value[:32], value[32:36] + value[36:40])


def fold(value, count):
    rows = value.shape[0] // count
    return jnp.concatenate([value[i * rows : (i + 1) * rows] for i in range(count)], axis=1)


def unfold(value, part):
    return jnp.concatenate(
        [value[:, i : i + part] for i in range(0, value.shape[1], part)], axis=0
    )


def mix_step(sources, targets):
    each = sources[0].shape[0] // len(targets)
    for i, target in enumerate(targets):
        here = slice(i * each, (i + 1) * each)
        first, second = load_split(sources[0][here]), load_split(sources[1][here])
        target[...] = join_split(first[0] + second[0], first[1] + second[1])


def merge_step(sources, targets):
    a_ref, b_ref = sources
    rows = a_ref.shape[0] // len(targets)
    for i, target in enumerate(targets):
        here = slice(i * rows, (i + 1) * rows)
        target[...] = (a_ref[here].astype(F32) + b_ref[here].astype(F32)).astype(BF)


def relay_kernel(part, first_ref, second_ref, own_ref, next_ref):
    width = own_ref.shape[1] - part
    for i, ref in enumerate((first_ref, second_ref)):
        here = slice(i * BLOCK, (i + 1) * BLOCK)
        own_ref[here] = ref[:, : width + part]
        next_ref[here, :width] = ref[:, :width]
        next_ref[here, width:] = ref[:, width + part :]


def join_step(sources, targets):
    rows = 0
    for source in sources:
        targets[0][rows : rows + source.shape[0]] = source[...]
        rows += source.shape[0]


def matrix_kernel(order, near_view, far_view, near_ref, far_ref, *refs):
    outs, (mark, held, sems) = refs[:-3], refs[-3:]
    mark[...] = jnp.zeros_like(mark)
    seq_me = lax.axis_index("seq")
    shards = len(order)
    half = shards // 2
    near_ref = near_ref.at[near_view[0] : near_view[0] + near_view[1]]
    far_ref = far_ref.at[far_view[0] : far_view[0] + far_view[1]]
    rows = near_ref.shape[0] // half
    each = shards // len(outs)
    copies = []
    for t in range(shards):
        place = jnp.int32(0)
        for m in range(shards):
            place = jnp.where(shard_at(order, m, seq_me) == t, m, place)
        start = pl.multiple_of((place & (half - 1)) * rows, rows)

        @pl.when(place < half)
        def _():
            held[t] = near_ref[pl.ds(start, rows), :].astype(F32)

        @pl.when(place >= half)
        def _():
            held[t] = far_ref[pl.ds(start, rows), :].astype(F32)

        first = (t % each) * rows
        copy = pltpu.make_async_copy(
            held.at[t], outs[t // each].at[first : first + rows, :], sems.at[t]
        )
        copy.start()
        copies.append(copy)
    for copy in copies:
        copy.wait()


def vector_kernel(a_at, b_at, a_ref, b_ref, g1, b1, qb, kb, vb, ob, g2, b2, ub, db, wk_ref, wv_ref):
    me = lax.axis_index("fsdp")
    first, second = load_split(a_ref[a_at : a_at + 48]), load_split(b_ref[b_at : b_at + 48])
    part = g1.shape[0]
    total = unfold(first[0] + second[0], part)
    lines = unfold(first[1] + second[1], part)
    wk_ref[...] = total[:HDIM]
    wv_ref[...] = total[HDIM:]
    for i, targets in enumerate(((g1,), (b1,), (g2,), (b2,), (qb,), (ob, db))):
        for target in targets:
            target[...] = lines[i : i + 1].reshape(part)
    kp, vp = kb.shape[0], vb.shape[0]
    line = lines[6:7]
    count = HDIM // vp
    kb[...] = pick([line[:, p * kp : (p + 1) * kp] for p in range(count)], me).reshape(kp)
    vb[...] = pick(
        [line[:, HDIM + p * vp : HDIM + (p + 1) * vp] for p in range(count)], me
    ).reshape(vp)
    extra = ub.shape[0] // part
    ub[...] = jnp.concatenate([lines[8 + e : 9 + e] for e in range(extra)], axis=1).reshape(
        ub.shape[0]
    )


def shard_count(rows, devices):
    shards = devices
    while shards > 2 and (rows % shards or (rows // shards) % 16):
        shards //= 2
    return shards


def shard_order(bits):
    order = [0]
    for bit in reversed(bits):
        order = order + [r ^ bit for r in order]
    return order


def on_device(
    tokens,
    block_order,
    doc_lengths,
    norm_one_gain,
    norm_one_bias,
    query_weight,
    query_bias,
    key_weight,
    key_bias,
    value_weight,
    value_bias,
    out_weight,
    out_bias,
    norm_two_gain,
    norm_two_bias,
    up_weight,
    up_bias,
    down_weight,
    down_bias,
    cotangent,
):
    _, rows, width = tokens.shape
    hidden = up_weight.shape[0]
    part = query_weight.shape[0]
    fsdp = lax.axis_size("fsdp")
    seqs = lax.axis_size("seq")
    slots = 2 * seqs
    fbits = bits_of(fsdp)
    sbits = bits_of(seqs)
    rels = rel_order(fsdp)
    fsdp_me = lax.axis_index("fsdp")
    seq_me = lax.axis_index("seq")
    x_own = tokens.reshape(rows, width)
    dy_own = cotangent.reshape(rows, width)

    def spread(value):
        parts = [value]
        for bit in reversed(fbits):
            parts = parts + [swap(v, "fsdp", bit) for v in parts]
        return parts

    pieces = (
        x_own,
        dy_own,
        query_weight,
        out_weight,
        norm_one_gain,
        norm_one_bias,
        norm_two_gain,
        norm_two_bias,
        query_bias,
        out_bias,
        down_bias,
        key_bias,
        value_bias,
        key_weight.T,
        value_weight.T,
    )
    sequence = Sequence()
    run = sequence.run
    pack, both_0, qo_0, bulk_0 = run(
        pack_kernel,
        (
            shape((2 * HDIM + 16, part), BF),
            shape((2 * rows, width), BF),
            shape((2 * part, width), BF),
            shape((2 * rows + 2 * part, width), BF),
        ),
        pieces,
        [pltpu.VMEM(v.shape, BF) for v in pieces[4:]] + [pltpu.SemaphoreType.DMA((len(pieces) + 4,))],
        limit=60,
        name="pack",
        time=2,
        in_specs=[HBM] * len(pieces),
    )
    packs = spread(pack)
    qo_2 = swap(qo_0, "fsdp", 2)
    both_2 = swap(both_0, "fsdp", 2)
    bulk_1 = swap(bulk_0, "fsdp", 1)

    own_blocks = lax.dynamic_slice_in_dim(block_order, 2 * seq_me, 2)
    offsets = jnp.arange(BLOCK, dtype=jnp.int32)
    own_pos = (own_blocks[:, None] * BLOCK + offsets[None, :]).reshape(rows)
    frequencies = 10000.0 ** (-2.0 * jnp.arange(HALF, dtype=F32) / ROT)
    angles = own_pos.astype(F32)[None, :] * frequencies[:, None]
    cs = run(
        table_kernel,
        shape((ROT, rows), F32),
        (jnp.cos(angles), jnp.sin(angles)),
        name="tables",
        time=5,
    )

    n1, kv_own, vec, wkv = run(
        functools.partial(front_kernel, rels),
        (
            shape((rows, width), BF),
            shape((rows, 2 * HDIM), BF),
            shape((16, width), F32),
            shape((2 * HDIM, width), BF),
        ),
        (x_own, *packs, cs),
        [pltpu.VMEM((fsdp, 16, part), F32), pltpu.VMEM((fsdp, 2 * HDIM, part), BF)],
        name="front",
        time=1,
    )

    kv = kv_own
    for bit in reversed(sbits[3:]):
        kv = join_all(sequence, kv, swap(kv, "seq", bit))
    kv_parts = [kv] + [swap(kv, "seq", bit) for bit in (sbits[2], sbits[1], sbits[1] + sbits[2])]
    kv_bits = sbits

    up_bits, dn_bits = sbits[:2], [sbits[1], sbits[0]]
    seq_orders = (shard_order(up_bits), shard_order(dn_bits))

    def others(bits):
        return sorted((b for b in sbits if b not in bits), key=lambda b: (b > sbits[2], -b))

    chunk_out = shape((2, rows, width), BF)
    n1c_out = shape((2, rows, part), BF)
    sums_out = shape((8, max(hidden, width)), F32)
    mlp_scratch = [
        pltpu.VMEM((2 * rows, width), F32),
        pltpu.VMEM((2 * rows, width), BF),
        pltpu.VMEM((2 * rows, width), BF),
    ]
    most = min(slots, slots // 2 + 1)
    chunk_blocks = 3
    most_chunks = -(-most // chunk_blocks)
    chunk = chunk_blocks * BLOCK
    per_group = HEADS
    while most_chunks * chunk * per_group * BLOCK * 8 > 20 * MIB and per_group > 2:
        per_group = {12: 6, 6: 4, 4: 2}[per_group]
    lanes = per_group * BLOCK
    span = per_group * HDIM
    def attend(side, early, outs):
        return run(
            functools.partial(attend_kernel, kv_bits, sbits, side, per_group, chunk_blocks, most),
            outs,
            (block_order, doc_lengths, qt, do_t, *kv_parts, cs, *early),
            [
                pltpu.VMEM((most_chunks, chunk, lanes), F32),
                pltpu.VMEM((most_chunks, chunk, lanes), F32),
                pltpu.VMEM((chunk, lanes), BF),
                pltpu.VMEM((chunk, lanes), BF),
                pltpu.VMEM((most_chunks, chunk, BLOCK), F32),
                pltpu.VMEM((most_chunks * chunk, 2 * HDIM), BF),
                pltpu.VMEM((most_chunks, 2 * HDIM, chunk), BF),
                pltpu.VMEM((slots * BLOCK, 2 * HDIM), F32),
                pltpu.VMEM((HDIM, lanes), BF),
                pltpu.VMEM((HDIM, lanes), BF),
                pltpu.VMEM((HDIM, lanes), F32),
                pltpu.VMEM((HDIM, lanes), F32),
                pltpu.SMEM((2, slots), jnp.int32),
            ],
            limit=36 if slots <= 16 else 60,
            name="attend",
            time=(2, 14)[side],
            grid=(HEADS // per_group,),
            in_specs=[
                SMEM,
                SMEM,
                pl.BlockSpec((span, BLOCK), lambda g: (g, side)),
                pl.BlockSpec((span, BLOCK), lambda g: (g, side)),
                VMEM,
                VMEM,
                pl.BlockSpec((ROT, BLOCK), lambda g: (0, side)),
            ]
            + [VMEM] * len(early),
        )

    far_out = shape((BLOCK, width + 2 * part), BF)
    def matrix(item, order, count):
        near, far = item.pair()
        each = 2 * near.rows // len(order)
        views = [(view.start, view.rows) for view in (near, far)]
        return run(
            functools.partial(matrix_kernel, order, *views),
            (shape((2 * near.rows // count, width), F32),) * count + (shape((8, 128), F32),),
            (near.array, far.array),
            [
                pltpu.VMEM((len(order), each, width), F32),
                pltpu.SemaphoreType.DMA((len(order),)),
            ],
            name="matrix",
            out_specs=(HBM,) * count + (VMEM,),
        )[:count]

    keep_a, send_a, n1a, early_up, early_dn, early_sums = run(
        functools.partial(mlp_kernel, None, False),
        (
            chunk_out,
            chunk_out,
            n1c_out,
            shape((hidden, width), F32),
            shape((hidden, width), F32),
            sums_out,
        ),
        (both_0, bulk_1, up_weight, down_weight, up_bias, vec),
        mlp_scratch,
        limit=24,
        name="mlp_near",
        time=0,
    )
    back_a = swap(send_a, "fsdp", 1)
    kv_near = join_all(sequence, *kv_parts)
    kv_parts = [kv_near, swap(kv_near, "seq", sbits[0])]
    task = (join_step, [View(qo_2, 0, part)], 1), (join_step, [View(qo_2, part, part)], 1)
    views = sequence.stage(task)
    qo_3 = [swap(views[t, 0].array, "fsdp", 1) for t in range(2)]
    qt, do_t, wq, wo = run(
        functools.partial(query_kernel, rels),
        (
            shape((width, rows), BF),
            shape((width, rows), BF),
            shape((width, width), BF),
            shape((width, width), BF),
        ),
        (n1, both_0, vec, cs, qo_0, qo_2, bulk_1, *qo_3),
        name="query",
    )

    own, far_0, near, dkv = attend(
        0,
        (),
        (
            shape((BLOCK, width), BF),
            far_out,
            shape((BLOCK, width + part), BF),
            shape((slots * BLOCK, 2 * HDIM), F32),
        ),
    )
    z2 = [swap(far_0, "fsdp", 2)]
    both_3 = swap(join_all(sequence, both_2), "fsdp", 1)
    keep_b, send_b, n1b, upk, ups, dnk, dns, sums = run(
        functools.partial(mlp_kernel, seq_orders, True),
        (chunk_out, chunk_out, n1c_out)
        + (shape((hidden // 2, width), BF),) * 4
        + (sums_out,),
        (both_2, both_3, up_weight, down_weight, up_bias, vec, early_up, early_dn, early_sums),
        mlp_scratch + [pltpu.VMEM((hidden, width), F32)] * 2,
        limit=28,
        name="mlp_far",
        time=14,
        after=(back_a,),
    )
    up = Sum(upk, ups, up_bits, others(up_bits))
    dn = Sum(dnk, dns, dn_bits, others(dn_bits))
    own, far_1, z_near, dkv_near, dkv_far = attend(
        1,
        (own, near, dkv),
        (shape((rows, width), BF), far_out, shape((rows, width + part), BF))
        + (shape((seqs * BLOCK, 2 * HDIM), BF),) * 2,
    )
    z2.append(swap(far_1, "fsdp", 2))
    dkv = Reduce(dkv_near, dkv_far, sbits)
    z1 = swap(z_near, "fsdp", 1)
    flow(sequence, up, dn)
    z2, relay_z = run(
        functools.partial(relay_kernel, part),
        (shape((rows, width + part), BF),) * 2,
        z2,
        name="relay",
    )
    z3 = swap(relay_z, "fsdp", 1)
    flow(sequence, dkv)
    flow(sequence, up)
    qo_bits = sbits[:2]
    qo_order = shard_order(qo_bits)
    qok, qos = run(
        functools.partial(weight_kernel, qo_order),
        (shape((part, width), BF),) * 2,
        (n1a, n1b, own, z_near, z1, z2, z3, both_0, bulk_1, both_2, both_3),
        [pltpu.VMEM((2 * part, width), F32)],
        name="weight",
    )
    qo = Sum(qok, qos, qo_bits, others(qo_bits), small=True)
    while dkv.left():
        flow(sequence, dkv)
    flow(sequence, dn)
    mixed = shape((48 * fsdp // 2, width), BF)
    dn1, near_t, far_t = run(
        functools.partial(tail_kernel, rels),
        (shape((rows, width), F32), mixed, mixed),
        (both_0, n1, z_near, wq, wkv, vec, cs, *[v.array for v in dkv.pair()], sums),
        [pltpu.VMEM((fsdp, 2 * HDIM + 8, part), F32)],
        name="tail",
    )
    mix = Mix(near_t, far_t, fbits, [sbits[1], sbits[0], sbits[2]] + sbits[3:])
    while up.left() > 2:
        flow(sequence, up)
    flow(sequence, up)
    flow(sequence, qo)
    flow(sequence, mix)
    flow(sequence, qo, up)
    flow(sequence, mix)
    flow(sequence, mix)
    while dn.left() > 2:
        flow(sequence, dn)
    flow(sequence, dn)
    back_b = swap(send_b, "fsdp", 1)
    back = sequence.stage([(merge_step, [View(keep_b), View(back_b)], 1)])[0, 0].array
    back = swap(back, "fsdp", 2)
    flow(sequence, qo)
    while mix.left() > 1:
        flow(sequence, mix)
    flow(sequence, mix)
    while qo.left() > 1:
        flow(sequence, qo)
    flow(sequence, qo)
    flow(sequence, dn)
    layer_out, grad_tokens, _ = run(
        output_kernel,
        (shape((rows, width), BF),) * 2 + (shape((8, 128), F32),),
        (both_0, own, wo, vec, dn1, keep_a, back_a, back),
        name="output",
    )
    (grad_up,) = matrix(up, seq_orders[0], 1)
    vector = shape((part,), F32)
    g1, b1, qb, kb, vb, ob, g2, b2, ub, db, wk, wv = run(
        functools.partial(vector_kernel, *[v.start for v in mix.pair()]),
        (
            vector,
            vector,
            vector,
            shape(key_bias.shape, F32),
            shape(value_bias.shape, F32),
            vector,
            vector,
            vector,
            shape((hidden,), F32),
            vector,
            shape((HDIM, part), F32),
            shape((HDIM, part), F32),
        ),
        tuple(v.array for v in mix.pair()),
        limit=16,
        name="vector",
    )
    grad_query, grad_out = matrix(qo, qo_order, 2)
    (grad_down,) = matrix(dn, seq_orders[1], 1)
    return (
        layer_out.reshape(1, rows, width),
        grad_tokens.reshape(1, rows, width),
        g1,
        b1,
        grad_query,
        qb,
        wk.T,
        kb,
        wv.T,
        vb,
        grad_out,
        ob,
        g2,
        b2,
        grad_up,
        ub,
        grad_down,
        db,
    )


def solution(mesh):
    split = P("fsdp")
    matrix = P("fsdp", None)
    stream = P("fsdp", "seq", None)
    return jax.shard_map(
        on_device,
        mesh=mesh,
        in_specs=(
            stream,
            P(),
            matrix,
            split,
            split,
            matrix,
            split,
            matrix,
            split,
            matrix,
            split,
            matrix,
            split,
            split,
            split,
            matrix,
            split,
            matrix,
            split,
            stream,
        ),
        out_specs=(
            stream,
            stream,
            split,
            split,
            matrix,
            split,
            matrix,
            split,
            matrix,
            split,
            matrix,
            split,
            split,
            split,
            matrix,
            split,
            matrix,
            split,
        ),
        check_vma=False,
    )
```

```python
import functools

import jax
import jax.numpy as jnp
from jax import lax
from jax.experimental import pallas as pl
from jax.experimental.pallas import tpu as pltpu
from jax.sharding import PartitionSpec as P

HEADS = 12
HDIM = 64
ROT = 16
HALF = ROT // 2
BLOCK = 128

NEGATIVE = -1e30
EPSILON = 1e-05
SQRT_HALF = 0.7071067811865476
GAUSS_FACTOR = 0.3989422804014327
SCALE = HDIM ** (-0.5)
BF = jnp.bfloat16
F32 = jnp.float32
MIB = 1024 * 1024
VMEM = pl.BlockSpec(memory_space=pltpu.VMEM)
SMEM = pl.BlockSpec(memory_space=pltpu.SMEM)
ANY = pl.BlockSpec(memory_space=pl.ANY)
HBM = pl.BlockSpec(memory_space=pltpu.HBM)

NN = (((1,), (0,)), ((), ()))
NT = (((1,), (1,)), ((), ()))
TN = (((0,), (0,)), ((), ()))


def dot(left, right, dims=NN):
    return lax.dot_general(left, right, dims, preferred_element_type=F32)


def shape(dims, dtype):
    return jax.ShapeDtypeStruct(dims, dtype)


def params(limit=48):
    return pltpu.CompilerParams(vmem_limit_bytes=limit * MIB)


def micros(time):
    return pl.CostEstimate(flops=max(1, time * 1000000000), bytes_accessed=1000, transcendentals=0)


class Sequence:
    def __init__(self):
        self.last = ()

    def run(self, kernel, outs, ins, scratch=(), limit=16, name=None, after=(), time=0, token=True, **specs):
        single = isinstance(outs, jax.ShapeDtypeStruct)
        self.last = self.last + tuple(after)
        count, extra = len(ins), len(self.last)

        def body(*refs):
            kernel(*refs[:count], *refs[count + extra :])

        results = pl.pallas_call(
            body,
            out_shape=outs,
            in_specs=list(specs.get("in_specs", [VMEM] * count)) + [ANY] * extra,
            out_specs=specs.get("out_specs", VMEM if single else (VMEM,) * len(outs)),
            grid=specs.get("grid", ()),
            scratch_shapes=list(scratch),
            compiler_params=params(limit),
            cost_estimate=micros(time),
            name=name,
        )(*ins, *self.last)
        if token:
            self.last = (min((results,) if single else results, key=lambda v: v.size),)
        return results

    def stage(self, tasks, bundles=(), after=()):
        bundles = [list(bundle) for bundle in bundles]
        placed = {key for bundle in bundles for key in bundle}
        for t, (_, _, parts) in enumerate(tasks):
            bundles += [[(t, p)] for p in range(parts) if (t, p) not in placed]
        sizes = {}
        for t, (kind, views, parts) in enumerate(tasks):
            rows = sum(v.rows for v in views) if kind is join_step else views[0].rows
            for p in range(parts):
                sizes[t, p] = rows // parts
        ins, outs, spots = [], [], {}
        for index, bundle in enumerate(bundles):
            start = 0
            for key in bundle:
                spots[key] = (index, start, sizes[key])
                start += sizes[key]
            like = tasks[bundle[0][0]][1][0].array
            outs.append(shape((start,) + like.shape[1:], BF))
        plan = []
        for t, (kind, views, parts) in enumerate(tasks):
            sources = []
            for view in views:
                at = next((i for i, v in enumerate(ins) if v is view.array), len(ins))
                if at == len(ins):
                    ins.append(view.array)
                sources.append((at, view.start, view.rows))
            plan.append((kind, sources, [spots[t, p] for p in range(parts)]))

        def kernel(*refs):
            def pieces(found, offset):
                return [refs[offset + i].at[start : start + size] for i, start, size in found]

            for kind, sources, targets in plan:
                kind(pieces(sources, 0), pieces(targets, len(ins)))

        results = self.run(kernel, tuple(outs), ins, name="stage", after=after)
        return {key: View(results[i], start, rows) for key, (i, start, rows) in spots.items()}


class View:
    def __init__(self, array, start=0, rows=None):
        self.array, self.start = array, start
        self.rows = array.shape[0] if rows is None else rows


class Sum:
    def __init__(self, near, far, bits, rest, small=False):
        self.small = small
        self.near, self.coming = View(near), View(swap(far, "seq", bits[0]))
        plan = [(bit, 2) for bit in bits[1:]] + [(bit, 1) for bit in rest]
        plan += [(bits[-1], 1)] + [(bit, -1) for bit in reversed(bits[:-1])]
        self.plan = [("seq", bit, parts) for bit, parts in plan]

    def left(self):
        return len(self.plan)

    def task(self):
        parts = self.plan[0][2]
        if parts == -1:
            return (join_step, [self.near, self.coming], 1)
        return (merge_step, [self.near, self.coming], parts)

    def pair(self):
        return (self.near, self.coming)


class Reduce(Sum):
    def __init__(self, near, far, bits):
        Sum.__init__(self, near, far, bits, [])
        self.plan = self.plan[: len(bits) - 1]


class Mix(Sum):
    def __init__(self, near, far, fbits, sbits):
        self.small = True
        self.near, self.coming = View(near), View(swap(far, "fsdp", fbits[0]))
        self.plan = [("fsdp", bit, 2) for bit in fbits[1:]] + [("seq", bit, 1) for bit in sbits]

    def task(self):
        return (mix_step, [self.near, self.coming], self.plan[0][2])


def join_all(sequence, *arrays, after=()):
    task = (join_step, [View(v) for v in arrays], 1)
    return sequence.stage([task], after=after)[0, 0].array


def flow(sequence, *items, extra=(), after=(), together=False):
    tasks = [item.task() for item in items] + list(extra)
    groups = {}
    for t, item in enumerate(items):
        axis, bit, _ = item.plan[0]
        key = (axis, bit, 0 if item.small or together else 1 + t)
        groups.setdefault(key, []).append((t, tasks[t][2] - 1))
    views = sequence.stage(tasks, groups.values(), after)
    for (axis, bit, _), keys in groups.items():
        sent = swap(views[keys[0]].array, axis, bit)
        for t, part in keys:
            view = views[t, part]
            items[t].near = views[t, 0]
            items[t].coming = View(sent, view.start, view.rows)
            items[t].plan.pop(0)
    return [views[len(items) + i, 0].array for i in range(len(extra))]


def swap(value, axis, bit):
    size = lax.axis_size(axis)
    return lax.ppermute(value, axis, [(i, i ^ bit) for i in range(size)])


def bits_of(size):
    return [1 << i for i in range(size.bit_length() - 1)]


def normalize(values):
    center = values - jnp.mean(values, -1, keepdims=True)
    inverse_std = lax.rsqrt(jnp.mean(center * center, -1, keepdims=True) + EPSILON)
    return (center * inverse_std, inverse_std)


def pick(pieces, index):
    result = pieces[-1]
    for i in range(len(pieces) - 2, -1, -1):
        result = jnp.where(index == i, pieces[i], result)
    return result


def rel_order(size):
    order = [0]
    for bit in reversed(bits_of(size)):
        order = order + [r ^ bit for r in order]
    return order


def pack_kernel(*refs):
    count = len(refs) // 2
    pack_ref, both_ref, qo_ref, bulk_ref = refs[count : count + 4]
    sems = refs[-1]
    rows, part = refs[0].shape[0], refs[2].shape[0]
    held = (both_ref.at[:rows], both_ref.at[rows:], qo_ref.at[:part], qo_ref.at[part:])
    held += refs[count + 4 : -1]
    start = 0
    pairs = [(refs[i], held[i]) for i in range(count)]
    for ref in refs[:4]:
        size = ref.shape[0]
        pairs.append((ref, bulk_ref.at[start : start + size]))
        start += size
    copies = [pltpu.make_async_copy(*pair, sems.at[i]) for i, pair in enumerate(pairs)]
    for copy in copies:
        copy.start()
    for copy in copies:
        copy.wait()
    g1, b1, g2, b2, qb, ob, db, kb, vb, wk_ref, wv_ref = held[4:]
    small = jnp.concatenate(
        [
            kb[...].astype(F32).reshape(1, kb.shape[0]),
            vb[...].astype(F32).reshape(1, vb.shape[0]),
            jnp.zeros((1, part - kb.shape[0] - vb.shape[0]), F32),
        ],
        axis=1,
    )
    lines = [ref[...].astype(F32).reshape(1, part) for ref in (g1, b1, g2, b2, qb, ob, db)]
    lines = jnp.concatenate(lines + [small, jnp.zeros((8, part), F32)], axis=0)
    pack_ref[:HDIM] = wk_ref[...]
    pack_ref[HDIM : 2 * HDIM] = wv_ref[...]
    pack_ref[2 * HDIM :] = lines.astype(BF)


def table_kernel(cosine, sine, out):
    out[:HALF] = cosine[...]
    out[HALF:] = sine[...]


def front_kernel(rels, x_ref, *refs):
    count = len(rels)
    packs = refs[:count]
    cs_ref, n1_ref, kv_ref, vec_ref, wkv_ref, pieces, weights = refs[count:]
    me = lax.axis_index("fsdp")
    for rel, pack in zip(rels, packs):
        weights[rel ^ me] = pack[: 2 * HDIM, :]
        pieces[rel ^ me] = pack[2 * HDIM :, :].astype(F32)
    wkv = jnp.concatenate([weights[p] for p in range(count)], axis=1)
    wkv_ref[...] = wkv
    vec = jnp.concatenate([pieces[p] for p in range(count)], axis=1)
    vec_ref[...] = vec
    normal, _ = normalize(x_ref[...].astype(F32))
    n1 = (normal * vec[0:1] + vec[1:2]).astype(BF)
    n1_ref[...] = n1
    key_part, value_part = ROT // count, HDIM // count
    key_bias = jnp.concatenate([pieces[p][7:8, :key_part] for p in range(count)], axis=1)
    value_bias = jnp.concatenate(
        [pieces[p][7:8, key_part : key_part + value_part] for p in range(count)], axis=1
    )
    bias = jnp.concatenate([key_bias, jnp.zeros((1, HDIM - ROT), F32), value_bias], axis=1)
    turned = (dot(n1, wkv, NT) + bias).T
    cosine, sine = cs_ref[:HALF], cs_ref[HALF:]
    first, second = turned[:HALF], turned[HALF:ROT]
    turned = jnp.concatenate(
        [first * cosine - second * sine, second * cosine + first * sine, turned[ROT:]], axis=0
    )
    kv_ref[...] = turned.T.astype(BF)


def query_kernel(rels, n1_ref, both_ref, vec_ref, cs_ref, *refs):
    count = len(rels) - 1
    part = refs[0].shape[0] // 2
    tops = [pack.shape[0] - 2 * part for pack in refs[:count]]
    pairs = [
        (pack.at[top : top + part], pack.at[top + part : top + 2 * part])
        for pack, top in zip(refs[:count], tops)
    ]
    pairs.append(refs[count : count + 2])
    qt_ref, dot_ref, wq_ref, wo_ref = refs[count + 2 :]
    me = lax.axis_index("fsdp")
    for rel, (near, far) in zip(rels, pairs):
        start = pl.multiple_of((rel ^ me) * part, part)
        wq_ref[pl.ds(start, part), :] = near[...]
        wo_ref[pl.ds(start, part), :] = far[...]
    turned = (dot(n1_ref[...], wq_ref[...]) + vec_ref[4:5]).T
    cosine, sine = cs_ref[:HALF], cs_ref[HALF:]
    for h in range(HEADS):
        base = h * HDIM
        first, second = turned[base : base + HALF], turned[base + HALF : base + ROT]
        head = jnp.concatenate(
            [
                first * cosine - second * sine,
                second * cosine + first * sine,
                turned[base + ROT : base + HDIM],
            ],
            axis=0,
        )
        qt_ref[base : base + HDIM, :] = (head.astype(BF).astype(F32) * SCALE).astype(BF)
    dy = both_ref[n1_ref.shape[0] :]
    dot_ref[...] = dot(dy, wo_ref[...], NT).T.astype(BF)


def mlp_kernel(seq_orders, last, *refs):
    both, refs = refs[:2], refs[2:]
    if last:
        up_ref, down_ref, ub_ref, vec_ref, early_up, early_dn, early_sums = refs[:7]
        keep_ref, send_ref, n1c_ref, upk_ref, ups_ref, dnk_ref, dns_ref, sums_ref = refs[7:15]
        normal_s, n2_s, dy_s, acc_up, acc_dn = refs[15:]
    else:
        up_ref, down_ref, ub_ref, vec_ref = refs[:4]
        keep_ref, send_ref, n1c_ref, acc_up, acc_dn, sums_ref = refs[4:10]
        normal_s, n2_s, dy_s = refs[10:]
    me = lax.axis_index("fsdp")
    seq_me = lax.axis_index("seq")
    hidden, width = up_ref.shape
    part = n1c_ref.shape[2]
    rows = n1c_ref.shape[1]
    for i in range(2):
        here = slice(i * rows, (i + 1) * rows)
        x, dy = both[i][:rows], both[i][rows : 2 * rows]
        dy_s[here] = dy
        normal, _ = normalize(x.astype(F32))
        normal_s[here] = normal
        n1 = normal * vec_ref[0:1] + vec_ref[1:2]
        n1c_ref[i] = pick(
            [n1[:, p * part : (p + 1) * part] for p in range(width // part)], me
        ).astype(BF)
        n2_s[here] = (normal * vec_ref[2:3] + vec_ref[3:4]).astype(BF)
    n2, dy = n2_s[...], dy_s[...]
    out = None
    dn2 = None
    tile = 256
    bias = ub_ref[...].astype(F32).reshape(1, hidden)
    sums = []
    for c in range(hidden // tile):
        here = slice(c * tile, (c + 1) * tile)
        up_c, down_c = up_ref[here, :], down_ref[here, :]
        u = dot(n2, up_c, NT) + bias[:, here]
        dg = dot(dy, down_c, NT)
        phi = 0.5 * (1.0 + lax.erf(u * SQRT_HALF))
        g = (u * phi).astype(BF)
        du = (dg * (phi + u * jnp.exp(-0.5 * u * u) * GAUSS_FACTOR)).astype(BF)
        out_c = dot(g, down_c)
        dn2_c = dot(du, up_c)
        out = out_c if out is None else out + out_c
        dn2 = dn2_c if dn2 is None else dn2 + dn2_c
        grad_down, grad_up = dot(g, dy, TN), dot(du, n2, TN)
        if last:
            grad_down, grad_up = grad_down + early_dn[here, :], grad_up + early_up[here, :]
        acc_dn[here, :] = grad_down
        acc_up[here, :] = grad_up
        sums.append(jnp.sum(du.astype(F32), axis=0, keepdims=True))
    lines = [
        jnp.sum(dn2 * normal_s[...], axis=0, keepdims=True),
        jnp.sum(dn2, axis=0, keepdims=True),
        jnp.concatenate(sums, axis=1),
    ]
    for i, line in enumerate(lines):
        size = line.shape[1]
        if last:
            line = line + early_sums[i : i + 1, :size]
        sums_ref[i : i + 1, :size] = line
    for i, target in enumerate((keep_ref, send_ref)):
        here = slice(i * rows, (i + 1) * rows)
        target[0] = out[here].astype(BF)
        target[1] = (dn2[here] * vec_ref[2:3]).astype(BF)
    if last:
        spread_shards(acc_up, seq_orders[0], seq_me, upk_ref, ups_ref)
        spread_shards(acc_dn, seq_orders[1], seq_me, dnk_ref, dns_ref)


def attend_kernel(kv_bits, dkv_bits, side, per_group, chunk_blocks, most, order_ref, len_ref, *refs):
    qt_ref, dot_ref, *kv_refs, cs_ref = refs[:5]
    refs = refs[5:]
    if side == 1:
        early, refs = refs[:3], refs[3:]
    else:
        early = ()
    count = 4 if side == 0 else 5
    attend_side(
        (kv_bits, dkv_bits),
        side,
        per_group,
        chunk_blocks,
        most,
        order_ref,
        len_ref,
        qt_ref,
        dot_ref,
        kv_refs,
        cs_ref,
        early,
        refs[:count],
        *refs[count:],
    )


def attend_side(
    orders,
    side,
    per_group,
    chunk_blocks,
    most,
    order_ref,
    len_ref,
    qt_ref,
    dot_ref,
    kv_refs,
    cs_ref,
    early,
    outs_refs,
    s_scr,
    p_scr,
    pb_scr,
    ds_scr,
    bias_scr,
    kv_scr,
    kvt_scr,
    dkv_scr,
    qs,
    dos,
    ot,
    dqt,
    inverse,
):
    group = pl.program_id(0)
    o_ref, far_ref, near_ref = outs_refs[:3]
    seq_me = lax.axis_index("seq")
    half = held = kv_refs[0].shape[0]
    slots = 2 * held // BLOCK
    chunk = chunk_blocks * BLOCK
    lanes = per_group * BLOCK
    @pl.when(group == 0)
    def _():
        if side == 0:
            dkv_scr[...] = jnp.zeros_like(dkv_scr)
        else:
            dkv_scr[...] = early[2][...]
            for source, target in zip(early[:2], (o_ref, near_ref)):
                target[:BLOCK] = source[...]

        @pl.loop(0, slots)
        def _(i):
            rel = (i // 2) ^ seq_me
            for at, bits in enumerate(orders):
                place = jnp.int32(0)
                for bit in bits:
                    place = place * 2 + (rel // bit) % 2
                inverse[at, order_ref[i]] = place * 2 + i % 2

    block = order_ref[2 * seq_me + side]
    base = block * BLOCK
    end_1 = len_ref[0, 0]
    end_2 = end_1 + len_ref[0, 1]
    end_3 = end_2 + len_ref[0, 2]

    def start_of(position):
        low = jnp.where(position >= end_1, end_1, 0)
        low = jnp.where(position >= end_2, end_2, low)
        return jnp.where(position >= end_3, end_3, low)

    q_pos = base + lax.broadcasted_iota(jnp.int32, (1, BLOCK), 1)
    q_start = start_of(q_pos)
    low_block = jnp.maximum(start_of(base) // BLOCK, block - (most - 1))
    chunks = (block - low_block + chunk_blocks) // chunk_blocks

    def slot_of(j, at):
        return inverse[at, jnp.minimum(low_block + j, block)]

    @pl.loop(0, chunks * chunk_blocks)
    def _(j):
        start = slot_of(j, 0) * BLOCK
        here = pl.ds(pl.multiple_of(j * BLOCK, BLOCK), BLOCK)
        for i, kv_ref in enumerate(kv_refs):

            @pl.when(start // held == i)
            def _():
                there = pl.multiple_of(start - i * held, BLOCK)
                kv_scr[here, :] = kv_ref[pl.ds(there, BLOCK), :]

    for h in range(per_group):
        cols = slice(h * BLOCK, (h + 1) * BLOCK)
        qs[:, cols] = qt_ref[h * HDIM : (h + 1) * HDIM, :]
        dos[:, cols] = dot_ref[h * HDIM : (h + 1) * HDIM, :]

    pairs = per_group // 2

    def columns(h):
        return slice(h * BLOCK, (h + 1) * BLOCK)

    def score_step(c, top):
        keys = kv_scr[pl.ds(c * chunk, chunk), :HDIM]
        k_pos = (low_block + c * chunk_blocks) * BLOCK + lax.broadcasted_iota(
            jnp.int32, (chunk, BLOCK), 0
        )
        allowed = jnp.logical_and(k_pos <= q_pos, k_pos >= q_start)
        bias_scr[c] = jnp.where(allowed, 0.0, NEGATIVE)
        tops = []
        for pair in range(pairs):
            s = dot(keys, qs[:, pair * 2 * BLOCK : (pair + 1) * 2 * BLOCK])
            for half_at in range(2):
                part = s[:, columns(half_at)] + bias_scr[c]
                s_scr[c, :, columns(2 * pair + half_at)] = part
                tops.append(jnp.max(part, axis=0, keepdims=True))
        return jnp.maximum(top, jnp.concatenate(tops, axis=1))

    top = lax.fori_loop(0, chunks, score_step, jnp.full((1, lanes), NEGATIVE, F32))

    def weight_step(c, carry):
        total, delta = carry
        totals, deltas = [], []
        values = kv_scr[pl.ds(c * chunk, chunk), HDIM:]
        for pair in range(pairs):
            dp = dot(values, dos[:, pair * 2 * BLOCK : (pair + 1) * 2 * BLOCK])
            for half_at in range(2):
                cols = columns(2 * pair + half_at)
                part = dp[:, columns(half_at)]
                p_scr[c, :, cols] = part
                e = jnp.exp(s_scr[c, :, cols] - top[:, cols])
                s_scr[c, :, cols] = e
                totals.append(jnp.sum(e, axis=0, keepdims=True))
                deltas.append(jnp.sum(e * part, axis=0, keepdims=True))
        return (
            total + jnp.concatenate(totals, axis=1),
            delta + jnp.concatenate(deltas, axis=1),
        )

    zero = jnp.zeros((1, lanes), F32)
    total, delta = lax.fori_loop(0, chunks, weight_step, (zero, zero))
    shrink = 1.0 / total
    delta = delta * shrink
    ot[...] = jnp.zeros_like(ot)
    dqt[...] = jnp.zeros_like(dqt)

    def grad_step(c, _):
        kvt = kvt_scr[c]
        for pair in range(pairs):
            both = slice(pair * 2 * BLOCK, (pair + 1) * 2 * BLOCK)
            for half_at in range(2):
                cols = columns(2 * pair + half_at)
                p = s_scr[c, :, cols] * shrink[:, cols]
                pb_scr[:, cols] = p.astype(BF)
                ds_scr[:, cols] = (p * (p_scr[c, :, cols] - delta[:, cols])).astype(BF)
            ot[:, both] += dot(kvt[HDIM:], pb_scr[:, both])
            dqt[:, both] += dot(kvt[:HDIM], ds_scr[:, both])
        dk = dot(ds_scr[...], qs[...], NT)
        dv = dot(pb_scr[...], dos[...], NT)
        both = jnp.concatenate([dk, dv], axis=1)
        for b in range(chunk_blocks):

            @pl.when(low_block + c * chunk_blocks + b <= block)
            def _():
                place = slot_of(c * chunk_blocks + b, 1) * BLOCK
                dkv_scr[pl.ds(pl.multiple_of(place, BLOCK), BLOCK), :] += both[
                    b * BLOCK : (b + 1) * BLOCK
                ]

        return 0

    @pl.loop(0, chunks)
    def _(c):
        kvt_scr[c] = kv_scr[pl.ds(c * chunk, chunk), :].astype(F32).T.astype(BF)

    lax.fori_loop(0, chunks, grad_step, 0)
    cosine, sine = cs_ref[:HALF], cs_ref[HALF:]
    outs, grads = [], []
    for h in range(per_group):
        cols = slice(h * BLOCK, (h + 1) * BLOCK)
        outs.append(ot[:, cols])
        grad = dqt[:, cols] * SCALE
        first, second = grad[:HALF], grad[HALF:ROT]
        grads.append(first * cosine + second * sine)
        grads.append(second * cosine - first * sine)
        grads.append(grad[ROT:])
    width = o_ref.shape[1]
    here = slice(side * BLOCK, (side + 1) * BLOCK)
    span = per_group * HDIM
    across = pl.ds(0 if span == width else pl.multiple_of(group * span, span), span)
    o_ref[here, across] = jnp.concatenate(outs, axis=0).T.astype(BF)
    grad = jnp.concatenate(grads, axis=0).T.astype(BF)
    far_ref[:, across] = grad
    near_ref[here, across] = grad

    @pl.when(group == pl.num_programs(0) - 1)
    def _():
        me = lax.axis_index("fsdp")
        part = near_ref.shape[1] - width
        count = width // part
        o = o_ref[here, :].astype(F32)
        pieces = [o[:, p * part : (p + 1) * part] for p in range(count)]
        near_ref[here, width:] = pick(pieces, me ^ 1).astype(BF)
        far_ref[:, width:] = jnp.concatenate(
            [pick(pieces, me ^ 2), pick(pieces, me ^ 3)], axis=1
        ).astype(BF)

        if side == 0:
            outs_refs[3][...] = dkv_scr[...]
        else:
            outs_refs[3][...] = dkv_scr[:half].astype(BF)
            outs_refs[4][...] = dkv_scr[half:].astype(BF)


def output_kernel(both_ref, o_ref, wo_ref, vec_ref, dn1_ref, a_ref, b_ref, c_ref, *outs):
    layer_ref, grad_ref, mark = outs
    mark[...] = jnp.zeros_like(mark)
    rows = o_ref.shape[0]
    x, dy = both_ref[:rows].astype(F32), both_ref[rows:].astype(F32)
    mlp = a_ref[0].astype(F32) + b_ref[0].astype(F32) + c_ref[0].astype(F32)
    attention = dot(o_ref[...], wo_ref[...]) + vec_ref[5:6]
    layer_ref[...] = (x + attention + mlp + vec_ref[6:7]).astype(BF)
    normal, inverse_std = normalize(x)
    total = a_ref[1].astype(F32) + b_ref[1].astype(F32) + c_ref[1].astype(F32)
    total = total + dn1_ref[...] * vec_ref[0:1]
    grad_ref[...] = (
        dy
        + inverse_std
        * (
            total
            - jnp.mean(total, -1, keepdims=True)
            - normal * jnp.mean(total * normal, -1, keepdims=True)
        )
    ).astype(BF)


def shard_at(order, m, seq_me):
    return (order[m] ^ seq_me) & order[-1]


def spread_shards(source, order, seq_me, near, far):
    shards = len(order)
    rows = source.shape[0] // shards
    half = shards // 2
    for m in range(shards):
        start = pl.multiple_of(shard_at(order, m, seq_me) * rows, rows)
        target = near if m < half else far
        target[(m % half) * rows : (m % half + 1) * rows, :] = source[pl.ds(start, rows), :].astype(
            BF
        )


def weight_kernel(order, n1a_ref, n1b_ref, o_ref, own_ref, z1_ref, z2_ref, z3_ref, *refs):
    me = lax.axis_index("fsdp")
    rows, part = n1a_ref.shape[1:]
    dys = [ref.at[rows : 2 * rows] for ref in refs[:4]]
    near_ref, far_ref, grad = refs[4:]
    width = dys[0].shape[1]
    o = o_ref[...].astype(F32)
    own = pick([o[:, p * part : (p + 1) * part] for p in range(width // part)], me).astype(BF)
    items = (
        (n1a_ref[0], own_ref[:, :width], own, dys[0][...]),
        (n1a_ref[1], z1_ref[:, :width], z1_ref[:, width:], dys[1][...]),
        (n1b_ref[0], z2_ref[:, :width], z2_ref[:, width:], dys[2][...]),
        (n1b_ref[1], z3_ref[:, :width], z3_ref[:, width:], dys[3][...]),
    )
    grad_q = None
    grad_o = None
    for n1, dq, cols, dy in items:
        term_q, term_o = dot(n1, dq, TN), dot(cols, dy, TN)
        grad_q = term_q if grad_q is None else grad_q + term_q
        grad_o = term_o if grad_o is None else grad_o + term_o
    grad[:part] = grad_q
    grad[part:] = grad_o
    spread_shards(grad, order, lax.axis_index("seq"), near_ref, far_ref)


def tail_kernel(
    rels,
    both_ref,
    n1_ref,
    dq_ref,
    wq_ref,
    wkv_ref,
    vec_ref,
    cs_ref,
    dkvn_ref,
    dkvf_ref,
    sums_ref,
    dn1_ref,
    keep_ref,
    send_ref,
    vs,
):
    count = len(rels)
    me = lax.axis_index("fsdp")
    rows, width = n1_ref.shape
    part = width // count
    dkv = (dkvn_ref[...].astype(F32) + dkvf_ref[...].astype(F32)).T
    cosine, sine = cs_ref[:HALF], cs_ref[HALF:]
    first, second = dkv[:HALF], dkv[HALF:ROT]
    dkv = jnp.concatenate(
        [first * cosine + second * sine, second * cosine - first * sine, dkv[ROT:]], axis=0
    )
    dkv_sum = jnp.sum(dkv.astype(BF).T.astype(F32), axis=0, keepdims=True)
    dkv_t = dkv.astype(BF)
    dq = dq_ref[:, :width]
    dn1 = dot(dq, wq_ref[...], NT) + dot(dkv_t, wkv_ref[...], TN)
    dn1_ref[...] = dn1
    normal, _ = normalize(both_ref[:rows].astype(F32))
    dy = both_ref[rows:].astype(F32)
    grad_kv = dot(dkv_t, n1_ref[...])
    lines = jnp.concatenate(
        [
            jnp.sum(dn1 * normal, axis=0, keepdims=True),
            jnp.sum(dn1, axis=0, keepdims=True),
            sums_ref[0:1, :width],
            sums_ref[1:2, :width],
            jnp.sum(dq.astype(F32), axis=0, keepdims=True),
            jnp.sum(dy, axis=0, keepdims=True),
            jnp.concatenate(
                [jnp.concatenate([dkv_sum, jnp.zeros((1, part - 2 * HDIM), F32)], axis=1)] * count,
                axis=1,
            ),
            jnp.zeros((1, width), F32),
        ],
        axis=0,
    )
    for p in range(count):
        cols = slice(p * part, (p + 1) * part)
        vs[p, : 2 * HDIM, :] = grad_kv[:, cols]
        vs[p, 2 * HDIM :, :] = lines[:, cols]
    half = count // 2
    extra = sums_ref.shape[1] // part
    up_bias = jnp.concatenate(
        [sums_ref[2:3, e * part : (e + 1) * part] for e in range(extra)]
        + [jnp.zeros((8 - extra, part), F32)],
        axis=0,
    )
    size = keep_ref.shape[0] // half
    for m, rel in enumerate(rels):
        target = keep_ref if m < half else send_ref
        piece = vs[rel ^ me]
        last = up_bias if rel == 0 else jnp.zeros_like(up_bias)
        lines = jnp.concatenate([piece[2 * HDIM :], last], axis=0)
        target[(m % half) * size : (m % half + 1) * size] = join_split(
            fold(piece[: 2 * HDIM], count), fold(lines, count)
        )


def join_split(matrix, lines):
    high = lines.astype(BF).astype(F32)
    rest = jnp.zeros((8, matrix.shape[1]), F32)
    return jnp.concatenate([matrix, high, lines - high, rest], axis=0).astype(BF)


def load_split(value):
    value = value.astype(F32)
    return (value[:32], value[32:36] + value[36:40])


def fold(value, count):
    rows = value.shape[0] // count
    return jnp.concatenate([value[i * rows : (i + 1) * rows] for i in range(count)], axis=1)


def unfold(value, part):
    return jnp.concatenate(
        [value[:, i : i + part] for i in range(0, value.shape[1], part)], axis=0
    )


def mix_step(sources, targets):
    each = sources[0].shape[0] // len(targets)
    for i, target in enumerate(targets):
        here = slice(i * each, (i + 1) * each)
        first, second = load_split(sources[0][here]), load_split(sources[1][here])
        target[...] = join_split(first[0] + second[0], first[1] + second[1])


def merge_step(sources, targets):
    a_ref, b_ref = sources
    rows = a_ref.shape[0] // len(targets)
    for i, target in enumerate(targets):
        here = slice(i * rows, (i + 1) * rows)
        target[...] = (a_ref[here].astype(F32) + b_ref[here].astype(F32)).astype(BF)


def relay_kernel(part, first_ref, second_ref, own_ref, next_ref):
    width = own_ref.shape[1] - part
    for i, ref in enumerate((first_ref, second_ref)):
        here = slice(i * BLOCK, (i + 1) * BLOCK)
        own_ref[here] = ref[:, : width + part]
        next_ref[here, :width] = ref[:, :width]
        next_ref[here, width:] = ref[:, width + part :]


def join_step(sources, targets):
    rows = 0
    for source in sources:
        targets[0][rows : rows + source.shape[0]] = source[...]
        rows += source.shape[0]


def matrix_kernel(order, near_view, far_view, near_ref, far_ref, *refs):
    outs, (mark, held, sems) = refs[:-3], refs[-3:]
    mark[...] = jnp.zeros_like(mark)
    seq_me = lax.axis_index("seq")
    shards = len(order)
    half = shards // 2
    near_ref = near_ref.at[near_view[0] : near_view[0] + near_view[1]]
    far_ref = far_ref.at[far_view[0] : far_view[0] + far_view[1]]
    rows = near_ref.shape[0] // half
    each = shards // len(outs)
    copies = []
    for t in range(shards):
        place = jnp.int32(0)
        for m in range(shards):
            place = jnp.where(shard_at(order, m, seq_me) == t, m, place)
        start = pl.multiple_of((place & (half - 1)) * rows, rows)

        @pl.when(place < half)
        def _():
            held[t] = near_ref[pl.ds(start, rows), :].astype(F32)

        @pl.when(place >= half)
        def _():
            held[t] = far_ref[pl.ds(start, rows), :].astype(F32)

        first = (t % each) * rows
        copy = pltpu.make_async_copy(
            held.at[t], outs[t // each].at[first : first + rows, :], sems.at[t]
        )
        copy.start()
        copies.append(copy)
    for copy in copies:
        copy.wait()


def vector_kernel(a_at, b_at, a_ref, b_ref, g1, b1, qb, kb, vb, ob, g2, b2, ub, db, wk_ref, wv_ref):
    me = lax.axis_index("fsdp")
    first, second = load_split(a_ref[a_at : a_at + 48]), load_split(b_ref[b_at : b_at + 48])
    part = g1.shape[0]
    total = unfold(first[0] + second[0], part)
    lines = unfold(first[1] + second[1], part)
    wk_ref[...] = total[:HDIM]
    wv_ref[...] = total[HDIM:]
    for i, targets in enumerate(((g1,), (b1,), (g2,), (b2,), (qb,), (ob, db))):
        for target in targets:
            target[...] = lines[i : i + 1].reshape(part)
    kp, vp = kb.shape[0], vb.shape[0]
    line = lines[6:7]
    count = HDIM // vp
    kb[...] = pick([line[:, p * kp : (p + 1) * kp] for p in range(count)], me).reshape(kp)
    vb[...] = pick(
        [line[:, HDIM + p * vp : HDIM + (p + 1) * vp] for p in range(count)], me
    ).reshape(vp)
    extra = ub.shape[0] // part
    ub[...] = jnp.concatenate([lines[8 + e : 9 + e] for e in range(extra)], axis=1).reshape(
        ub.shape[0]
    )


def shard_count(rows, devices):
    shards = devices
    while shards > 2 and (rows % shards or (rows // shards) % 16):
        shards //= 2
    return shards


def shard_order(bits):
    order = [0]
    for bit in reversed(bits):
        order = order + [r ^ bit for r in order]
    return order


def on_device(
    tokens,
    block_order,
    doc_lengths,
    norm_one_gain,
    norm_one_bias,
    query_weight,
    query_bias,
    key_weight,
    key_bias,
    value_weight,
    value_bias,
    out_weight,
    out_bias,
    norm_two_gain,
    norm_two_bias,
    up_weight,
    up_bias,
    down_weight,
    down_bias,
    cotangent,
):
    _, rows, width = tokens.shape
    hidden = up_weight.shape[0]
    part = query_weight.shape[0]
    fsdp = lax.axis_size("fsdp")
    seqs = lax.axis_size("seq")
    slots = 2 * seqs
    fbits = bits_of(fsdp)
    sbits = bits_of(seqs)
    rels = rel_order(fsdp)
    fsdp_me = lax.axis_index("fsdp")
    seq_me = lax.axis_index("seq")
    x_own = tokens.reshape(rows, width)
    dy_own = cotangent.reshape(rows, width)

    def spread(value):
        parts = [value]
        for bit in reversed(fbits):
            parts = parts + [swap(v, "fsdp", bit) for v in parts]
        return parts

    pieces = (
        x_own,
        dy_own,
        query_weight,
        out_weight,
        norm_one_gain,
        norm_one_bias,
        norm_two_gain,
        norm_two_bias,
        query_bias,
        out_bias,
        down_bias,
        key_bias,
        value_bias,
        key_weight.T,
        value_weight.T,
    )
    sequence = Sequence()
    run = sequence.run
    pack, both_0, qo_0, bulk_0 = run(
        pack_kernel,
        (
            shape((2 * HDIM + 16, part), BF),
            shape((2 * rows, width), BF),
            shape((2 * part, width), BF),
            shape((2 * rows + 2 * part, width), BF),
        ),
        pieces,
        [pltpu.VMEM(v.shape, BF) for v in pieces[4:]] + [pltpu.SemaphoreType.DMA((len(pieces) + 4,))],
        limit=60,
        name="pack",
        time=2,
        in_specs=[HBM] * len(pieces),
    )
    packs = spread(pack)
    qo_2 = swap(qo_0, "fsdp", 2)
    both_2 = swap(both_0, "fsdp", 2)
    bulk_1 = swap(bulk_0, "fsdp", 1)

    own_blocks = lax.dynamic_slice_in_dim(block_order, 2 * seq_me, 2)
    offsets = jnp.arange(BLOCK, dtype=jnp.int32)
    own_pos = (own_blocks[:, None] * BLOCK + offsets[None, :]).reshape(rows)
    frequencies = 10000.0 ** (-2.0 * jnp.arange(HALF, dtype=F32) / ROT)
    angles = own_pos.astype(F32)[None, :] * frequencies[:, None]
    cs = run(
        table_kernel,
        shape((ROT, rows), F32),
        (jnp.cos(angles), jnp.sin(angles)),
        name="tables",
        time=5,
    )

    n1, kv_own, vec, wkv = run(
        functools.partial(front_kernel, rels),
        (
            shape((rows, width), BF),
            shape((rows, 2 * HDIM), BF),
            shape((16, width), F32),
            shape((2 * HDIM, width), BF),
        ),
        (x_own, *packs, cs),
        [pltpu.VMEM((fsdp, 16, part), F32), pltpu.VMEM((fsdp, 2 * HDIM, part), BF)],
        name="front",
        time=1,
    )

    kv = kv_own
    for bit in reversed(sbits[3:]):
        kv = join_all(sequence, kv, swap(kv, "seq", bit))
    kv_parts = [kv] + [swap(kv, "seq", bit) for bit in (sbits[2], sbits[1], sbits[1] + sbits[2])]
    kv_bits = sbits

    up_bits, dn_bits = sbits[:2], [sbits[1], sbits[0]]
    seq_orders = (shard_order(up_bits), shard_order(dn_bits))

    def others(bits):
        return sorted((b for b in sbits if b not in bits), key=lambda b: (b > sbits[2], -b))

    chunk_out = shape((2, rows, width), BF)
    n1c_out = shape((2, rows, part), BF)
    sums_out = shape((8, max(hidden, width)), F32)
    mlp_scratch = [
        pltpu.VMEM((2 * rows, width), F32),
        pltpu.VMEM((2 * rows, width), BF),
        pltpu.VMEM((2 * rows, width), BF),
    ]
    most = min(slots, slots // 2 + 1)
    chunk_blocks = 3
    most_chunks = -(-most // chunk_blocks)
    chunk = chunk_blocks * BLOCK
    per_group = HEADS
    while most_chunks * chunk * per_group * BLOCK * 8 > 20 * MIB and per_group > 2:
        per_group = {12: 6, 6: 4, 4: 2}[per_group]
    lanes = per_group * BLOCK
    span = per_group * HDIM
    def attend(side, early, outs):
        return run(
            functools.partial(attend_kernel, kv_bits, sbits, side, per_group, chunk_blocks, most),
            outs,
            (block_order, doc_lengths, qt, do_t, *kv_parts, cs, *early),
            [
                pltpu.VMEM((most_chunks, chunk, lanes), F32),
                pltpu.VMEM((most_chunks, chunk, lanes), F32),
                pltpu.VMEM((chunk, lanes), BF),
                pltpu.VMEM((chunk, lanes), BF),
                pltpu.VMEM((most_chunks, chunk, BLOCK), F32),
                pltpu.VMEM((most_chunks * chunk, 2 * HDIM), BF),
                pltpu.VMEM((most_chunks, 2 * HDIM, chunk), BF),
                pltpu.VMEM((slots * BLOCK, 2 * HDIM), F32),
                pltpu.VMEM((HDIM, lanes), BF),
                pltpu.VMEM((HDIM, lanes), BF),
                pltpu.VMEM((HDIM, lanes), F32),
                pltpu.VMEM((HDIM, lanes), F32),
                pltpu.SMEM((2, slots), jnp.int32),
            ],
            limit=36 if slots <= 16 else 60,
            name="attend",
            time=(2, 14)[side],
            grid=(HEADS // per_group,),
            in_specs=[
                SMEM,
                SMEM,
                pl.BlockSpec((span, BLOCK), lambda g: (g, side)),
                pl.BlockSpec((span, BLOCK), lambda g: (g, side)),
                VMEM,
                VMEM,
                pl.BlockSpec((ROT, BLOCK), lambda g: (0, side)),
            ]
            + [VMEM] * len(early),
        )

    far_out = shape((BLOCK, width + 2 * part), BF)
    def matrix(item, order, count):
        near, far = item.pair()
        each = 2 * near.rows // len(order)
        views = [(view.start, view.rows) for view in (near, far)]
        return run(
            functools.partial(matrix_kernel, order, *views),
            (shape((2 * near.rows // count, width), F32),) * count + (shape((8, 128), F32),),
            (near.array, far.array),
            [
                pltpu.VMEM((len(order), each, width), F32),
                pltpu.SemaphoreType.DMA((len(order),)),
            ],
            name="matrix",
            out_specs=(HBM,) * count + (VMEM,),
        )[:count]

    keep_a, send_a, n1a, early_up, early_dn, early_sums = run(
        functools.partial(mlp_kernel, None, False),
        (
            chunk_out,
            chunk_out,
            n1c_out,
            shape((hidden, width), F32),
            shape((hidden, width), F32),
            sums_out,
        ),
        (both_0, bulk_1, up_weight, down_weight, up_bias, vec),
        mlp_scratch,
        limit=24,
        name="mlp_near",
        time=0,
    )
    back_a = swap(send_a, "fsdp", 1)
    kv_near = join_all(sequence, *kv_parts)
    kv_parts = [kv_near, swap(kv_near, "seq", sbits[0])]
    task = (join_step, [View(qo_2, 0, part)], 1), (join_step, [View(qo_2, part, part)], 1)
    views = sequence.stage(task)
    qo_3 = [swap(views[t, 0].array, "fsdp", 1) for t in range(2)]
    qt, do_t, wq, wo = run(
        functools.partial(query_kernel, rels),
        (
            shape((width, rows), BF),
            shape((width, rows), BF),
            shape((width, width), BF),
            shape((width, width), BF),
        ),
        (n1, both_0, vec, cs, qo_0, qo_2, bulk_1, *qo_3),
        name="query",
    )

    own, far_0, near, dkv = attend(
        0,
        (),
        (
            shape((BLOCK, width), BF),
            far_out,
            shape((BLOCK, width + part), BF),
            shape((slots * BLOCK, 2 * HDIM), F32),
        ),
    )
    z2 = [swap(far_0, "fsdp", 2)]
    both_3 = swap(join_all(sequence, both_2), "fsdp", 1)
    keep_b, send_b, n1b, upk, ups, dnk, dns, sums = run(
        functools.partial(mlp_kernel, seq_orders, True),
        (chunk_out, chunk_out, n1c_out)
        + (shape((hidden // 2, width), BF),) * 4
        + (sums_out,),
        (both_2, both_3, up_weight, down_weight, up_bias, vec, early_up, early_dn, early_sums),
        mlp_scratch + [pltpu.VMEM((hidden, width), F32)] * 2,
        limit=28,
        name="mlp_far",
        time=14,
        after=(back_a,),
    )
    up = Sum(upk, ups, up_bits, others(up_bits))
    dn = Sum(dnk, dns, dn_bits, others(dn_bits))
    own, far_1, z_near, dkv_near, dkv_far = attend(
        1,
        (own, near, dkv),
        (shape((rows, width), BF), far_out, shape((rows, width + part), BF))
        + (shape((seqs * BLOCK, 2 * HDIM), BF),) * 2,
    )
    z2.append(swap(far_1, "fsdp", 2))
    dkv = Reduce(dkv_near, dkv_far, sbits)
    z1 = swap(z_near, "fsdp", 1)
    flow(sequence, up, dn)
    z2, relay_z = run(
        functools.partial(relay_kernel, part),
        (shape((rows, width + part), BF),) * 2,
        z2,
        name="relay",
    )
    z3 = swap(relay_z, "fsdp", 1)
    flow(sequence, dkv)
    flow(sequence, up)
    qo_bits = sbits[:2]
    qo_order = shard_order(qo_bits)
    qok, qos = run(
        functools.partial(weight_kernel, qo_order),
        (shape((part, width), BF),) * 2,
        (n1a, n1b, own, z_near, z1, z2, z3, both_0, bulk_1, both_2, both_3),
        [pltpu.VMEM((2 * part, width), F32)],
        name="weight",
    )
    qo = Sum(qok, qos, qo_bits, others(qo_bits), small=True)
    while dkv.left():
        flow(sequence, dkv)
    flow(sequence, dn)
    mixed = shape((48 * fsdp // 2, width), BF)
    dn1, near_t, far_t = run(
        functools.partial(tail_kernel, rels),
        (shape((rows, width), F32), mixed, mixed),
        (both_0, n1, z_near, wq, wkv, vec, cs, *[v.array for v in dkv.pair()], sums),
        [pltpu.VMEM((fsdp, 2 * HDIM + 8, part), F32)],
        name="tail",
    )
    mix = Mix(near_t, far_t, fbits, [sbits[1], sbits[0], sbits[2]] + sbits[3:])
    while up.left() > 2:
        flow(sequence, up)
    flow(sequence, up)
    flow(sequence, qo)
    flow(sequence, mix)
    flow(sequence, qo, up)
    flow(sequence, mix)
    flow(sequence, mix)
    while dn.left() > 2:
        flow(sequence, dn)
    flow(sequence, dn)
    back_b = swap(send_b, "fsdp", 1)
    back = sequence.stage([(merge_step, [View(keep_b), View(back_b)], 1)])[0, 0].array
    back = swap(back, "fsdp", 2)
    flow(sequence, qo)
    while mix.left() > 1:
        flow(sequence, mix)
    flow(sequence, mix)
    while qo.left() > 1:
        flow(sequence, qo)
    flow(sequence, qo)
    flow(sequence, dn)
    (grad_up,) = matrix(up, seq_orders[0], 1)
    layer_out, grad_tokens, _ = run(
        output_kernel,
        (shape((rows, width), BF),) * 2 + (shape((8, 128), F32),),
        (both_0, own, wo, vec, dn1, keep_a, back_a, back),
        name="output",
    )
    vector = shape((part,), F32)
    g1, b1, qb, kb, vb, ob, g2, b2, ub, db, wk, wv = run(
        functools.partial(vector_kernel, *[v.start for v in mix.pair()]),
        (
            vector,
            vector,
            vector,
            shape(key_bias.shape, F32),
            shape(value_bias.shape, F32),
            vector,
            vector,
            vector,
            shape((hidden,), F32),
            vector,
            shape((HDIM, part), F32),
            shape((HDIM, part), F32),
        ),
        tuple(v.array for v in mix.pair()),
        limit=16,
        name="vector",
    )
    grad_query, grad_out = matrix(qo, qo_order, 2)
    (grad_down,) = matrix(dn, seq_orders[1], 1)
    return (
        layer_out.reshape(1, rows, width),
        grad_tokens.reshape(1, rows, width),
        g1,
        b1,
        grad_query,
        qb,
        wk.T,
        kb,
        wv.T,
        vb,
        grad_out,
        ob,
        g2,
        b2,
        grad_up,
        ub,
        grad_down,
        db,
    )


def solution(mesh):
    split = P("fsdp")
    matrix = P("fsdp", None)
    stream = P("fsdp", "seq", None)
    return jax.shard_map(
        on_device,
        mesh=mesh,
        in_specs=(
            stream,
            P(),
            matrix,
            split,
            split,
            matrix,
            split,
            matrix,
            split,
            matrix,
            split,
            matrix,
            split,
            split,
            split,
            matrix,
            split,
            matrix,
            split,
            stream,
        ),
        out_specs=(
            stream,
            stream,
            split,
            split,
            matrix,
            split,
            matrix,
            split,
            matrix,
            split,
            matrix,
            split,
            split,
            split,
            matrix,
            split,
            matrix,
            split,
        ),
        check_vma=False,
    )
```
